32 devices in a mesh: groups: 2 (over y), patch: 4 (over z), sub: 2 (over x), half: 2 (over core).
Axes of the slice: x: 2, y: 2, z: 4, core: 2. Of those that a mesh axis runs over, the one named last changes fastest.
Arguments:
- vectors: float32 [2, 8192, 256], P(None, ('groups', 'patch', 'sub', 'half')), parts along dimension 1, may hold values from -600 to 600
- prestress: bfloat16 [8192, 3, 256], P(('groups', 'patch', 'sub', 'half')), parts along dimension 0, may hold values from -4 to 4
- thickness: float32 [8192, 256], P(('groups', 'patch', 'sub', 'half')), parts along dimension 0, may hold values from 0.5 to 2
- foundation: float32 [8192, 256], P(('groups', 'patch', 'sub', 'half')), parts along dimension 0, may hold values from 2 to 6
- patch_rows: int32 [64], P(('groups', 'patch', 'sub', 'half')), parts along dimension 0, may hold values from 64 to 128, as said below
- matched: int32 [64], P(('groups', 'patch', 'sub', 'half')), parts along dimension 0, may hold values from 0 to 31, as said below
- elem_row: int32 [8192], P(('groups', 'patch', 'sub', 'half')), parts along dimension 0, may hold values from 0 to 4095, as said below
Outputs:
- modes: float32 [2, 8192, 256], P(None, ('groups', 'patch', 'sub', 'half')), parts along dimension 1
The draws below stay inside these ranges and needn't reach their ends.
There are 2 independent parts, one for each index of `groups`. The reference program is written for one: setup_inputs(seed, part) draws one part's arguments, and reference() takes and returns one part's arrays. A program takes and returns all parts, laid end to end along the dimension named above; each array names one. Nothing has to cross between parts.
Inputs may be any that keep to these rules, and one draw needn't show every extreme that they name: `patch_rows`: the largest value is reached by some patch in every draw. A permutation of the patches; the patch matched to a patch lies on the device with the same sub and half indices and a patch index one above or one below, cyclically. `elem_row`: a permutation of the rows; of each device's rows, those in positions k * 16 to (k + 1) * 16 - 1 belong to patches of the device with index k along patch+sub+half.
All inputs are finite; a program needn't handle non-finite values.
Results may differ from the reference program's by a relative error of at most 0.0003.
Values may be sent and summed in bfloat16 or wider, within the bound.
No kernel may reach another device: no remote copies, remote signals or barrier semaphores. Data moves between devices by JAX's collectives and lax.ppermute only.
A program may use at most 64 MiB of HBM per device.

```python
import math
import jax
import jax.numpy as jnp

PROWS = 128
C = 256
PSLOT = 2
ITERS = 2
PATCHES = 32
ROWS = 4096
N_PATCH = 4
N_SUB = 2
N_HALF = 2


def draw_vectors(key, part):
    first, second, third = jax.random.split(key, 3)
    row_scale = jnp.exp(jax.random.uniform(second, (2, ROWS, 1), jnp.float32, 0.0, math.log(10.0)))
    col_scale = jnp.exp(jax.random.uniform(third, (2, 1, C), jnp.float32, 0.0, math.log(10.0)))
    base = jnp.clip(jax.random.normal(first, (2, ROWS, C), jnp.float32), -6.0, 6.0)
    return base * row_scale * col_scale


def draw_patch_rows(key, part):
    first, second = jax.random.split(key)
    lengths = jax.random.randint(first, (PATCHES,), PROWS // 2, PROWS + 1).astype(jnp.int32)
    where_full = jax.random.randint(second, (), 0, PATCHES)
    return lengths.at[where_full].set(PROWS)


def draw_matched(key, part):
    groups_inner = N_SUB * N_HALF
    first, second = jax.random.split(key)
    direction = jax.random.randint(first, (groups_inner,), 0, 2).astype(jnp.int32) * 2 - 1
    direction = direction.at[0].set(1).at[1].set(-1)
    scores = jax.random.randint(second, (N_PATCH, groups_inner, PSLOT), 0, 2 ** 18).astype(jnp.int32) * PSLOT + jnp.arange(PSLOT, dtype=jnp.int32)
    slot_order = jnp.argsort(scores, axis=-1, stable=True).astype(jnp.int32)
    owner = jnp.arange(N_PATCH, dtype=jnp.int32)[:, None, None]
    inner = jnp.arange(groups_inner, dtype=jnp.int32)[None, :, None]
    target = (owner + direction[None, :, None]) % N_PATCH
    return ((target * groups_inner + inner) * PSLOT + slot_order).reshape(-1).astype(jnp.int32)


def draw_elem_row(key, part):
    devices_all = N_PATCH * N_SUB * N_HALF
    rows_dev = PSLOT * PROWS
    per_peer = rows_dev // devices_all
    scores = jax.random.randint(key, (devices_all, rows_dev), 0, 2 ** 18).astype(jnp.int32) * rows_dev + jnp.arange(rows_dev, dtype=jnp.int32)
    order = jnp.argsort(scores, axis=-1, stable=True).astype(jnp.int32)
    order = order.reshape(devices_all, devices_all, per_peer).transpose(1, 0, 2)
    owner = jnp.arange(devices_all, dtype=jnp.int32)[None, :, None]
    return (owner * rows_dev + order).reshape(-1).astype(jnp.int32)


def level_of(stream_key, extent, pieces, smallest, high):
    def one(axis_at, shards_of):
        steps = jax.random.uniform(jax.random.fold_in(jax.random.fold_in(stream_key, 6), axis_at), (shards_of,), jnp.float32, smallest / len(pieces), high / len(pieces))
        return jnp.repeat(jnp.exp(steps), extent[axis_at] // shards_of).reshape((-1,) + (1,) * (len(extent) - axis_at - 1))

    level = one(*pieces[0])
    for cut in pieces[1:]:
        level = level * one(*cut)
    return level


def noise(key, dims, scale, bound, cuts=(), held_as=jnp.bfloat16):
    level = level_of(key, dims, cuts, -0.22, 0.18) if cuts else 1.0
    result = jax.random.normal(key, dims, jnp.float32) * scale * level
    return jnp.minimum(jnp.maximum(result, -bound), bound).astype(held_as)


def setup_inputs(seed: int = 0, part: int = 0) -> dict:
    key_of = jax.random.split(jax.random.key(seed), 8)
    part_splits = jax.random.split(jax.random.fold_in(key_of[7], part), 8)
    vectors = draw_vectors(jax.random.fold_in(jax.random.fold_in(key_of[7], part), 71), part)
    prestress = noise(part_splits[1], (ROWS, 3, C), 1.0, 4.0, ((0, 16),))
    thickness = jnp.clip(jnp.exp(math.log(2.0) - 1.3862944 * jax.random.uniform(part_splits[2], (ROWS, C), jnp.float32) ** level_of(part_splits[2], (ROWS, C), ((0, 16),), -0.2, 0.2)), 0.5, 2.0)
    foundation = jnp.clip(jnp.exp(math.log(6.0) - 1.0986123 * jax.random.uniform(part_splits[3], (ROWS, C), jnp.float32) ** level_of(part_splits[3], (ROWS, C), ((0, 16),), -0.2, 0.2)), 2.0, 6.0)
    patch_rows = draw_patch_rows(jax.random.fold_in(jax.random.fold_in(key_of[7], part), 71), part)
    matched = draw_matched(jax.random.fold_in(jax.random.fold_in(key_of[7], part), 71), part)
    elem_row = draw_elem_row(jax.random.fold_in(jax.random.fold_in(key_of[7], part), 71), part)
    return {"vectors": vectors, "prestress": prestress, "thickness": thickness, "foundation": foundation, "patch_rows": patch_rows, "matched": matched, "elem_row": elem_row}


step_size = 1.0
norm_scale = 16.0
penalty_value = 8.0
penalty_slope = 4.0

def second_rows(field):
    padded = jnp.pad(field, [(0, 0)] * (field.ndim - 2) + [(1, 1), (0, 0)])
    return padded[..., :-2, :] - 2.0 * field + padded[..., 2:, :]

def second_cols(field):
    padded = jnp.pad(field, [(0, 0)] * (field.ndim - 1) + [(1, 1)])
    return padded[..., :-2] - 2.0 * field + padded[..., 2:]

def forward_rows(field):
    zeros = jnp.zeros_like(field[..., :1, :])
    return jnp.concatenate([field[..., 1:, :], zeros], axis=-2) - field

def backward_rows(field):
    zeros = jnp.zeros_like(field[..., :1, :])
    return jnp.concatenate([zeros, field[..., :-1, :]], axis=-2) - field

def forward_cols(field):
    zeros = jnp.zeros_like(field[..., :1])
    return jnp.concatenate([field[..., 1:], zeros], axis=-1) - field

def backward_cols(field):
    zeros = jnp.zeros_like(field[..., :1])
    return jnp.concatenate([zeros, field[..., :-1]], axis=-1) - field

def stiffness(field, live, thickness, foundation):
    bend_rows = thickness * live * second_rows(field)
    bend_cols = thickness * second_cols(field)
    return live * (foundation * field + second_rows(bend_rows) + second_cols(bend_cols))

def geometric(field, live, stress):
    along_rows = forward_rows(field)
    along_cols = forward_cols(field)
    nuu = stress[:, :, 0, :]
    nvv = stress[:, :, 1, :]
    nuv = stress[:, :, 2, :]
    total = backward_rows(nuu * along_rows + nuv * along_cols) + backward_cols(nvv * along_cols + nuv * along_rows)
    return live * total

def edges(field, lengths):

    def row_pick(index):
        where_rows = jnp.broadcast_to(index[None, :, None, None], (field.shape[0], field.shape[1], 1, field.shape[3]))
        return jnp.take_along_axis(field, where_rows, axis=2)[:, :, 0, :]
    top = jnp.stack([row_pick(lengths - 2), row_pick(lengths - 1)], axis=2)
    bottom = field[:, :, 0:2, :]
    return (top, bottom)

def interface(field, lengths, top, bottom, partner_top, partner_bottom):
    jump_top = top[:, :, 1, :] - partner_bottom[:, :, 0, :]
    slope_top = top[:, :, 1, :] - top[:, :, 0, :] - (partner_bottom[:, :, 1, :] - partner_bottom[:, :, 0, :])
    jump_bottom = partner_top[:, :, 1, :] - bottom[:, :, 0, :]
    slope_bottom = partner_top[:, :, 1, :] - partner_top[:, :, 0, :] - (bottom[:, :, 1, :] - bottom[:, :, 0, :])
    rows = jnp.arange(field.shape[2], dtype=jnp.int32)[None, :, None]
    last = lengths[:, None, None] - 1
    added = jnp.where(rows == last, (penalty_value * jump_top + penalty_slope * slope_top)[:, :, None, :], 0.0)
    added = added + jnp.where(rows == last - 1, (-penalty_slope * slope_top)[:, :, None, :], 0.0)
    added = added + jnp.where(rows == 0, (-penalty_value * jump_bottom + penalty_slope * slope_bottom)[:, :, None, :], 0.0)
    added = added + jnp.where(rows == 1, (-penalty_slope * slope_bottom)[:, :, None, :], 0.0)
    return added

def products(field, kfield, gfield):
    return jnp.stack([jnp.sum(field[0] * kfield[0]), jnp.sum(field[0] * kfield[1]), jnp.sum(field[1] * kfield[1]), jnp.sum(field[0] * gfield[0]), jnp.sum(field[0] * gfield[1]), jnp.sum(field[1] * gfield[1])])

def advance(field, kfield, gfield, totals, precond, cells):
    first_a = totals[0]
    cross_k = totals[1]
    second_a = totals[2]
    first_g = totals[3]
    cross_g = totals[4]
    second_g = totals[5]
    ratio = cross_k / first_a
    other = field[1] - ratio * field[0]
    other_k = kfield[1] - ratio * kfield[0]
    other_g = gfield[1] - ratio * gfield[0]
    other_a = second_a - ratio * cross_k
    other_q = second_g - 2.0 * ratio * cross_g + ratio * ratio * first_g
    first_mu = first_g / first_a
    other_mu = other_q / other_a
    new_first = (field[0] + step_size * precond * (gfield[0] - first_mu * kfield[0])) * jnp.sqrt(norm_scale * cells / first_a)
    new_other = (other + step_size * precond * (other_g - other_mu * other_k)) * jnp.sqrt(norm_scale * cells / other_a)
    return jnp.stack([new_first, new_other])

def reference(vectors, prestress, thickness, foundation, patch_rows, matched, elem_row):
    placed = jnp.zeros((ROWS, 3, C), jnp.bfloat16).at[elem_row].set(prestress)
    stress = placed.astype(jnp.float32).reshape(PATCHES, PROWS, 3, C)
    rows = jnp.arange(PROWS, dtype=jnp.int32)[None, :]
    live = (rows < patch_rows[:, None]).astype(jnp.float32)[:, :, None]
    thick = thickness.reshape(PATCHES, PROWS, C)
    support = foundation.reshape(PATCHES, PROWS, C)
    precond = live / (support + 12.0 * thick)
    inverse = jnp.zeros((PATCHES,), jnp.int32).at[matched].set(jnp.arange(PATCHES, dtype=jnp.int32))
    field = vectors.reshape(2, PATCHES, PROWS, C) * live
    cells = jnp.float32(ROWS * C)
    for step in range(ITERS):
        top, bottom = edges(field, patch_rows)
        partner_bottom = bottom[:, matched]
        partner_top = top[:, inverse]
        kfield = stiffness(field, live, thick, support) + interface(field, patch_rows, top, bottom, partner_top, partner_bottom)
        gfield = geometric(field, live, stress)
        totals = products(field, kfield, gfield)
        field = advance(field, kfield, gfield, totals, precond, cells)
    return field.reshape(2, ROWS, C)
```

```python
import functools

import jax
import jax.numpy as jnp
from jax import lax
from jax.experimental import pallas as pl
from jax.experimental.pallas import tpu as pltpu
from jax.sharding import PartitionSpec as P

norm_scale = 16.0
penalty_value = 8.0
penalty_slope = 4.0
LANES = 128

UU = [(a, b) for a in range(4) for b in range(a, 4)]
NAMES = (
    [("kuu", a, b) for a, b in UU]
    + [("guu", a, b) for a, b in UU]
    + [("kxx", 0, 0), ("kxx", 0, 1), ("kxx", 1, 1)]
    + [("gxx", 0, 0), ("gxx", 0, 1), ("gxx", 1, 1)]
    + [("kpk", 0, 0), ("kpk", 0, 1), ("kpk", 1, 1)]
    + [("kpg", a, b) for a in range(2) for b in range(2)]
    + [("gpg", 0, 0), ("gpg", 0, 1), ("gpg", 1, 1)]
)
AT = {name: k for k, name in enumerate(NAMES)}
SUMS = 40
TILES = SUMS // 8


def passed_along(array, axis, by):
    peers = lax.axis_size(axis)
    return lax.ppermute(array, axis, [(i, (i + by) % peers) for i in range(peers)])


def summed_over(array, axis):
    total = array
    for by in range(1, lax.axis_size(axis)):
        total = total + passed_along(array, axis, by)
    return total


def iota(shape, axis):
    return lax.broadcasted_iota(jnp.int32, shape, axis)


def row_after(w):
    n = w.shape[0]
    return jnp.where(iota(w.shape, 0) < n - 1, pltpu.roll(w, n - 1, 0), 0.0)


def row_before(w):
    return jnp.where(iota(w.shape, 0) > 0, pltpu.roll(w, 1, 0), 0.0)


def col_after(w):
    n = w.shape[1]
    return jnp.where(iota(w.shape, 1) < n - 1, pltpu.roll(w, n - 1, 1), 0.0)


def col_before(w):
    return jnp.where(iota(w.shape, 1) > 0, pltpu.roll(w, 1, 1), 0.0)


def second_rows(w):
    return row_before(w) + row_after(w) - 2.0 * w


def second_cols(w):
    return col_before(w) + col_after(w) - 2.0 * w


def stiffness(w, live, thick, support):
    bend_rows = jnp.where(live, thick * second_rows(w), 0.0)
    bend_cols = thick * second_cols(w)
    return jnp.where(live, support * w + second_rows(bend_rows) + second_cols(bend_cols), 0.0)


def geometric(w, live, nuu, nvv, nuv):
    along_rows = row_after(w) - w
    along_cols = col_after(w) - w
    rows = nuu * along_rows + nuv * along_cols
    cols = nvv * along_cols + nuv * along_rows
    return jnp.where(live, row_before(rows) - rows + col_before(cols) - cols, 0.0)


def live_of(rows_ref, slot, shape):
    return iota(shape, 0) < rows_ref[slot]


def column_sums(product):
    return jnp.sum(product, axis=0, keepdims=True)


def packed(sums):
    totals = jnp.sum(sums, axis=1, keepdims=True)
    lane = iota((8, LANES), 1)
    out = jnp.zeros((8, LANES), jnp.float32)
    for tile in range(TILES):
        out = jnp.where(lane == tile, totals[8 * tile : 8 * tile + 8], out)
    return out


def pack_kernel(rows_ref, mine_ref, match_ref, stress_ref, elem_ref, vec_ref, pay_ref, edge_ref):
    rows_dev, ncol = stress_ref.shape[1:]
    slots = rows_ref.shape[0]
    prows = rows_dev // slots
    for j in range(3):
        pay_ref[:, j * ncol : (j + 1) * ncol] = stress_ref[j]
    square = (rows_dev, rows_dev)
    spread = jnp.broadcast_to(elem_ref[...].astype(jnp.float32), square)
    column = jnp.sum(
        jnp.where(iota(square, 0) == iota(square, 1), spread, 0.0), axis=1, keepdims=True
    )
    pay_ref[:, 3 * ncol :] = jnp.broadcast_to(column, (rows_dev, LANES)).astype(jnp.bfloat16)
    for s in range(slots):
        last = s * prows + rows_ref[s] - 1
        for v in range(2):
            at = 4 * (2 * s + v)
            edge_ref[at : at + 1, :] = vec_ref[v, pl.ds(last - 1, 1), :]
            edge_ref[at + 1 : at + 2, :] = vec_ref[v, pl.ds(last, 1), :]
            edge_ref[at + 2 : at + 4, :] = vec_ref[v, s * prows : s * prows + 2, :]
        at = 8 * slots
        edge_ref[at + s : at + s + 1, :] = jnp.full((1, ncol), mine_ref[s], jnp.int32).astype(jnp.float32)
        edge_ref[at + slots + s : at + slots + s + 1, :] = jnp.full((1, ncol), match_ref[s], jnp.int32).astype(jnp.float32)
    used = 10 * slots
    edge_ref[used:, :] = jnp.zeros((edge_ref.shape[0] - used, ncol), jnp.float32)


def stiff_kernel(
    rows_ref, mine_ref, match_ref, vec_ref, thick_ref, support_ref, edge_ref, below_ref, above_ref,
    k_ref, uk_ref, prec_ref,
):
    slots = rows_ref.shape[0]
    rows_dev, ncol = thick_ref.shape
    prows = rows_dev // slots
    for s in range(slots):
        at = slice(s * prows, (s + 1) * prows)
        live = live_of(rows_ref, s, (prows, ncol))
        thick, support = thick_ref[at, :], support_ref[at, :]
        prec = jnp.where(live, 1.0 / (support + 12.0 * thick), 0.0)
        prec_ref[at, :] = prec
        for v in range(2):
            w = jnp.where(live, vec_ref[v, at, :], 0.0)
            k_ref[v, at, :] = stiffness(w, live, thick, support)
        last = s * prows + rows_ref[s] - 1
        first = s * prows
        for v in range(2):
            own = edge_ref[4 * (2 * s + v) : 4 * (2 * s + v) + 4, :]
            top = jnp.zeros((2, ncol), jnp.float32)
            bottom = jnp.zeros((2, ncol), jnp.float32)
            for ref in (below_ref, above_ref):
                for t in range(slots):
                    strip = ref[4 * (2 * t + v) : 4 * (2 * t + v) + 4, :]
                    label = ref[8 * slots + t : 8 * slots + t + 1, :]
                    wants = ref[9 * slots + t : 9 * slots + t + 1, :]
                    top = top + jnp.where(wants == mine_ref[s].astype(jnp.float32), strip[0:2], 0.0)
                    bottom = bottom + jnp.where(label == match_ref[s].astype(jnp.float32), strip[2:4], 0.0)
            jump_t = own[1:2] - bottom[0:1]
            slope_t = own[1:2] - own[0:1] - (bottom[1:2] - bottom[0:1])
            jump_b = top[1:2] - own[2:3]
            slope_b = top[1:2] - top[0:1] - (own[3:4] - own[2:3])
            k_ref[v, pl.ds(last, 1), :] += penalty_value * jump_t + penalty_slope * slope_t
            k_ref[v, pl.ds(last - 1, 1), :] += -penalty_slope * slope_t
            k_ref[v, first : first + 1, :] += -penalty_value * jump_b + penalty_slope * slope_b
            k_ref[v, first + 1 : first + 2, :] += -penalty_slope * slope_b
        for v in range(2):
            uk_ref[v, at, :] = prec * k_ref[v, at, :]


def gram_kernel(
    rows_ref, match_ref, arrived_ref, vec_ref, thick_ref, support_ref, prec_ref, k_ref, uk_ref,
    ug_ref, stress_ref, out_ref, sums_ref, g_ref,
):
    slots = rows_ref.shape[0]
    rows_dev, ncol = thick_ref.shape
    prows = rows_dev // slots
    index = arrived_ref[:, 3 * ncol :].astype(jnp.float32)
    lane = iota(index.shape, 1).astype(jnp.float32)
    pick = jnp.concatenate(
        [
            jnp.where(index == lane + float(h * LANES), 1.0, 0.0).astype(jnp.bfloat16)
            for h in range(rows_dev // LANES)
        ],
        axis=1,
    )
    placed = lax.dot_general(
        pick, arrived_ref[:, : 3 * ncol], (((0,), (0,)), ((), ())), preferred_element_type=jnp.float32
    )
    for j in range(3):
        stress_ref[j] = placed[:, j * ncol : (j + 1) * ncol]
    sums_ref[...] = jnp.zeros_like(sums_ref)

    def add(name, product):
        k = AT[name]
        sums_ref[k : k + 1, :] += column_sums(product)

    for s in range(slots):
        at = slice(s * prows, (s + 1) * prows)
        shape = (prows, ncol)
        live = live_of(rows_ref, s, shape)
        thick, support, prec = thick_ref[at, :], support_ref[at, :], prec_ref[at, :]
        nuu, nvv, nuv = (stress_ref[j, at, :] for j in range(3))
        for v in range(2):
            w = jnp.where(live, vec_ref[v, at, :], 0.0)
            g_ref[v] = geometric(w, live, nuu, nvv, nuv)
            ug_ref[v, at, :] = prec * g_ref[v]
        for a in range(2):
            wa = jnp.where(live, vec_ref[a, at, :], 0.0)
            for b in range(a, 2):
                add(("kxx", a, b), wa * k_ref[b, at, :])
                add(("gxx", a, b), wa * g_ref[b])
                add(("kpk", a, b), k_ref[a, at, :] * uk_ref[b, at, :])
                add(("gpg", a, b), g_ref[a] * ug_ref[b, at, :])
            for b in range(2):
                add(("kpg", a, b), k_ref[a, at, :] * ug_ref[b, at, :])
        basis = [(ug_ref, 0), (ug_ref, 1), (uk_ref, 0), (uk_ref, 1)]
        for a in range(4):
            ref, v = basis[a]
            w = ref[v, at, :]
            kw = stiffness(w, live, thick, support)
            gw = geometric(w, live, nuu, nvv, nuv)
            for b in range(a + 1):
                ref, v = basis[b]
                other = ref[v, at, :]
                add(("kuu", b, a), other * kw)
                add(("guu", b, a), other * gw)
        last = s * prows + rows_ref[s] - 1
        for a in range(4):
            ref, v = basis[a]
            to = 4 * (4 * s + a)
            out_ref[to : to + 1, :] = ref[v, pl.ds(last - 1, 1), :]
            out_ref[to + 1 : to + 2, :] = ref[v, pl.ds(last, 1), :]
            out_ref[to + 2 : to + 4, :] = ref[v, s * prows : s * prows + 2, :]
    to = 16 * slots
    out_ref[to : to + 8, :LANES] = packed(sums_ref[...])
    for s in range(slots):
        out_ref[to + s : to + s + 1, LANES:] = jnp.full((1, ncol - LANES), match_ref[s], jnp.int32).astype(jnp.float32)


def apply_kernel(
    rows_ref, thick_ref, support_ref, prec_ref, stress_ref, ug_ref, uk_ref, pk_ref, pg_ref,
):
    slots = rows_ref.shape[0]
    rows_dev, ncol = thick_ref.shape
    prows = rows_dev // slots
    for s in range(slots):
        at = slice(s * prows, (s + 1) * prows)
        live = live_of(rows_ref, s, (prows, ncol))
        thick, support, prec = thick_ref[at, :], support_ref[at, :], prec_ref[at, :]
        nuu, nvv, nuv = (stress_ref[j, at, :] for j in range(3))
        for a, (ref, v) in enumerate([(ug_ref, 0), (ug_ref, 1), (uk_ref, 0), (uk_ref, 1)]):
            w = ref[v, at, :]
            pk_ref[a, at, :] = prec * stiffness(w, live, thick, support)
            pg_ref[a, at, :] = prec * geometric(w, live, nuu, nvv, nuv)


def line_kernel(slots, line_ref, out_ref, sums_ref):
    owners, _, ncol = line_ref.shape
    tag = 16 * slots
    total = line_ref[0, tag : tag + 8, :LANES]
    for z in range(1, owners):
        total = total + line_ref[z, tag : tag + 8, :LANES]
    sums_ref[...] = jnp.zeros_like(sums_ref)
    for z in range(owners):
        for s in range(slots):
            wanted = line_ref[z, tag + s : tag + s + 1, LANES : 2 * LANES][:, :1]
            jumps, slopes = [], []
            for a in range(4):
                own = line_ref[z, 4 * (4 * s + a) : 4 * (4 * s + a) + 2, :]
                bottom = jnp.zeros((2, ncol), jnp.float32)
                for near in {(z + 1) % owners, (z - 1) % owners}:
                    for t in range(slots):
                        strip = line_ref[near, 4 * (4 * t + a) + 2 : 4 * (4 * t + a) + 4, :]
                        bottom = bottom + jnp.where(wanted == float(near * slots + t), strip, 0.0)
                jumps.append(own[1:2] - bottom[0:1])
                slopes.append(own[1:2] - own[0:1] - (bottom[1:2] - bottom[0:1]))
            for a, b in UU:
                k = AT["kuu", a, b]
                sums_ref[k : k + 1, :] += (
                    penalty_value * jumps[a] * jumps[b] + penalty_slope * slopes[a] * slopes[b]
                )
    out_ref[...] = total + packed(sums_ref[...])


def form(table, left, right):
    total = None
    for i, c in left.items():
        for j, d in right.items():
            term = c * d * table[i, j]
            total = term if total is None else total + term
    return total


def final_kernel(
    cells, rows_ref, mine_ref, match_ref, total_ref, vec_ref, ug_ref, uk_ref, prec_ref, pk_ref, pg_ref,
    edge_ref, below_ref, above_ref, sent_ref, line_ref, out_ref,
):
    slots = rows_ref.shape[0]
    rows_dev, ncol = prec_ref.shape
    prows = rows_dev // slots
    owners = line_ref.shape[0]
    total = total_ref[...]

    def value(*name):
        k = AT[name]
        return total[k % 8 : k % 8 + 1, k // 8 : k // 8 + 1]

    k_table, g_table = {}, {}

    def put(table, i, j, what):
        table[i, j] = what
        table[j, i] = what

    for a in range(2):
        for b in range(2):
            lo, hi = min(a, b), max(a, b)
            put(k_table, a, b, value("kxx", lo, hi))
            put(g_table, a, b, value("gxx", lo, hi))
            put(k_table, a, 2 + b, value("kpg", a, b))
            put(k_table, a, 4 + b, value("kpk", lo, hi))
            put(g_table, a, 2 + b, value("gpg", lo, hi))
            put(g_table, a, 4 + b, value("kpg", b, a))
    for a, b in UU:
        put(k_table, 2 + a, 2 + b, value("kuu", a, b))
        put(g_table, 2 + a, 2 + b, value("guu", a, b))

    first_a, cross_k, second_a = k_table[0, 0], k_table[0, 1], k_table[1, 1]
    first_g, cross_g, second_g = g_table[0, 0], g_table[0, 1], g_table[1, 1]
    ratio = cross_k / first_a
    other_a = second_a - ratio * cross_k
    other_q = second_g - 2.0 * ratio * cross_g + ratio * ratio * first_g
    mu_first = first_g / first_a
    mu_other = other_q / other_a
    scale_first = jnp.sqrt(norm_scale * cells / first_a)
    scale_other = jnp.sqrt(norm_scale * cells / other_a)
    one = jnp.ones_like(ratio)
    new_first = {0: scale_first, 2: scale_first, 4: -scale_first * mu_first}
    new_second = {
        0: -scale_other * ratio,
        1: scale_other,
        2: -scale_other * ratio,
        3: scale_other,
        4: scale_other * mu_other * ratio,
        5: -scale_other * mu_other,
    }
    a1 = form(k_table, new_first, new_first)
    c = form(k_table, new_first, new_second)
    a2 = form(k_table, new_second, new_second)
    g1 = form(g_table, new_first, new_first)
    h = form(g_table, new_first, new_second)
    g2 = form(g_table, new_second, new_second)
    r = c / a1
    b2 = a2 - r * c
    q2 = g2 - 2.0 * r * h + r * r * g1
    mus = [g1 / a1, q2 / b2]
    scales = [jnp.sqrt(norm_scale * cells / a1), jnp.sqrt(norm_scale * cells / b2)]
    zero = jnp.zeros_like(one)
    lead = [new_first, {i: new_second[i] - r * new_first.get(i, zero) for i in new_second}]
    for s in range(slots):
        at = slice(s * prows, (s + 1) * prows)
        live = live_of(rows_ref, s, (prows, ncol))
        basis = [jnp.where(live, vec_ref[v, at, :], 0.0) for v in range(2)]
        basis += [ug_ref[v, at, :] for v in range(2)] + [uk_ref[v, at, :] for v in range(2)]
        for v in range(2):
            acc = None
            coef = dict(lead[v])
            for i in (0, 1):
                if i in lead[v]:
                    coef[2 + i] = coef.get(2 + i, zero) + lead[v][i]
                    coef[4 + i] = coef.get(4 + i, zero) - mus[v] * lead[v][i]
            for i, f in coef.items():
                term = (scales[v] * f) * basis[i]
                acc = term if acc is None else acc + term
            for i in range(2, 6):
                if i in lead[v]:
                    f = scales[v] * lead[v][i]
                    acc = acc + f * pg_ref[i - 2, at, :] - (f * mus[v]) * pk_ref[i - 2, at, :]
            out_ref[v, at, :] = acc
    for s in range(slots):
        own_id = mine_ref[s].astype(jnp.float32)
        want_id = match_ref[s].astype(jnp.float32)
        last = s * prows + rows_ref[s] - 1
        first = s * prows
        own, top, bottom = [], [], []
        for a in range(4):
            own.append(sent_ref[4 * (4 * s + a) : 4 * (4 * s + a) + 4, :])
            t_part = jnp.zeros((2, ncol), jnp.float32)
            b_part = jnp.zeros((2, ncol), jnp.float32)
            for z in range(owners):
                for t in range(slots):
                    strip = line_ref[z, 4 * (4 * t + a) : 4 * (4 * t + a) + 4, :]
                    wants = line_ref[z, 16 * slots + t : 16 * slots + t + 1, LANES : 2 * LANES][:, :1]
                    t_part = t_part + jnp.where(wants == own_id, strip[0:2], 0.0)
                    b_part = b_part + jnp.where(want_id == float(z * slots + t), strip[2:4], 0.0)
            top.append(t_part)
            bottom.append(b_part)
        for v in range(2):
            sides = []
            for strips in (own, top, bottom):
                acc = None
                for i in range(2, 6):
                    if i in lead[v]:
                        term = lead[v][i] * strips[i - 2]
                        acc = term if acc is None else acc + term
                sides.append(acc)
            o, t, b = sides
            jump_t = o[1:2] - b[0:1]
            slope_t = o[1:2] - o[0:1] - (b[1:2] - b[0:1])
            jump_b = t[1:2] - o[2:3]
            slope_b = t[1:2] - t[0:1] - (o[3:4] - o[2:3])
            gain = -scales[v] * mus[v]

            def put_row(row, what):
                out_ref[v, pl.ds(row, 1), :] += gain * prec_ref[pl.ds(row, 1), :] * what

            put_row(last, penalty_value * jump_t + penalty_slope * slope_t)
            put_row(last - 1, -penalty_slope * slope_t)
            put_row(first, -penalty_value * jump_b + penalty_slope * slope_b)
            put_row(first + 1, -penalty_slope * slope_b)


def call(body, outs, kinds, scratch=(), flops=1_000_000):
    spaces = {"s": pltpu.SMEM, "v": pltpu.VMEM}
    return pl.pallas_call(
        body,
        out_shape=[jax.ShapeDtypeStruct(s, d) for s, d in outs],
        in_specs=[pl.BlockSpec(memory_space=spaces[k]) for k in kinds],
        out_specs=[pl.BlockSpec(memory_space=pltpu.VMEM) for _ in outs],
        scratch_shapes=[pltpu.VMEM(s, jnp.float32) for s in scratch],
        compiler_params=pltpu.CompilerParams(vmem_limit_bytes=32 * 1024 * 1024),
        cost_estimate=pl.CostEstimate(flops=flops, bytes_accessed=2_000_000, transcendentals=0),
    )


def per_device(vectors, prestress, thickness, foundation, patch_rows, matched, elem_row):
    owners = lax.axis_size("patch")
    inner = lax.axis_size(("sub", "half"))
    slots = patch_rows.shape[0]
    rows_dev, ncol = thickness.shape
    f32 = jnp.float32
    mine = lax.axis_index("patch") * slots + jnp.arange(slots, dtype=jnp.int32)
    match = matched // (inner * slots) * slots + matched % slots
    local_row = (elem_row % rows_dev).reshape(1, rows_dev)
    cells = float(owners * inner * rows_dev * ncol)

    width = 3 * ncol + LANES
    edge_rows = -(-10 * slots // 8) * 8
    payload, edges = call(
        pack_kernel,
        [((rows_dev, width), jnp.bfloat16), ((edge_rows, ncol), f32)],
        "sssvvv",
    )(patch_rows, mine, match, jnp.transpose(prestress, (1, 0, 2)), local_row, vectors)
    arrived = lax.all_to_all(
        payload, ("patch", "sub", "half"), split_axis=0, concat_axis=0, tiled=True
    )
    below = passed_along(edges, "patch", 1)
    above = passed_along(edges, "patch", -1)
    field = ((2, rows_dev, ncol), f32)
    four = ((4, rows_dev, ncol), f32)
    one = ((rows_dev, ncol), f32)
    k_x, u_k, prec = call(stiff_kernel, [field, field, one], "sssvvvvvv")(
        patch_rows, mine, match, vectors, thickness, foundation, edges, below, above
    )
    sent_rows = 16 * slots + 8
    u_g, stress, sent = call(
        gram_kernel,
        [field, ((3, rows_dev, ncol), f32), ((sent_rows, ncol), f32)],
        "ssvvvvvvv",
        [(SUMS, ncol), (2, rows_dev // slots, ncol)],
    )(patch_rows, match, arrived, vectors, thickness, foundation, prec, k_x, u_k)
    line = lax.all_to_all(
        jnp.broadcast_to(sent[None], (owners, sent_rows, ncol)), "patch", split_axis=0, concat_axis=0, tiled=True
    )
    pk, pg = call(apply_kernel, [four, four], "svvvvvv")(
        patch_rows, thickness, foundation, prec, stress, u_g, u_k
    )
    (total,) = call(
        functools.partial(line_kernel, slots), [((8, LANES), f32)], "v", [(SUMS, ncol)]
    )(line)
    total = summed_over(summed_over(total, "half"), "sub")
    (modes,) = call(functools.partial(final_kernel, cells), [field], "sssvvvvvvvvvvvv")(
        patch_rows, mine, match, total, vectors, u_g, u_k, prec, pk, pg, edges, below, above, sent, line
    )
    return modes


def solution(mesh):
    in_specs = (
        P(None, ("groups", "patch", "sub", "half"), None),
        P(("groups", "patch", "sub", "half"), None, None),
        P(("groups", "patch", "sub", "half"), None),
        P(("groups", "patch", "sub", "half"), None),
        P(("groups", "patch", "sub", "half")),
        P(("groups", "patch", "sub", "half")),
        P(("groups", "patch", "sub", "half")),
    )
    out_specs = P(None, ("groups", "patch", "sub", "half"), None)
    return jax.shard_map(
        per_device, mesh=mesh, in_specs=in_specs, out_specs=out_specs, check_vma=False
    )
```

```python
import functools

import jax
import jax.numpy as jnp
from jax import lax
from jax.experimental import pallas as pl
from jax.experimental.pallas import tpu as pltpu
from jax.sharding import PartitionSpec as P

norm_scale = 16.0
penalty_value = 8.0
penalty_slope = 4.0
LANES = 128

UU = [(a, b) for a in range(4) for b in range(a, 4)]
NAMES = (
    [("kuu", a, b) for a, b in UU]
    + [("guu", a, b) for a, b in UU]
    + [("kxx", 0, 0), ("kxx", 0, 1), ("kxx", 1, 1)]
    + [("gxx", 0, 0), ("gxx", 0, 1), ("gxx", 1, 1)]
    + [("kpk", 0, 0), ("kpk", 0, 1), ("kpk", 1, 1)]
    + [("kpg", a, b) for a in range(2) for b in range(2)]
    + [("gpg", 0, 0), ("gpg", 0, 1), ("gpg", 1, 1)]
)
AT = {name: k for k, name in enumerate(NAMES)}
SUMS = 40
TILES = SUMS // 8


def passed_along(array, axis, by):
    peers = lax.axis_size(axis)
    return lax.ppermute(array, axis, [(i, (i + by) % peers) for i in range(peers)])


def summed_over(array, axis):
    total = array
    for by in range(1, lax.axis_size(axis)):
        total = total + passed_along(array, axis, by)
    return total


def iota(shape, axis):
    return lax.broadcasted_iota(jnp.int32, shape, axis)


def row_after(w):
    n = w.shape[0]
    return jnp.where(iota(w.shape, 0) < n - 1, pltpu.roll(w, n - 1, 0), 0.0)


def row_before(w):
    return jnp.where(iota(w.shape, 0) > 0, pltpu.roll(w, 1, 0), 0.0)


def col_after(w):
    n = w.shape[1]
    return jnp.where(iota(w.shape, 1) < n - 1, pltpu.roll(w, n - 1, 1), 0.0)


def col_before(w):
    return jnp.where(iota(w.shape, 1) > 0, pltpu.roll(w, 1, 1), 0.0)


def second_rows(w):
    return row_before(w) + row_after(w) - 2.0 * w


def second_cols(w):
    return col_before(w) + col_after(w) - 2.0 * w


def stiffness(w, live, thick, support):
    bend_rows = jnp.where(live, thick * second_rows(w), 0.0)
    bend_cols = thick * second_cols(w)
    return jnp.where(live, support * w + second_rows(bend_rows) + second_cols(bend_cols), 0.0)


def geometric(w, live, nuu, nvv, nuv):
    along_rows = row_after(w) - w
    along_cols = col_after(w) - w
    rows = nuu * along_rows + nuv * along_cols
    cols = nvv * along_cols + nuv * along_rows
    return jnp.where(live, row_before(rows) - rows + col_before(cols) - cols, 0.0)


def live_of(rows_ref, slot, shape):
    return iota(shape, 0) < rows_ref[slot]


def column_sums(product):
    return jnp.sum(product, axis=0, keepdims=True)


def packed(sums):
    totals = jnp.sum(sums, axis=1, keepdims=True)
    lane = iota((8, LANES), 1)
    out = jnp.zeros((8, LANES), jnp.float32)
    for tile in range(TILES):
        out = jnp.where(lane == tile, totals[8 * tile : 8 * tile + 8], out)
    return out


def place(rows_ref, matched_ref, slots):
    inner = lax.axis_size(("sub", "half"))
    mine = [lax.axis_index("patch") * slots + s for s in range(slots)]
    match = [
        matched_ref[s] // (inner * slots) * slots + lax.rem(matched_ref[s], slots) for s in range(slots)
    ]
    return mine, match


def label(number, ncol):
    return jnp.full((1, ncol), number, jnp.int32).astype(jnp.float32)


def pack_kernel(stress_ref, elem_ref, pay_ref, elem, index, sems):
    rows_dev, ncol = stress_ref.shape[1:]
    get = pltpu.make_async_copy(elem_ref, elem, sems.at[0])
    get.start()
    planes = [
        pltpu.make_async_copy(
            stress_ref.at[j], pay_ref.at[:, pl.ds(j * ncol, ncol)], sems.at[1 + j]
        )
        for j in range(3)
    ]
    for copy in planes:
        copy.start()
    get.wait()
    square = (rows_dev, rows_dev)
    if rows_dev & (rows_dev - 1) == 0:
        local = jnp.bitwise_and(elem[...], rows_dev - 1)
    else:
        local = lax.rem(elem[...], rows_dev)
    spread = jnp.broadcast_to(local.astype(jnp.float32), square)
    column = jnp.sum(
        jnp.where(iota(square, 0) == iota(square, 1), spread, 0.0), axis=1, keepdims=True
    )
    index[...] = jnp.broadcast_to(column, (rows_dev, LANES)).astype(jnp.bfloat16)
    put = pltpu.make_async_copy(index, pay_ref.at[:, pl.ds(3 * ncol, LANES)], sems.at[4])
    put.start()
    for copy in planes:
        copy.wait()
    put.wait()


def edge_kernel(rows_ref, matched_ref, vec_ref, edge_ref):
    slots = rows_ref.shape[0]
    rows_dev, ncol = vec_ref.shape[1:]
    prows = rows_dev // slots
    mine, match = place(rows_ref, matched_ref, slots)
    for s in range(slots):
        last = s * prows + rows_ref[s] - 1
        for v in range(2):
            at = 4 * (2 * s + v)
            edge_ref[at : at + 1, :] = vec_ref[v, pl.ds(last - 1, 1), :]
            edge_ref[at + 1 : at + 2, :] = vec_ref[v, pl.ds(last, 1), :]
            edge_ref[at + 2 : at + 4, :] = vec_ref[v, s * prows : s * prows + 2, :]
        at = 8 * slots
        edge_ref[at + s : at + s + 1, :] = label(mine[s], ncol)
        edge_ref[at + slots + s : at + slots + s + 1, :] = label(match[s], ncol)
    used = 10 * slots
    edge_ref[used:, :] = jnp.zeros((edge_ref.shape[0] - used, ncol), jnp.float32)


def stiff_kernel(rows_ref, vec_ref, thick_ref, support_ref, k_ref, uk_ref, prec_ref, sums_ref):
    slots = rows_ref.shape[0]
    rows_dev, ncol = thick_ref.shape
    prows = rows_dev // slots
    sums_ref[...] = jnp.zeros_like(sums_ref)

    def add(name, product):
        k = AT[name]
        sums_ref[k : k + 1, :] += column_sums(product)

    for s in range(slots):
        at = slice(s * prows, (s + 1) * prows)
        live = live_of(rows_ref, s, (prows, ncol))
        thick, support = thick_ref[at, :], support_ref[at, :]
        prec_ref[at, :] = jnp.where(live, 1.0 / (support + 12.0 * thick), 0.0)
        for v in range(2):
            w = jnp.where(live, vec_ref[v, at, :], 0.0)
            k_ref[v, at, :] = stiffness(w, live, thick, support)
            uk_ref[v, at, :] = prec_ref[at, :] * k_ref[v, at, :]
        for a in range(2):
            wa = jnp.where(live, vec_ref[a, at, :], 0.0)
            for b in range(a, 2):
                add(("kxx", a, b), wa * k_ref[b, at, :])
                add(("kpk", a, b), k_ref[a, at, :] * uk_ref[b, at, :])


def interface_rows(own, top, bottom):
    jump_t = own[1:2] - bottom[0:1]
    slope_t = own[1:2] - own[0:1] - (bottom[1:2] - bottom[0:1])
    jump_b = top[1:2] - own[2:3]
    slope_b = top[1:2] - top[0:1] - (own[3:4] - own[2:3])
    return (
        -penalty_slope * slope_t,
        penalty_value * jump_t + penalty_slope * slope_t,
        -penalty_value * jump_b + penalty_slope * slope_b,
        -penalty_slope * slope_b,
    )


def edge_places(rows_ref, slot, prows):
    last = slot * prows + rows_ref[slot] - 1
    return (last - 1, last, slot * prows, slot * prows + 1)


def bend_kernel(
    rows_ref, matched_ref, arrived_ref, vec_ref, prec_ref, uk_ref, edge_ref, below_ref, above_ref,
    g_ref, ug_ref, stress_ref, extra_ref, out_ref,
):
    slots = rows_ref.shape[0]
    rows_dev, ncol = prec_ref.shape
    prows = rows_dev // slots
    halves = ncol // LANES
    mine, match = place(rows_ref, matched_ref, slots)
    index = arrived_ref[:, 3 * ncol :].astype(jnp.float32)
    lane = iota(index.shape, 1).astype(jnp.float32)
    pick = jnp.concatenate(
        [
            jnp.where(index == lane + float(h * LANES), 1.0, 0.0).astype(jnp.bfloat16)
            for h in range(rows_dev // LANES)
        ],
        axis=1,
    )
    placed = lax.dot_general(
        pick, arrived_ref[:, : 3 * ncol], (((0,), (0,)), ((), ())), preferred_element_type=jnp.float32
    )
    for j in range(3):
        stress_ref[j] = placed[:, j * ncol : (j + 1) * ncol]
    rows_sent = 16 * slots

    def send(to, row):
        for h in range(halves):
            out_ref[h * rows_sent + to : h * rows_sent + to + row.shape[0], :] = row[:, h * LANES : (h + 1) * LANES]

    for s in range(slots):
        at = slice(s * prows, (s + 1) * prows)
        live = live_of(rows_ref, s, (prows, ncol))
        nuu, nvv, nuv = (stress_ref[j, at, :] for j in range(3))
        for v in range(2):
            w = jnp.where(live, vec_ref[v, at, :], 0.0)
            g_ref[v, at, :] = geometric(w, live, nuu, nvv, nuv)
            ug_ref[v, at, :] = prec_ref[at, :] * g_ref[v, at, :]
        own_id, want_id = mine[s].astype(jnp.float32), match[s].astype(jnp.float32)
        places = edge_places(rows_ref, s, prows)
        for v in range(2):
            own = edge_ref[4 * (2 * s + v) : 4 * (2 * s + v) + 4, :]
            top = jnp.zeros((2, ncol), jnp.float32)
            bottom = jnp.zeros((2, ncol), jnp.float32)
            for ref in (below_ref, above_ref):
                for t in range(slots):
                    strip = ref[4 * (2 * t + v) : 4 * (2 * t + v) + 4, :]
                    label_t = ref[8 * slots + t : 8 * slots + t + 1, :]
                    wants = ref[9 * slots + t : 9 * slots + t + 1, :]
                    top = top + jnp.where(wants == own_id, strip[0:2], 0.0)
                    bottom = bottom + jnp.where(label_t == want_id, strip[2:4], 0.0)
            added = interface_rows(own, top, bottom)
            for i, row in enumerate(places):
                to = 4 * (2 * s + v) + i
                extra_ref[to : to + 1, :] = added[i]
                send(4 * (4 * s + 2 + v) + i, uk_ref[v, pl.ds(row, 1), :] + prec_ref[pl.ds(row, 1), :] * added[i])
                send(4 * (4 * s + v) + i, ug_ref[v, pl.ds(row, 1), :])
    tag = halves * rows_sent
    for s in range(slots):
        out_ref[tag + s : tag + s + 1, :] = label(match[s], LANES)
    out_ref[tag + slots :, :] = jnp.zeros((out_ref.shape[0] - tag - slots, LANES), jnp.float32)


def gram_kernel(
    rows_ref, extra_ref, vec_ref, thick_ref, support_ref, prec_ref, k_in, uk_in, sums_in,
    g_ref, ug_ref, stress_ref, uk_ref, kuk_ref, kug_ref, gu_ref, tile_ref, sums_ref, k_ref,
):
    slots = rows_ref.shape[0]
    rows_dev, ncol = thick_ref.shape
    prows = rows_dev // slots
    sums_ref[...] = sums_in[...]

    def add(name, product):
        k = AT[name]
        sums_ref[k : k + 1, :] += column_sums(product)

    for s in range(slots):
        at = slice(s * prows, (s + 1) * prows)
        live = live_of(rows_ref, s, (prows, ncol))
        thick, support, prec = thick_ref[at, :], support_ref[at, :], prec_ref[at, :]
        nuu, nvv, nuv = (stress_ref[j, at, :] for j in range(3))
        places = edge_places(rows_ref, s, prows)
        for v in range(2):
            k_ref[v, at, :] = k_in[v, at, :]
            uk_ref[v, at, :] = uk_in[v, at, :]
        add_k = [[extra_ref[4 * (2 * s + v) + i : 4 * (2 * s + v) + i + 1, :] for i in range(4)] for v in range(2)]
        for a in range(2):
            for b in range(a, 2):
                for i, row in enumerate(places):
                    p = prec_ref[pl.ds(row, 1), :]
                    ka, kb = k_in[a, pl.ds(row, 1), :], k_in[b, pl.ds(row, 1), :]
                    add(("kxx", a, b), vec_ref[a, pl.ds(row, 1), :] * add_k[b][i])
                    add(("kpk", a, b), p * (ka * add_k[b][i] + add_k[a][i] * (kb + add_k[b][i])))
        for v in range(2):
            for i, row in enumerate(places):
                k_ref[v, pl.ds(row, 1), :] += add_k[v][i]
                uk_ref[v, pl.ds(row, 1), :] += prec_ref[pl.ds(row, 1), :] * add_k[v][i]
        for v in range(2):
            kuk_ref[v, at, :] = stiffness(uk_ref[v, at, :], live, thick, support)
            kug_ref[v, at, :] = stiffness(ug_ref[v, at, :], live, thick, support)
        for a in range(2):
            wa = jnp.where(live, vec_ref[a, at, :], 0.0)
            for b in range(a, 2):
                add(("gxx", a, b), wa * g_ref[b, at, :])
                add(("gpg", a, b), g_ref[a, at, :] * ug_ref[b, at, :])
                add(("kuu", a, b), ug_ref[a, at, :] * kug_ref[b, at, :])
                add(("kuu", 2 + a, 2 + b), uk_ref[a, at, :] * kuk_ref[b, at, :])
            for b in range(2):
                add(("kpg", a, b), k_ref[a, at, :] * ug_ref[b, at, :])
                add(("kuu", a, 2 + b), ug_ref[a, at, :] * kuk_ref[b, at, :])
        basis = [(ug_ref, 0), (ug_ref, 1), (uk_ref, 0), (uk_ref, 1)]
        for a in range(4):
            ref, v = basis[a]
            gu_ref[a, at, :] = geometric(ref[v, at, :], live, nuu, nvv, nuv)
            for b in range(a + 1):
                ref, v = basis[b]
                add(("guu", b, a), ref[v, at, :] * gu_ref[a, at, :])
    tile_ref[...] = packed(sums_ref[...])


def strip_of(line_ref, z, at, rows, slots):
    halves = (line_ref.shape[1] - 1) // (16 * slots)
    return jnp.concatenate(
        [line_ref[z, h * 16 * slots + at : h * 16 * slots + at + rows, :] for h in range(halves)], axis=1
    )


def wanted_of(line_ref, z, slot, slots):
    halves = (line_ref.shape[1] - 1) // (16 * slots)
    tag = halves * 16 * slots
    return line_ref[z, tag + slot : tag + slot + 1, :1]


def line_kernel(slots, line_ref, out_ref, sums_ref):
    owners = line_ref.shape[0]
    sums_ref[...] = jnp.zeros_like(sums_ref)
    sums = {pair: None for pair in UU}
    for z in range(owners):
        for s in range(slots):
            wanted = wanted_of(line_ref, z, s, slots)
            jumps, slopes = [], []
            for a in range(4):
                own = strip_of(line_ref, z, 4 * (4 * s + a), 2, slots)
                bottom = jnp.zeros_like(own)
                for near in sorted({(z + 1) % owners, (z - 1) % owners}):
                    for t in range(slots):
                        strip = strip_of(line_ref, near, 4 * (4 * t + a) + 2, 2, slots)
                        bottom = bottom + jnp.where(wanted == float(near * slots + t), strip, 0.0)
                jumps.append(own[1:2] - bottom[0:1])
                slopes.append(own[1:2] - own[0:1] - (bottom[1:2] - bottom[0:1]))
            for a, b in UU:
                term = penalty_value * jumps[a] * jumps[b] + penalty_slope * slopes[a] * slopes[b]
                sums[a, b] = term if sums[a, b] is None else sums[a, b] + term
    for pair in UU:
        k = AT[("kuu",) + pair]
        sums_ref[k : k + 1, :] = sums[pair]
    out_ref[...] = packed(sums_ref[...])


def join_kernel(rows_ref, matched_ref, line_ref, kug_in, kuk_in, kug_ref, kuk_ref):
    kug_ref[...] = kug_in[...]
    kuk_ref[...] = kuk_in[...]
    slots = rows_ref.shape[0]
    rows_dev, ncol = kug_in.shape[1:]
    prows = rows_dev // slots
    owners = line_ref.shape[0]
    mine, match = place(rows_ref, matched_ref, slots)
    me = lax.axis_index("patch")
    for s in range(slots):
        own_id, want_id = mine[s].astype(jnp.float32), match[s].astype(jnp.float32)
        places = edge_places(rows_ref, s, prows)
        for a in range(4):
            own = jnp.zeros((4, ncol), jnp.float32)
            top = jnp.zeros((2, ncol), jnp.float32)
            bottom = jnp.zeros((2, ncol), jnp.float32)
            for z in range(owners):
                for t in range(slots):
                    strip = strip_of(line_ref, z, 4 * (4 * t + a), 4, slots)
                    top = top + jnp.where(wanted_of(line_ref, z, t, slots) == own_id, strip[0:2], 0.0)
                    bottom = bottom + jnp.where(want_id == float(z * slots + t), strip[2:4], 0.0)
                    if t == s:
                        own = own + jnp.where(me == z, strip, 0.0)
            ref = kug_ref if a < 2 else kuk_ref
            for row, added in zip(places, interface_rows(own, top, bottom)):
                ref[a % 2, pl.ds(row, 1), :] += added


def form(table, left, right):
    total = None
    for i, c in left.items():
        row = None
        for j, d in right.items():
            term = d * table[i, j]
            row = term if row is None else row + term
        total = c * row if total is None else total + c * row
    return total


def final_kernel(
    cells, rows_ref, total_ref, vec_ref, ug_ref, uk_ref, prec_ref, kug_ref, kuk_ref, gu_ref, out_ref
):
    slots = rows_ref.shape[0]
    rows_dev, ncol = prec_ref.shape
    prows = rows_dev // slots
    total = total_ref[...]

    def value(*name):
        k = AT[name]
        return total[k % 8 : k % 8 + 1, k // 8 : k // 8 + 1]

    k_table, g_table = {}, {}

    def put(table, i, j, what):
        table[i, j] = what
        table[j, i] = what

    for a in range(2):
        for b in range(2):
            lo, hi = min(a, b), max(a, b)
            put(k_table, a, b, value("kxx", lo, hi))
            put(g_table, a, b, value("gxx", lo, hi))
            put(k_table, a, 2 + b, value("kpg", a, b))
            put(k_table, a, 4 + b, value("kpk", lo, hi))
            put(g_table, a, 2 + b, value("gpg", lo, hi))
            put(g_table, a, 4 + b, value("kpg", b, a))
    for a, b in UU:
        put(k_table, 2 + a, 2 + b, value("kuu", a, b))
        put(g_table, 2 + a, 2 + b, value("guu", a, b))

    first_a, cross_k, second_a = k_table[0, 0], k_table[0, 1], k_table[1, 1]
    first_g, cross_g, second_g = g_table[0, 0], g_table[0, 1], g_table[1, 1]
    ratio = cross_k / first_a
    other_a = second_a - ratio * cross_k
    other_q = second_g - 2.0 * ratio * cross_g + ratio * ratio * first_g
    mu_first = first_g / first_a
    mu_other = other_q / other_a
    scale_first = jnp.sqrt(norm_scale * cells / first_a)
    scale_other = jnp.sqrt(norm_scale * cells / other_a)
    new_first = {0: scale_first, 2: scale_first, 4: -scale_first * mu_first}
    new_second = {
        0: -scale_other * ratio,
        1: scale_other,
        2: -scale_other * ratio,
        3: scale_other,
        4: scale_other * mu_other * ratio,
        5: -scale_other * mu_other,
    }
    a1 = form(k_table, new_first, new_first)
    c = form(k_table, new_first, new_second)
    a2 = form(k_table, new_second, new_second)
    g1 = form(g_table, new_first, new_first)
    h = form(g_table, new_first, new_second)
    g2 = form(g_table, new_second, new_second)
    r = c / a1
    b2 = a2 - r * c
    q2 = g2 - 2.0 * r * h + r * r * g1
    mus = [g1 / a1, q2 / b2]
    scales = [jnp.sqrt(norm_scale * cells / a1), jnp.sqrt(norm_scale * cells / b2)]
    lead = [
        {i: scales[0] * f for i, f in new_first.items()},
        {i: scales[1] * (f - r * new_first[i] if i in new_first else f) for i, f in new_second.items()},
    ]
    for s in range(slots):
        at = slice(s * prows, (s + 1) * prows)
        live = live_of(rows_ref, s, (prows, ncol))
        basis = [jnp.where(live, vec_ref[v, at, :], 0.0) for v in range(2)]
        basis += [ug_ref[v, at, :] for v in range(2)] + [uk_ref[v, at, :] for v in range(2)]
        for v in range(2):
            coef = dict(lead[v])
            for i in (0, 1):
                if i in lead[v]:
                    coef[2 + i] = coef[2 + i] + lead[v][i]
                    coef[4 + i] = coef[4 + i] - mus[v] * lead[v][i]
            acc = inside = None
            for i, f in coef.items():
                term = f * basis[i]
                acc = term if acc is None else acc + term
            for i in range(2, 6):
                if i in lead[v]:
                    k_part = kug_ref[i - 2, at, :] if i < 4 else kuk_ref[i - 4, at, :]
                    term = lead[v][i] * gu_ref[i - 2, at, :] - (lead[v][i] * mus[v]) * k_part
                    inside = term if inside is None else inside + term
            out_ref[v, at, :] = acc + prec_ref[at, :] * inside


def call(body, outs, kinds, scratch=(), flops=1_000_000, out_kind="v"):
    spaces = {"s": pltpu.SMEM, "v": pltpu.VMEM, "h": pltpu.HBM}
    return pl.pallas_call(
        body,
        out_shape=[jax.ShapeDtypeStruct(s, d) for s, d in outs],
        in_specs=[pl.BlockSpec(memory_space=spaces[k]) for k in kinds],
        out_specs=[pl.BlockSpec(memory_space=spaces[out_kind]) for _ in outs],
        scratch_shapes=list(scratch),
        compiler_params=pltpu.CompilerParams(vmem_limit_bytes=32 * 1024 * 1024),
        cost_estimate=pl.CostEstimate(flops=flops, bytes_accessed=2_000_000, transcendentals=0),
    )


def per_device(vectors, prestress, thickness, foundation, patch_rows, matched, elem_row):
    owners = lax.axis_size("patch")
    inner = lax.axis_size(("sub", "half"))
    slots = patch_rows.shape[0]
    rows_dev, ncol = thickness.shape
    f32, bf16 = jnp.float32, jnp.bfloat16
    cells = float(owners * inner * rows_dev * ncol)
    field = ((2, rows_dev, ncol), f32)
    one = ((rows_dev, ncol), f32)
    sums = ((SUMS, ncol), f32)
    tile = ((8, LANES), f32)

    width = 3 * ncol + LANES
    (payload,) = call(
        pack_kernel,
        [((rows_dev, width), bf16)],
        "hh",
        [
            pltpu.VMEM((1, rows_dev), jnp.int32),
            pltpu.VMEM((rows_dev, LANES), bf16),
            pltpu.SemaphoreType.DMA((5,)),
        ],
        out_kind="h",
    )(jnp.transpose(prestress, (1, 0, 2)), elem_row.reshape(1, rows_dev))
    arrived = lax.all_to_all(
        payload, ("patch", "sub", "half"), split_axis=0, concat_axis=0, tiled=True
    )
    edge_rows = -(-10 * slots // 8) * 8
    (edges,) = call(edge_kernel, [((edge_rows, ncol), f32)], "ssv")(patch_rows, matched, vectors)
    below = passed_along(edges, "patch", 1)
    above = passed_along(edges, "patch", -1)
    k_x, u_k, prec, part = call(stiff_kernel, [field, field, one, sums], "svvv")(
        patch_rows, vectors, thickness, foundation
    )
    sent_rows = (ncol // LANES) * 16 * slots + -(-slots // 8) * 8
    g_x, u_g, stress, extra, sent = call(
        bend_kernel,
        [field, field, ((3, rows_dev, ncol), f32), ((8 * slots, ncol), f32), ((sent_rows, LANES), f32)],
        "ssvvvvvvv",
    )(patch_rows, matched, arrived, vectors, prec, u_k, edges, below, above)
    line = lax.all_to_all(
        jnp.broadcast_to(sent[None], (owners, sent_rows, LANES)), "patch", split_axis=0, concat_axis=0, tiled=True
    )
    u_k, k_uk, k_ug, g_u, local = call(
        gram_kernel,
        [field, field, field, ((4, rows_dev, ncol), f32), tile],
        "svvvvvvvvvvv",
        [pltpu.VMEM((SUMS, ncol), f32), pltpu.VMEM((2, rows_dev, ncol), f32)],
    )(patch_rows, extra, vectors, thickness, foundation, prec, k_x, u_k, part, g_x, u_g, stress)
    local = summed_over(local, "patch")
    (across,) = call(
        functools.partial(line_kernel, slots), [tile], "v", [pltpu.VMEM((SUMS, ncol), f32)]
    )(line)
    total = summed_over(summed_over(local + across, "half"), "sub")
    k_ug, k_uk = call(join_kernel, [field, field], "ssvvv")(
        patch_rows, matched, line, k_ug, k_uk
    )
    (modes,) = call(functools.partial(final_kernel, cells), [field], "svvvvvvvv")(
        patch_rows, total, vectors, u_g, u_k, prec, k_ug, k_uk, g_u
    )
    return modes


def solution(mesh):
    in_specs = (
        P(None, ("groups", "patch", "sub", "half"), None),
        P(("groups", "patch", "sub", "half"), None, None),
        P(("groups", "patch", "sub", "half"), None),
        P(("groups", "patch", "sub", "half"), None),
        P(("groups", "patch", "sub", "half")),
        P(("groups", "patch", "sub", "half")),
        P(("groups", "patch", "sub", "half")),
    )
    out_specs = P(None, ("groups", "patch", "sub", "half"), None)
    return jax.shard_map(
        per_device, mesh=mesh, in_specs=in_specs, out_specs=out_specs, check_vma=False
    )
```

```python
import functools

import jax
import jax.numpy as jnp
from jax import lax
from jax.experimental import pallas as pl
from jax.experimental.pallas import tpu as pltpu
from jax.sharding import PartitionSpec as P

norm_scale = 16.0
penalty_value = 8.0
penalty_slope = 4.0
LANES = 128

UU = [(a, b) for a in range(4) for b in range(a, 4)]
NAMES = (
    [("kuu", a, b) for a, b in UU]
    + [("guu", a, b) for a, b in UU]
    + [("kxx", 0, 0), ("kxx", 0, 1), ("kxx", 1, 1)]
    + [("gxx", 0, 0), ("gxx", 0, 1), ("gxx", 1, 1)]
    + [("kpk", 0, 0), ("kpk", 0, 1), ("kpk", 1, 1)]
    + [("kpg", a, b) for a in range(2) for b in range(2)]
    + [("gpg", 0, 0), ("gpg", 0, 1), ("gpg", 1, 1)]
)
AT = {name: k for k, name in enumerate(NAMES)}
SUMS = 40
TILES = SUMS // 8


def passed_along(array, axis, by):
    peers = lax.axis_size(axis)
    return lax.ppermute(array, axis, [(i, (i + by) % peers) for i in range(peers)])


def summed_over(array, axis):
    total = array
    for by in range(1, lax.axis_size(axis)):
        total = total + passed_along(array, axis, by)
    return total


def iota(shape, axis):
    return lax.broadcasted_iota(jnp.int32, shape, axis)


def row_after(w):
    n = w.shape[0]
    return jnp.where(iota(w.shape, 0) < n - 1, pltpu.roll(w, n - 1, 0), 0.0)


def row_before(w):
    return jnp.where(iota(w.shape, 0) > 0, pltpu.roll(w, 1, 0), 0.0)


def col_after(w):
    n = w.shape[1]
    return jnp.where(iota(w.shape, 1) < n - 1, pltpu.roll(w, n - 1, 1), 0.0)


def col_before(w):
    return jnp.where(iota(w.shape, 1) > 0, pltpu.roll(w, 1, 1), 0.0)


def second_rows(w):
    return row_before(w) + row_after(w) - 2.0 * w


def second_cols(w):
    return col_before(w) + col_after(w) - 2.0 * w


def stiffness(w, live, thick, support):
    bend_rows = jnp.where(live, thick * second_rows(w), 0.0)
    bend_cols = thick * second_cols(w)
    return jnp.where(live, support * w + second_rows(bend_rows) + second_cols(bend_cols), 0.0)


def geometric(w, live, nuu, nvv, nuv):
    along_rows = row_after(w) - w
    along_cols = col_after(w) - w
    rows = nuu * along_rows + nuv * along_cols
    cols = nvv * along_cols + nuv * along_rows
    return jnp.where(live, row_before(rows) - rows + col_before(cols) - cols, 0.0)


def live_of(rows_ref, slot, shape):
    return iota(shape, 0) < rows_ref[slot]


def column_sums(product):
    return jnp.sum(product, axis=0, keepdims=True)


def packed(rows):
    rows = list(rows)
    rows += [jnp.zeros_like(rows[0])] * (-len(rows) % 8)
    lane = iota((8, LANES), 1)
    out = jnp.zeros((8, LANES), jnp.float32)
    for tile in range(len(rows) // 8):
        total = jnp.sum(jnp.concatenate(rows[8 * tile : 8 * tile + 8], axis=0), axis=1, keepdims=True)
        out = jnp.where(lane == tile, total, out)
    return out


def place(rows_ref, matched_ref, slots):
    inner = lax.axis_size(("sub", "half"))
    mine = [lax.axis_index("patch") * slots + s for s in range(slots)]
    match = [
        matched_ref[s] // (inner * slots) * slots + lax.rem(matched_ref[s], slots) for s in range(slots)
    ]
    return mine, match


def label(number, ncol):
    return jnp.full((1, ncol), number, jnp.int32).astype(jnp.float32)


def pack_kernel(stress_ref, elem_ref, pay_ref, elem, held, sems):
    rows_dev, ncol = stress_ref.shape[1:]
    get = pltpu.make_async_copy(elem_ref, elem, sems.at[0])
    get.start()
    planes = [
        pltpu.make_async_copy(stress_ref.at[j], held.at[:, pl.ds(j * ncol, ncol)], sems.at[1 + j])
        for j in range(3)
    ]
    for copy in planes:
        copy.start()
    get.wait()
    square = (rows_dev, rows_dev)
    if rows_dev & (rows_dev - 1) == 0:
        local = jnp.bitwise_and(elem[...], rows_dev - 1)
    else:
        local = lax.rem(elem[...], rows_dev)
    spread = jnp.broadcast_to(local.astype(jnp.float32), square)
    column = jnp.sum(
        jnp.where(iota(square, 0) == iota(square, 1), spread, 0.0), axis=1, keepdims=True
    )
    held[:, 3 * ncol :] = jnp.broadcast_to(column, (rows_dev, LANES)).astype(jnp.bfloat16)
    for copy in planes:
        copy.wait()
    put = pltpu.make_async_copy(held, pay_ref, sems.at[4])
    put.start()
    put.wait()


def edge_kernel(rows_ref, matched_ref, vec_ref, edge_ref):
    slots = rows_ref.shape[0]
    rows_dev, ncol = vec_ref.shape[1:]
    prows = rows_dev // slots
    mine, match = place(rows_ref, matched_ref, slots)
    for s in range(slots):
        last = s * prows + rows_ref[s] - 1
        for v in range(2):
            at = 4 * (2 * s + v)
            edge_ref[at : at + 1, :] = vec_ref[v, pl.ds(last - 1, 1), :]
            edge_ref[at + 1 : at + 2, :] = vec_ref[v, pl.ds(last, 1), :]
            edge_ref[at + 2 : at + 4, :] = vec_ref[v, s * prows : s * prows + 2, :]
        at = 8 * slots
        edge_ref[at + s : at + s + 1, :] = label(mine[s], ncol)
        edge_ref[at + slots + s : at + slots + s + 1, :] = label(match[s], ncol)
    used = 10 * slots
    edge_ref[used:, :] = jnp.zeros((edge_ref.shape[0] - used, ncol), jnp.float32)


def folded(product):
    return jnp.sum(product.reshape(product.shape[0] // 8, 8, product.shape[1]), axis=0)


def stiff_kernel(rows_ref, vec_ref, thick_ref, support_ref, k_ref, uk_ref, kuk_ref, prec_ref, sums_ref):
    slots = rows_ref.shape[0]
    rows_dev, ncol = thick_ref.shape
    prows = rows_dev // slots
    sums_ref[...] = jnp.zeros_like(sums_ref)

    def add(name, product):
        k = 8 * AT[name]
        sums_ref[k : k + 8, :] += folded(product)

    for s in range(slots):
        at = slice(s * prows, (s + 1) * prows)
        live = live_of(rows_ref, s, (prows, ncol))
        thick, support = thick_ref[at, :], support_ref[at, :]
        prec_ref[at, :] = jnp.where(live, 1.0 / (support + 12.0 * thick), 0.0)
        for v in range(2):
            w = jnp.where(live, vec_ref[v, at, :], 0.0)
            k_ref[v, at, :] = stiffness(w, live, thick, support)
            uk_ref[v, at, :] = prec_ref[at, :] * k_ref[v, at, :]
        for v in range(2):
            kuk_ref[v, at, :] = stiffness(uk_ref[v, at, :], live, thick, support)
        for a in range(2):
            wa = jnp.where(live, vec_ref[a, at, :], 0.0)
            for b in range(a, 2):
                add(("kxx", a, b), wa * k_ref[b, at, :])
                add(("kpk", a, b), k_ref[a, at, :] * uk_ref[b, at, :])
                add(("kuu", 2 + a, 2 + b), uk_ref[a, at, :] * kuk_ref[b, at, :])


def interface_rows(own, top, bottom):
    jump_t = own[1:2] - bottom[0:1]
    slope_t = own[1:2] - own[0:1] - (bottom[1:2] - bottom[0:1])
    jump_b = top[1:2] - own[2:3]
    slope_b = top[1:2] - top[0:1] - (own[3:4] - own[2:3])
    return (
        -penalty_slope * slope_t,
        penalty_value * jump_t + penalty_slope * slope_t,
        -penalty_value * jump_b + penalty_slope * slope_b,
        -penalty_slope * slope_b,
    )


def edge_places(rows_ref, slot, prows):
    last = slot * prows + rows_ref[slot] - 1
    return (last - 1, last, slot * prows, slot * prows + 1)


def gram_kernel(
    rows_ref, matched_ref, arrived_ref, vec_ref, thick_ref, support_ref, prec_ref, k_in, uk_in, kuk_in, sums_in,
    edge_ref, below_ref, above_ref, ug_ref, uk_ref, kuk_ref, stress_ref, out_ref, sums_ref, g_ref, k_ref,
):
    slots = rows_ref.shape[0]
    rows_dev, ncol = prec_ref.shape
    prows = rows_dev // slots
    halves = ncol // LANES
    mine, match = place(rows_ref, matched_ref, slots)
    index = arrived_ref[:, 3 * ncol :].astype(jnp.float32)
    lane = iota(index.shape, 1).astype(jnp.float32)
    pick = jnp.concatenate(
        [
            jnp.where(index == lane + float(h * LANES), 1.0, 0.0).astype(jnp.bfloat16)
            for h in range(rows_dev // LANES)
        ],
        axis=1,
    )
    placed = lax.dot_general(
        pick, arrived_ref[:, : 3 * ncol], (((0,), (0,)), ((), ())), preferred_element_type=jnp.float32
    )
    for j in range(3):
        stress_ref[j] = placed[:, j * ncol : (j + 1) * ncol]
    sums_ref[...] = sums_in[...]
    rows_sent = 16 * slots

    def add(name, product):
        k = 8 * AT[name]
        sums_ref[k : k + 8, :] += folded(product)

    def add_row(name, product):
        k = 8 * AT[name]
        sums_ref[k : k + 1, :] += product

    def send(to, row):
        for h in range(halves):
            out_ref[h * rows_sent + to : h * rows_sent + to + 1, :] = row[:, h * LANES : (h + 1) * LANES]

    k_ref[...] = k_in[...]
    uk_ref[...] = uk_in[...]
    kuk_ref[...] = kuk_in[...]
    for s in range(slots):
        own_id, want_id = mine[s].astype(jnp.float32), match[s].astype(jnp.float32)
        places = edge_places(rows_ref, s, prows)
        added, scaled = [], []
        for v in range(2):
            own = edge_ref[4 * (2 * s + v) : 4 * (2 * s + v) + 4, :]
            top = jnp.zeros((2, ncol), jnp.float32)
            bottom = jnp.zeros((2, ncol), jnp.float32)
            for ref in (below_ref, above_ref):
                for t in range(slots):
                    strip = ref[4 * (2 * t + v) : 4 * (2 * t + v) + 4, :]
                    label_t = ref[8 * slots + t : 8 * slots + t + 1, :]
                    wants = ref[9 * slots + t : 9 * slots + t + 1, :]
                    top = top + jnp.where(wants == own_id, strip[0:2], 0.0)
                    bottom = bottom + jnp.where(label_t == want_id, strip[2:4], 0.0)
            added.append(interface_rows(own, top, bottom))
            scaled.append([prec_ref[pl.ds(row, 1), :] * n for row, n in zip(places, added[v])])
        last_tile = (rows_ref[s] - 1) // 8 * 8 - 8
        for base, pair in ((0, (2, 3)), (last_tile, (0, 1))):
            start = s * prows + base
            at = pl.ds(pl.multiple_of(start, 8), 16)
            row = iota((16, ncol), 0)
            live = row + base < rows_ref[s]
            parts = [
                sum(jnp.where(row == places[i] - start, scaled[v][i], 0.0) for i in pair)
                for v in range(2)
            ]
            thick, support = thick_ref[at, :], support_ref[at, :]
            extra = [stiffness(part, live, thick, support) for part in parts]
            for x in range(2):
                for y in range(x, 2):
                    k = 8 * AT["kuu", 2 + x, 2 + y]
                    sums_ref[k : k + 8, :] += folded(
                        uk_in[x, at, :] * extra[y] + parts[x] * (kuk_in[y, at, :] + extra[y])
                    )
            for v in range(2):
                kuk_ref[v, at, :] += extra[v]
        for a in range(2):
            for b in range(a, 2):
                for i, row in enumerate(places):
                    ka, kb = k_in[a, pl.ds(row, 1), :], k_in[b, pl.ds(row, 1), :]
                    add_row(("kxx", a, b), vec_ref[a, pl.ds(row, 1), :] * added[b][i])
                    add_row(("kpk", a, b), ka * scaled[b][i] + scaled[a][i] * (kb + added[b][i]))
        for v in range(2):
            for i, row in enumerate(places):
                k_ref[v, pl.ds(row, 1), :] += added[v][i]
                uk_ref[v, pl.ds(row, 1), :] += scaled[v][i]
    for s in range(slots):
        at = slice(s * prows, (s + 1) * prows)
        live = live_of(rows_ref, s, (prows, ncol))
        thick, support = thick_ref[at, :], support_ref[at, :]
        nuu, nvv, nuv = (stress_ref[j, at, :] for j in range(3))
        for v in range(2):
            w = jnp.where(live, vec_ref[v, at, :], 0.0)
            g_ref[v, at, :] = geometric(w, live, nuu, nvv, nuv)
            ug_ref[v, at, :] = prec_ref[at, :] * g_ref[v, at, :]
        for a in range(2):
            wa = jnp.where(live, vec_ref[a, at, :], 0.0)
            for b in range(a, 2):
                add(("gxx", a, b), wa * g_ref[b, at, :])
                add(("gpg", a, b), g_ref[a, at, :] * ug_ref[b, at, :])
            for b in range(2):
                add(("kpg", a, b), k_ref[a, at, :] * ug_ref[b, at, :])
                add(("kuu", a, 2 + b), ug_ref[a, at, :] * kuk_ref[b, at, :])
        basis = [(ug_ref, 0), (ug_ref, 1), (uk_ref, 0), (uk_ref, 1)]
        bends = []
        for v in range(2):
            w = ug_ref[v, at, :]
            bends.append((w, jnp.where(live, second_rows(w), 0.0), second_cols(w)))
        for b in range(2):
            w, r, c = bends[b]
            sw, tr, tc = support * w, thick * r, thick * c
            for a in range(b + 1):
                add(("kuu", a, b), bends[a][0] * sw + bends[a][1] * tr + bends[a][2] * tc)
        first = []
        for ref, v in basis:
            w = ref[v, at, :]
            first.append((row_after(w) - w, col_after(w) - w))
        for b in range(4):
            r, c = first[b]
            fr, fc = nuu * r + nuv * c, nvv * c + nuv * r
            for a in range(b + 1):
                add(("guu", a, b), first[a][0] * fr + first[a][1] * fc)
        for i, row in enumerate(edge_places(rows_ref, s, prows)):
            for a, (ref, v) in enumerate(basis):
                send(4 * (4 * s + a) + i, ref[v, pl.ds(row, 1), :])
    tag = halves * rows_sent
    tile = packed([column_sums(sums_ref[8 * k : 8 * k + 8, :]) for k in range(len(NAMES))])
    lane = iota(tile.shape, 1)
    for s in range(slots):
        tile = jnp.where(lane == LANES - slots + s, match[s].astype(jnp.float32), tile)
    out_ref[tag:, :] = tile


def apply_kernel(rows_ref, thick_ref, support_ref, stress_ref, ug_ref, uk_ref, kug_ref, gu_ref):
    slots = rows_ref.shape[0]
    rows_dev, ncol = thick_ref.shape
    prows = rows_dev // slots
    for s in range(slots):
        at = slice(s * prows, (s + 1) * prows)
        live = live_of(rows_ref, s, (prows, ncol))
        thick, support = thick_ref[at, :], support_ref[at, :]
        nuu, nvv, nuv = (stress_ref[j, at, :] for j in range(3))
        for a, (ref, v) in enumerate([(ug_ref, 0), (ug_ref, 1), (uk_ref, 0), (uk_ref, 1)]):
            w = ref[v, at, :]
            gu_ref[a, at, :] = geometric(w, live, nuu, nvv, nuv)
            if a < 2:
                kug_ref[v, at, :] = stiffness(w, live, thick, support)


def strip_of(ref, at, rows, slots):
    halves = (ref.shape[0] - 8) // (16 * slots)
    return jnp.concatenate(
        [ref[h * 16 * slots + at : h * 16 * slots + at + rows, :] for h in range(halves)], axis=1
    )


def wanted_of(ref, slot, slots):
    tag = ref.shape[0] - 8
    return ref[tag : tag + 1, LANES - slots + slot : LANES - slots + slot + 1]


def line_kernel(slots, *refs):
    line, out_ref = refs[:-1], refs[-1]
    owners = len(line)
    tag = line[0].shape[0] - 8
    me = lax.axis_index("patch")
    total = line[0][tag:, :]
    for z in range(1, owners):
        total = total + line[z][tag:, :]
    sums = {}
    for z in range(owners):
        for s in range(slots):
            wanted = wanted_of(line[z], s, slots)
            jumps, slopes = [], []
            for a in range(4):
                own = strip_of(line[z], 4 * (4 * s + a), 2, slots)
                bottom = jnp.zeros_like(own)
                for near in sorted({(z + 1) % owners, (z - 1) % owners}):
                    there = lax.rem(me - near + owners, owners)
                    for t in range(slots):
                        strip = strip_of(line[near], 4 * (4 * t + a) + 2, 2, slots)
                        is_it = wanted == (there * slots + t).astype(jnp.float32)
                        bottom = bottom + jnp.where(is_it, strip, 0.0)
                jumps.append(own[1:2] - bottom[0:1])
                slopes.append(own[1:2] - own[0:1] - (bottom[1:2] - bottom[0:1]))
            for a, b in UU:
                term = penalty_value * jumps[a] * jumps[b] + penalty_slope * slopes[a] * slopes[b]
                sums[a, b] = sums[a, b] + term if (a, b) in sums else term
    out_ref[...] = total + packed([sums[pair] for pair in UU])


def join_kernel(slots, rows_ref, matched_ref, *refs):
    line, (kug_in, kuk_in, kug_ref, kuk_ref) = refs[:-4], refs[-4:]
    kug_ref[...] = kug_in[...]
    kuk_ref[...] = kuk_in[...]
    rows_dev, ncol = kug_in.shape[1:]
    prows = rows_dev // slots
    owners = len(line)
    mine, match = place(rows_ref, matched_ref, slots)
    me = lax.axis_index("patch")
    for s in range(slots):
        own_id, want_id = mine[s].astype(jnp.float32), match[s]
        places = edge_places(rows_ref, s, prows)
        for a in range(4):
            own = strip_of(line[0], 4 * (4 * s + a), 4, slots)
            top = jnp.zeros((2, ncol), jnp.float32)
            bottom = jnp.zeros((2, ncol), jnp.float32)
            for near in sorted({1, owners - 1}):
                there = lax.rem(me - near + owners, owners)
                for t in range(slots):
                    strip = strip_of(line[near], 4 * (4 * t + a), 4, slots)
                    top = top + jnp.where(wanted_of(line[near], t, slots) == own_id, strip[0:2], 0.0)
                    bottom = bottom + jnp.where(want_id == there * slots + t, strip[2:4], 0.0)
            ref = kug_ref if a < 2 else kuk_ref
            for row, added in zip(places, interface_rows(own, top, bottom)):
                ref[a % 2, pl.ds(row, 1), :] += added


def form(table, left, right):
    total = None
    for i, c in left.items():
        row = None
        for j, d in right.items():
            term = d * table[i, j]
            row = term if row is None else row + term
        total = c * row if total is None else total + c * row
    return total


def final_kernel(
    cells, rows_ref, total_ref, vec_ref, ug_ref, uk_ref, prec_ref, kug_ref, kuk_ref, gu_ref, out_ref
):
    slots = rows_ref.shape[0]
    rows_dev, ncol = prec_ref.shape
    prows = rows_dev // slots
    total = total_ref[...]

    def value(*name):
        k = AT[name]
        return total[k % 8 : k % 8 + 1, k // 8 : k // 8 + 1]

    k_table, g_table = {}, {}

    def put(table, i, j, what):
        table[i, j] = what
        table[j, i] = what

    for a in range(2):
        for b in range(2):
            lo, hi = min(a, b), max(a, b)
            put(k_table, a, b, value("kxx", lo, hi))
            put(g_table, a, b, value("gxx", lo, hi))
            put(k_table, a, 2 + b, value("kpg", a, b))
            put(k_table, a, 4 + b, value("kpk", lo, hi))
            put(g_table, a, 2 + b, value("gpg", lo, hi))
            put(g_table, a, 4 + b, value("kpg", b, a))
    for a, b in UU:
        put(k_table, 2 + a, 2 + b, value("kuu", a, b))
        put(g_table, 2 + a, 2 + b, value("guu", a, b))

    first_a, cross_k, second_a = k_table[0, 0], k_table[0, 1], k_table[1, 1]
    first_g, cross_g, second_g = g_table[0, 0], g_table[0, 1], g_table[1, 1]
    ratio = cross_k / first_a
    other_a = second_a - ratio * cross_k
    other_q = second_g - 2.0 * ratio * cross_g + ratio * ratio * first_g
    mu_first = first_g / first_a
    mu_other = other_q / other_a
    scale_first = jnp.sqrt(norm_scale * cells / first_a)
    scale_other = jnp.sqrt(norm_scale * cells / other_a)
    new_first = {0: scale_first, 2: scale_first, 4: -scale_first * mu_first}
    new_second = {
        0: -scale_other * ratio,
        1: scale_other,
        2: -scale_other * ratio,
        3: scale_other,
        4: scale_other * mu_other * ratio,
        5: -scale_other * mu_other,
    }
    a1 = form(k_table, new_first, new_first)
    c = form(k_table, new_first, new_second)
    a2 = form(k_table, new_second, new_second)
    g1 = form(g_table, new_first, new_first)
    h = form(g_table, new_first, new_second)
    g2 = form(g_table, new_second, new_second)
    r = c / a1
    b2 = a2 - r * c
    q2 = g2 - 2.0 * r * h + r * r * g1
    mus = [g1 / a1, q2 / b2]
    scales = [jnp.sqrt(norm_scale * cells / a1), jnp.sqrt(norm_scale * cells / b2)]
    lead = [
        {i: scales[0] * f for i, f in new_first.items()},
        {i: scales[1] * (f - r * new_first[i] if i in new_first else f) for i, f in new_second.items()},
    ]
    for s in range(slots):
        at = slice(s * prows, (s + 1) * prows)
        live = live_of(rows_ref, s, (prows, ncol))
        basis = [jnp.where(live, vec_ref[v, at, :], 0.0) for v in range(2)]
        basis += [ug_ref[v, at, :] for v in range(2)] + [uk_ref[v, at, :] for v in range(2)]
        for v in range(2):
            coef = dict(lead[v])
            for i in (0, 1):
                if i in lead[v]:
                    coef[2 + i] = coef[2 + i] + lead[v][i]
                    coef[4 + i] = coef[4 + i] - mus[v] * lead[v][i]
            acc = inside = None
            for i, f in coef.items():
                term = f * basis[i]
                acc = term if acc is None else acc + term
            for i in range(2, 6):
                if i in lead[v]:
                    k_part = kug_ref[i - 2, at, :] if i < 4 else kuk_ref[i - 4, at, :]
                    term = lead[v][i] * gu_ref[i - 2, at, :] - (lead[v][i] * mus[v]) * k_part
                    inside = term if inside is None else inside + term
            out_ref[v, at, :] = acc + prec_ref[at, :] * inside


def call(body, outs, kinds, scratch=(), flops=1_000_000, out_kind="v"):
    spaces = {"s": pltpu.SMEM, "v": pltpu.VMEM, "h": pltpu.HBM}
    return pl.pallas_call(
        body,
        out_shape=[pltpu.HBM(s, d) if out_kind == "h" else jax.ShapeDtypeStruct(s, d) for s, d in outs],
        in_specs=[pl.BlockSpec(memory_space=spaces[k]) for k in kinds],
        out_specs=[pl.BlockSpec(memory_space=spaces[out_kind]) for _ in outs],
        scratch_shapes=list(scratch),
        compiler_params=pltpu.CompilerParams(vmem_limit_bytes=32 * 1024 * 1024),
        cost_estimate=pl.CostEstimate(flops=flops, bytes_accessed=2_000_000, transcendentals=0),
    )


def per_device(vectors, prestress, thickness, foundation, patch_rows, matched, elem_row):
    owners = lax.axis_size("patch")
    inner = lax.axis_size(("sub", "half"))
    slots = patch_rows.shape[0]
    rows_dev, ncol = thickness.shape
    f32, bf16 = jnp.float32, jnp.bfloat16
    cells = float(owners * inner * rows_dev * ncol)
    field = ((2, rows_dev, ncol), f32)
    one = ((rows_dev, ncol), f32)
    sums = ((8 * SUMS, ncol), f32)
    tile = ((8, LANES), f32)

    width = 3 * ncol + LANES
    (payload,) = call(
        pack_kernel,
        [((rows_dev, width), bf16)],
        "hh",
        [
            pltpu.VMEM((1, rows_dev), jnp.int32),
            pltpu.VMEM((rows_dev, width), bf16),
            pltpu.SemaphoreType.DMA((5,)),
        ],
        out_kind="h",
    )(
        pltpu.with_memory_space_constraint(jnp.transpose(prestress, (1, 0, 2)), pltpu.HBM),
        pltpu.with_memory_space_constraint(elem_row.reshape(1, rows_dev), pltpu.HBM),
    )
    arrived = lax.all_to_all(
        payload, ("patch", "sub", "half"), split_axis=0, concat_axis=0, tiled=True
    )
    edge_rows = -(-10 * slots // 8) * 8
    (edges,) = call(edge_kernel, [((edge_rows, ncol), f32)], "ssv")(patch_rows, matched, vectors)
    below = passed_along(edges, "patch", 1)
    above = passed_along(edges, "patch", -1)
    k_x, u_k, k_uk, prec, part = call(stiff_kernel, [field, field, field, one, sums], "svvv")(
        patch_rows, vectors, thickness, foundation
    )
    sent_rows = (ncol // LANES) * 16 * slots + 8
    u_g, u_k, k_uk, stress, sent = call(
        gram_kernel,
        [field, field, field, ((3, rows_dev, ncol), f32), ((sent_rows, LANES), f32)],
        "ssvvvvvvvvvvvv",
        [pltpu.VMEM(sums[0], f32), pltpu.VMEM(field[0], f32), pltpu.VMEM(field[0], f32)],
    )(
        patch_rows, matched, arrived, vectors, thickness, foundation, prec, k_x, u_k, k_uk, part,
        edges, below, above,
    )
    line = [sent] + [passed_along(sent, "patch", by) for by in range(1, owners)]
    k_ug, g_u = call(apply_kernel, [field, ((4, rows_dev, ncol), f32)], "svvvvv")(
        patch_rows, thickness, foundation, stress, u_g, u_k
    )
    (total,) = call(functools.partial(line_kernel, slots), [tile], "v" * owners)(*line)
    total = summed_over(summed_over(total, "half"), "sub")
    k_ug, k_uk = call(functools.partial(join_kernel, slots), [field, field], "ss" + "v" * (owners + 2))(
        patch_rows, matched, *line, k_ug, k_uk
    )
    (modes,) = call(functools.partial(final_kernel, cells), [field], "svvvvvvvv")(
        patch_rows, total, vectors, u_g, u_k, prec, k_ug, k_uk, g_u
    )
    return modes


def solution(mesh):
    in_specs = (
        P(None, ("groups", "patch", "sub", "half"), None),
        P(("groups", "patch", "sub", "half"), None, None),
        P(("groups", "patch", "sub", "half"), None),
        P(("groups", "patch", "sub", "half"), None),
        P(("groups", "patch", "sub", "half")),
        P(("groups", "patch", "sub", "half")),
        P(("groups", "patch", "sub", "half")),
    )
    out_specs = P(None, ("groups", "patch", "sub", "half"), None)
    return jax.shard_map(
        per_device, mesh=mesh, in_specs=in_specs, out_specs=out_specs, check_vma=False
    )
```

```python
import functools

import jax
import jax.numpy as jnp
from jax import lax
from jax.experimental import pallas as pl
from jax.experimental.pallas import tpu as pltpu
from jax.sharding import PartitionSpec as P

norm_scale = 16.0
penalty_value = 8.0
penalty_slope = 4.0
LANES = 128

UU = [(a, b) for a in range(4) for b in range(a, 4)]
NAMES = (
    [("kuu", a, b) for a, b in UU]
    + [("guu", a, b) for a, b in UU]
    + [("kxx", 0, 0), ("kxx", 0, 1), ("kxx", 1, 1)]
    + [("gxx", 0, 0), ("gxx", 0, 1), ("gxx", 1, 1)]
    + [("kpk", 0, 0), ("kpk", 0, 1), ("kpk", 1, 1)]
    + [("kpg", a, b) for a in range(2) for b in range(2)]
    + [("gpg", 0, 0), ("gpg", 0, 1), ("gpg", 1, 1)]
)
AT = {name: k for k, name in enumerate(NAMES)}
SUMS = 40
TILES = SUMS // 8


def passed_along(array, axis, by):
    peers = lax.axis_size(axis)
    return lax.ppermute(array, axis, [(i, (i + by) % peers) for i in range(peers)])


def summed_over_both(array, outer, inner):
    across, within = lax.axis_size(outer), lax.axis_size(inner)
    shifts = [(o, i) for o in range(across) for i in range(within)]
    total = array
    for o, i in shifts[1:]:
        pairs = [
            (x * within + y, (x + o) % across * within + (y + i) % within) for x, y in shifts
        ]
        total = total + lax.ppermute(array, (outer, inner), pairs)
    return total


def iota(shape, axis):
    return lax.broadcasted_iota(jnp.int32, shape, axis)


def row_after(w):
    rows = w[0].shape[0]
    zero = jnp.zeros((8, LANES), jnp.float32)
    return [pltpu.roll(jnp.concatenate([p, zero], axis=0), rows + 7, 0)[:rows] for p in w]


def row_before(w):
    rows = w[0].shape[0]
    zero = jnp.zeros((8, LANES), jnp.float32)
    return [pltpu.roll(jnp.concatenate([p, zero], axis=0), 1, 0)[:rows] for p in w]


def col_after(w):
    at_end = iota(w[0].shape, 1) == LANES - 1
    turned = [pltpu.roll(p, LANES - 1, 1) for p in w]
    return [jnp.where(at_end, n, p) for p, n in zip(turned, turned[1:] + [0.0])]


def col_before(w):
    at_start = iota(w[0].shape, 1) == 0
    turned = [pltpu.roll(p, 1, 1) for p in w]
    return [jnp.where(at_start, n, p) for p, n in zip(turned, [0.0] + turned[:-1])]


def each(f, *fields):
    return [f(*parts) for parts in zip(*fields)]


def minus(u, w):
    return each(lambda a, b: a - b, u, w)


def times(u, w):
    return each(lambda a, b: a * b, u, w)


def second_rows(w):
    return each(lambda a, b, c: a + b - (c + c), row_before(w), row_after(w), w)


def second_cols(w):
    return each(lambda a, b, c: a + b - (c + c), col_before(w), col_after(w), w)


def stiffness(w, live_thick, thick, support):
    bend_rows = times(live_thick, second_rows(w))
    bend_cols = times(thick, second_cols(w))
    return each(
        lambda f, a, r, c: f * a + (r + c), support, w, second_rows(bend_rows), second_cols(bend_cols)
    )


def fluxes(w, stress):
    along_rows = minus(row_after(w), w)
    along_cols = minus(col_after(w), w)
    nuu, nvv, nuv = stress
    rows = each(lambda n, r, m, c: n * r + m * c, nuu, along_rows, nuv, along_cols)
    cols = each(lambda n, c, m, r: n * c + m * r, nvv, along_cols, nuv, along_rows)
    return along_rows, along_cols, rows, cols


def geometric(w, stress):
    _, _, rows, cols = fluxes(w, stress)
    return each(
        lambda rb, r, cb, c: (rb - r) + (cb - c), row_before(rows), rows, col_before(cols), cols
    )


def cut(value):
    return [value[:, h * LANES : (h + 1) * LANES] for h in range(value.shape[1] // LANES)]


def joined(w):
    return jnp.concatenate(w, axis=1)


def live_of(rows_ref, slot, shape):
    return iota(shape, 0) < rows_ref[slot]


def masked(live, value):
    return [jnp.where(live, p, 0.0) for p in cut(value)]


def column_sums(product):
    return jnp.sum(product, axis=0, keepdims=True)


def folded(w):
    total = sum(w[1:], w[0])
    return jnp.sum(total.reshape(total.shape[0] // 8, 8, LANES), axis=0)


def packed(rows):
    rows = list(rows)
    rows += [jnp.zeros_like(rows[0])] * (-len(rows) % 8)
    lane = iota((8, LANES), 1)
    out = jnp.zeros((8, LANES), jnp.float32)
    for tile in range(len(rows) // 8):
        total = jnp.sum(jnp.concatenate(rows[8 * tile : 8 * tile + 8], axis=0), axis=1, keepdims=True)
        out = jnp.where(lane == tile, total, out)
    return out


def place(rows_ref, matched_ref, slots):
    inner = lax.axis_size(("sub", "half"))
    mine = [lax.axis_index("patch") * slots + s for s in range(slots)]
    match = [
        matched_ref[s] // (inner * slots) * slots + lax.rem(matched_ref[s], slots) for s in range(slots)
    ]
    return mine, match


def label(number, ncol):
    return jnp.full((1, ncol), number, jnp.int32).astype(jnp.float32)


def pack_kernel(stress_ref, elem_ref, pay_ref, elem, held, sems):
    rows_dev, ncol = stress_ref.shape[1:]
    get = pltpu.make_async_copy(elem_ref, elem, sems.at[0])
    get.start()
    planes = [
        pltpu.make_async_copy(stress_ref.at[j], held.at[:, pl.ds(j * ncol, ncol)], sems.at[1 + j])
        for j in range(3)
    ]
    for copy in planes:
        copy.start()
    get.wait()
    square = (rows_dev, rows_dev)
    if rows_dev & (rows_dev - 1) == 0:
        local = jnp.bitwise_and(elem[...], rows_dev - 1)
    else:
        local = lax.rem(elem[...], rows_dev)
    spread = jnp.broadcast_to(local.astype(jnp.float32), square)
    column = jnp.sum(
        jnp.where(iota(square, 0) == iota(square, 1), spread, 0.0), axis=1, keepdims=True
    )
    held[:, 3 * ncol :] = jnp.broadcast_to(column, (rows_dev, LANES)).astype(jnp.bfloat16)
    tail = pl.ds(3 * ncol, LANES)
    out = [pltpu.make_async_copy(held.at[:, tail], pay_ref.at[:, tail], sems.at[4])]
    out[0].start()
    for j in range(3):
        planes[j].wait()
        part = pl.ds(j * ncol, ncol)
        out.append(pltpu.make_async_copy(held.at[:, part], pay_ref.at[:, part], sems.at[5 + j]))
        out[-1].start()
    for copy in out:
        copy.wait()


def edge_kernel(rows_ref, matched_ref, vec_ref, edge_ref):
    slots = rows_ref.shape[0]
    rows_dev, ncol = vec_ref.shape[1:]
    prows = rows_dev // slots
    mine, match = place(rows_ref, matched_ref, slots)
    for s in range(slots):
        last = s * prows + rows_ref[s] - 1
        for v in range(2):
            at = 4 * (2 * s + v)
            edge_ref[at : at + 1, :] = vec_ref[v, pl.ds(last - 1, 1), :]
            edge_ref[at + 1 : at + 2, :] = vec_ref[v, pl.ds(last, 1), :]
            edge_ref[at + 2 : at + 4, :] = vec_ref[v, s * prows : s * prows + 2, :]
        at = 8 * slots
        edge_ref[at + s : at + s + 1, :] = label(mine[s], ncol)
        edge_ref[at + slots + s : at + slots + s + 1, :] = label(match[s], ncol)
    used = 10 * slots
    edge_ref[used:, :] = jnp.zeros((edge_ref.shape[0] - used, ncol), jnp.float32)


FIRST = [("kxx", 0, 0), ("kxx", 0, 1), ("kxx", 1, 1), ("kpk", 0, 0), ("kpk", 0, 1), ("kpk", 1, 1)]
FIRST += [("kuu", 2, 2), ("kuu", 2, 3), ("kuu", 3, 3)]


def stiff_kernel(rows_ref, vec_ref, thick_ref, support_ref, k_ref, uk_ref, kuk_ref, prec_ref, sums_ref):
    slots = rows_ref.shape[0]
    rows_dev, ncol = thick_ref.shape
    prows = rows_dev // slots
    totals = {}
    for s in range(slots):
        at = slice(s * prows, (s + 1) * prows)
        live = live_of(rows_ref, s, (prows, LANES))
        thick, support = cut(thick_ref[at, :]), cut(support_ref[at, :])
        live_thick = masked(live, thick_ref[at, :])
        prec = each(lambda f, t: jnp.where(live, 1.0 / (f + 12.0 * t), 0.0), support, thick)
        prec_ref[at, :] = joined(prec)
        for v in range(2):
            kw = stiffness(masked(live, vec_ref[v, at, :]), live_thick, thick, support)
            k_ref[v, at, :] = joined(kw)
            uk_ref[v, at, :] = joined(times(prec, kw))
        for v in range(2):
            kuk_ref[v, at, :] = joined(stiffness(cut(uk_ref[v, at, :]), live_thick, thick, support))
        for a in range(2):
            wa = masked(live, vec_ref[a, at, :])
            for b in range(a, 2):
                for name, product in (
                    (("kxx", a, b), times(wa, cut(k_ref[b, at, :]))),
                    (("kpk", a, b), times(cut(k_ref[a, at, :]), cut(uk_ref[b, at, :]))),
                    (("kuu", 2 + a, 2 + b), times(cut(uk_ref[a, at, :]), cut(kuk_ref[b, at, :]))),
                ):
                    part = folded(product)
                    totals[name] = totals[name] + part if s else part
    for k, name in enumerate(FIRST):
        sums_ref[8 * k : 8 * k + 8, :] = totals[name]


def interface_rows(own, top, bottom):
    jump_t = own[1:2] - bottom[0:1]
    slope_t = own[1:2] - own[0:1] - (bottom[1:2] - bottom[0:1])
    jump_b = top[1:2] - own[2:3]
    slope_b = top[1:2] - top[0:1] - (own[3:4] - own[2:3])
    return (
        -penalty_slope * slope_t,
        penalty_value * jump_t + penalty_slope * slope_t,
        -penalty_value * jump_b + penalty_slope * slope_b,
        -penalty_slope * slope_b,
    )


def edge_places(rows_ref, slot, prows):
    last = slot * prows + rows_ref[slot] - 1
    return (last - 1, last, slot * prows, slot * prows + 1)


def gram_kernel(
    rows_ref, matched_ref, arrived_ref, vec_ref, thick_ref, support_ref, prec_ref, k_in, uk_in, kuk_in, sums_in,
    edge_ref, below_ref, above_ref, ug_ref, uk_ref, kuk_ref, stress_ref, out_ref, g_ref, k_ref,
):
    slots = rows_ref.shape[0]
    rows_dev, ncol = prec_ref.shape
    prows = rows_dev // slots
    halves = ncol // LANES
    mine, match = place(rows_ref, matched_ref, slots)
    index = arrived_ref[:, 3 * ncol :].astype(jnp.float32)
    lane = iota(index.shape, 1).astype(jnp.float32)
    pick = jnp.concatenate(
        [
            jnp.where(index == lane + float(h * LANES), 1.0, 0.0).astype(jnp.bfloat16)
            for h in range(rows_dev // LANES)
        ],
        axis=1,
    )
    placed = lax.dot_general(
        pick, arrived_ref[:, : 3 * ncol], (((0,), (0,)), ((), ())), preferred_element_type=jnp.float32
    )
    for j in range(3):
        stress_ref[j] = placed[:, j * ncol : (j + 1) * ncol]
    rows_sent = 16 * slots
    totals = {name: sums_in[8 * k : 8 * k + 8, :] for k, name in enumerate(FIRST)}
    row_totals = {}

    def add(name, product):
        part = folded(product)
        totals[name] = totals[name] + part if name in totals else part

    def add_row(name, product):
        row_totals[name] = row_totals[name] + product if name in row_totals else product

    def send(to, row):
        for h in range(halves):
            out_ref[h * rows_sent + to : h * rows_sent + to + 1, :] = row[:, h * LANES : (h + 1) * LANES]

    k_ref[...] = k_in[...]
    uk_ref[...] = uk_in[...]
    kuk_ref[...] = kuk_in[...]
    late = []
    for s in range(slots):
        own_id, want_id = mine[s].astype(jnp.float32), match[s].astype(jnp.float32)
        places = edge_places(rows_ref, s, prows)
        added, scaled = [], []
        for v in range(2):
            own = edge_ref[4 * (2 * s + v) : 4 * (2 * s + v) + 4, :]
            top = jnp.zeros((2, ncol), jnp.float32)
            bottom = jnp.zeros((2, ncol), jnp.float32)
            for ref in (below_ref, above_ref):
                for t in range(slots):
                    strip = ref[4 * (2 * t + v) : 4 * (2 * t + v) + 4, :]
                    label_t = ref[8 * slots + t : 8 * slots + t + 1, :]
                    wants = ref[9 * slots + t : 9 * slots + t + 1, :]
                    top = top + jnp.where(wants == own_id, strip[0:2], 0.0)
                    bottom = bottom + jnp.where(label_t == want_id, strip[2:4], 0.0)
            added.append(interface_rows(own, top, bottom))
            scaled.append([prec_ref[pl.ds(row, 1), :] * n for row, n in zip(places, added[v])])
        last_tile = (rows_ref[s] - 1) // 8 * 8 - 8
        for base, pair in ((0, (2, 3)), (last_tile, (0, 1))):
            start = s * prows + base
            at = pl.ds(pl.multiple_of(start, 8), 16)
            row = iota((16, LANES), 0)
            live = row + base < rows_ref[s]
            parts = []
            for v in range(2):
                rows_cut = [cut(scaled[v][i]) for i in pair]
                parts.append(
                    [
                        sum(jnp.where(row == places[i] - start, rows_cut[j][h], 0.0) for j, i in enumerate(pair))
                        for h in range(halves)
                    ]
                )
            thick, support = cut(thick_ref[at, :]), cut(support_ref[at, :])
            live_thick = masked(live, thick_ref[at, :])
            extra = [stiffness(part, live_thick, thick, support) for part in parts]
            kuk = [cut(kuk_in[v, at, :]) for v in range(2)]
            for x in range(2):
                ux = cut(uk_in[x, at, :])
                for y in range(x, 2):
                    add(
                        ("kuu", 2 + x, 2 + y),
                        each(lambda u, e, p, k: u * e + p * (k + e), ux, extra[y], parts[x], kuk[y]),
                    )
            for v in range(2):
                late.append((kuk_ref, v, at, joined(each(lambda k, e: k + e, kuk[v], extra[v]))))
        for a in range(2):
            for b in range(a, 2):
                for i, row in enumerate(places):
                    ka, kb = k_in[a, pl.ds(row, 1), :], k_in[b, pl.ds(row, 1), :]
                    add_row(("kxx", a, b), vec_ref[a, pl.ds(row, 1), :] * added[b][i])
                    add_row(("kpk", a, b), ka * scaled[b][i] + scaled[a][i] * (kb + added[b][i]))
        for v in range(2):
            for i, row in enumerate(places):
                at = pl.ds(row, 1)
                late.append((k_ref, v, at, k_in[v, at, :] + added[v][i]))
                late.append((uk_ref, v, at, uk_in[v, at, :] + scaled[v][i]))
    for ref, v, at, value in late:
        ref[v, at, :] = value
    basis = [(ug_ref, 0), (ug_ref, 1), (uk_ref, 0), (uk_ref, 1)]
    for s in range(slots):
        at = slice(s * prows, (s + 1) * prows)
        live = live_of(rows_ref, s, (prows, LANES))
        stress = [cut(stress_ref[j, at, :]) for j in range(3)]
        prec = cut(prec_ref[at, :])
        gx = []
        for v in range(2):
            gx.append(geometric(masked(live, vec_ref[v, at, :]), stress))
            ug_ref[v, at, :] = joined(times(prec, gx[v]))
            g_ref[v, at, :] = joined(gx[v])
        for a in range(2):
            wa = masked(live, vec_ref[a, at, :])
            ga, ka, ua = cut(g_ref[a, at, :]), cut(k_ref[a, at, :]), cut(ug_ref[a, at, :])
            for b in range(2):
                ub = cut(ug_ref[b, at, :])
                if b >= a:
                    add(("gxx", a, b), times(wa, cut(g_ref[b, at, :])))
                    add(("gpg", a, b), times(ga, ub))
                add(("kpg", a, b), times(ka, ub))
                add(("kuu", a, 2 + b), times(ua, cut(kuk_ref[b, at, :])))
        thick, support = cut(thick_ref[at, :]), cut(support_ref[at, :])
        live_thick = masked(live, thick_ref[at, :])
        bends = []
        for v in range(2):
            w = cut(ug_ref[v, at, :])
            bends.append((w, second_rows(w), second_cols(w)))
        for b in range(2):
            w, r, c = bends[b]
            sw, tr, tc = times(support, w), times(live_thick, r), times(thick, c)
            for a in range(b + 1):
                add(
                    ("kuu", a, b),
                    each(lambda u, x, p, y, q, z: u * x + p * y + q * z, bends[a][0], sw, bends[a][1], tr, bends[a][2], tc),
                )
        first = []
        for b in range(4):
            ref, v = basis[b]
            r, c, fr, fc = fluxes(cut(ref[v, at, :]), stress)
            first.append((r, c))
            for a in range(b + 1):
                add(("guu", a, b), each(lambda p, x, q, y: p * x + q * y, first[a][0], fr, first[a][1], fc))
        for i, row in enumerate(edge_places(rows_ref, s, prows)):
            for a, (ref, v) in enumerate(basis):
                send(4 * (4 * s + a) + i, ref[v, pl.ds(row, 1), :])
    tag = halves * rows_sent
    rows = []
    for name in NAMES:
        row = column_sums(totals[name])
        if name in row_totals:
            row = row + sum(cut(row_totals[name]))
        rows.append(row)
    tile = packed(rows)
    lane = iota(tile.shape, 1)
    for s in range(slots):
        tile = jnp.where(lane == LANES - slots + s, match[s].astype(jnp.float32), tile)
    out_ref[tag:, :] = tile


def apply_kernel(
    rows_ref, vec_ref, thick_ref, support_ref, prec_ref, stress_ref, ug_ref, uk_ref, kuk_ref,
    a_ref, b_ref, c_ref, d_ref,
):
    slots = rows_ref.shape[0]
    rows_dev, ncol = thick_ref.shape
    prows = rows_dev // slots
    for s in range(slots):
        at = slice(s * prows, (s + 1) * prows)
        live = live_of(rows_ref, s, (prows, LANES))
        thick, support = cut(thick_ref[at, :]), cut(support_ref[at, :])
        live_thick = masked(live, thick_ref[at, :])
        prec = cut(prec_ref[at, :])
        stress = [cut(stress_ref[j, at, :]) for j in range(3)]
        for v in range(2):
            x, ug, uk = masked(live, vec_ref[v, at, :]), cut(ug_ref[v, at, :]), cut(uk_ref[v, at, :])
            gg, gk = geometric(ug, stress), geometric(uk, stress)
            kg = stiffness(ug, live_thick, thick, support)
            a_ref[v, at, :] = joined(each(lambda w, u, p, g: w + (u + u) + p * g, x, ug, prec, gg))
            b_ref[v, at, :] = joined(each(lambda u, p, g: u + p * g, uk, prec, gk))
            c_ref[v, at, :] = joined(each(lambda u, p, k: u + p * k, uk, prec, kg))
            d_ref[v, at, :] = joined(times(prec, cut(kuk_ref[v, at, :])))


def strip_of(ref, at, rows, slots):
    halves = (ref.shape[0] - 8) // (16 * slots)
    return jnp.concatenate(
        [ref[h * 16 * slots + at : h * 16 * slots + at + rows, :] for h in range(halves)], axis=1
    )


def wanted_of(ref, slot, slots):
    tag = ref.shape[0] - 8
    return ref[tag : tag + 1, LANES - slots + slot : LANES - slots + slot + 1]


def line_kernel(slots, *refs):
    line, out_ref = refs[:-2], refs[-1]
    owners = len(line)
    tag = line[0].shape[0] - 8
    me = lax.axis_index("patch")
    total = line[0][tag:, :]
    for z in range(1, owners):
        total = total + line[z][tag:, :]
    sums = {}
    for z in range(owners):
        for s in range(slots):
            wanted = wanted_of(line[z], s, slots)
            jumps, slopes = [], []
            for a in range(4):
                own = strip_of(line[z], 4 * (4 * s + a), 2, slots)
                bottom = jnp.zeros_like(own)
                for near in sorted({(z + 1) % owners, (z - 1) % owners}):
                    there = lax.rem(me - near + owners, owners)
                    for t in range(slots):
                        strip = strip_of(line[near], 4 * (4 * t + a) + 2, 2, slots)
                        is_it = wanted == (there * slots + t).astype(jnp.float32)
                        bottom = bottom + jnp.where(is_it, strip, 0.0)
                jumps.append(own[1:2] - bottom[0:1])
                slopes.append(own[1:2] - own[0:1] - (bottom[1:2] - bottom[0:1]))
            for a, b in UU:
                term = penalty_value * jumps[a] * jumps[b] + penalty_slope * slopes[a] * slopes[b]
                sums[a, b] = sums[a, b] + term if (a, b) in sums else term
    out_ref[...] = total + packed([sums[pair] for pair in UU])


def join_kernel(slots, rows_ref, matched_ref, prec_ref, *refs):
    line, (c_in, d_in, c_ref, d_ref) = refs[:-4], refs[-4:]
    c_ref[...] = c_in[...]
    d_ref[...] = d_in[...]
    rows_dev, ncol = c_in.shape[1:]
    prows = rows_dev // slots
    owners = len(line)
    mine, match = place(rows_ref, matched_ref, slots)
    me = lax.axis_index("patch")
    for s in range(slots):
        own_id, want_id = mine[s].astype(jnp.float32), match[s]
        places = edge_places(rows_ref, s, prows)
        for a in range(4):
            own = strip_of(line[0], 4 * (4 * s + a), 4, slots)
            top = jnp.zeros((2, ncol), jnp.float32)
            bottom = jnp.zeros((2, ncol), jnp.float32)
            for near in sorted({1, owners - 1}):
                there = lax.rem(me - near + owners, owners)
                for t in range(slots):
                    strip = strip_of(line[near], 4 * (4 * t + a), 4, slots)
                    top = top + jnp.where(wanted_of(line[near], t, slots) == own_id, strip[0:2], 0.0)
                    bottom = bottom + jnp.where(want_id == there * slots + t, strip[2:4], 0.0)
            ref = c_ref if a < 2 else d_ref
            for row, added in zip(places, interface_rows(own, top, bottom)):
                ref[a % 2, pl.ds(row, 1), :] += prec_ref[pl.ds(row, 1), :] * added


def form(table, left, right):
    total = None
    for i, c in left.items():
        row = None
        for j, d in right.items():
            term = d * table[i, j]
            row = term if row is None else row + term
        total = c * row if total is None else total + c * row
    return total


def final_kernel(cells, total_ref, a_ref, b_ref, c_ref, d_ref, out_ref, held, sems):
    rows_dev, ncol = a_ref.shape[1:]
    prows = rows_dev // 2
    total = total_ref[...]

    def value(*name):
        k = AT[name]
        return total[k % 8 : k % 8 + 1, k // 8 : k // 8 + 1]

    k_table, g_table = {}, {}

    def put(table, i, j, what):
        table[i, j] = what
        table[j, i] = what

    for a in range(2):
        for b in range(2):
            lo, hi = min(a, b), max(a, b)
            put(k_table, a, b, value("kxx", lo, hi))
            put(g_table, a, b, value("gxx", lo, hi))
            put(k_table, a, 2 + b, value("kpg", a, b))
            put(k_table, a, 4 + b, value("kpk", lo, hi))
            put(g_table, a, 2 + b, value("gpg", lo, hi))
            put(g_table, a, 4 + b, value("kpg", b, a))
    for a, b in UU:
        put(k_table, 2 + a, 2 + b, value("kuu", a, b))
        put(g_table, 2 + a, 2 + b, value("guu", a, b))

    first_a, cross_k, second_a = k_table[0, 0], k_table[0, 1], k_table[1, 1]
    first_g, cross_g, second_g = g_table[0, 0], g_table[0, 1], g_table[1, 1]
    ratio = cross_k / first_a
    other_a = second_a - ratio * cross_k
    other_q = second_g - 2.0 * ratio * cross_g + ratio * ratio * first_g
    mu_first = first_g / first_a
    mu_other = other_q / other_a
    scale_first = jnp.sqrt(norm_scale * cells / first_a)
    scale_other = jnp.sqrt(norm_scale * cells / other_a)
    new_first = {0: scale_first, 2: scale_first, 4: -scale_first * mu_first}
    new_second = {
        0: -scale_other * ratio,
        1: scale_other,
        2: -scale_other * ratio,
        3: scale_other,
        4: scale_other * mu_other * ratio,
        5: -scale_other * mu_other,
    }
    a1 = form(k_table, new_first, new_first)
    c = form(k_table, new_first, new_second)
    a2 = form(k_table, new_second, new_second)
    g1 = form(g_table, new_first, new_first)
    h = form(g_table, new_first, new_second)
    g2 = form(g_table, new_second, new_second)
    r = c / a1
    b2 = a2 - r * c
    q2 = g2 - 2.0 * r * h + r * r * g1
    mus = [g1 / a1, q2 / b2]
    scales = [jnp.sqrt(norm_scale * cells / a1), jnp.sqrt(norm_scale * cells / b2)]
    lead = [
        {i: scales[0] * f for i, f in new_first.items()},
        {i: scales[1] * (f - r * new_first[i] if i in new_first else f) for i, f in new_second.items()},
    ]
    copies = []
    for s in range(2):
        at = pl.ds(s * prows, prows)
        for v in range(2):
            acc = None
            for i in (0, 1):
                if i in lead[v]:
                    f, g = lead[v][i], lead[v][4 + i]
                    term = f * a_ref[i, at, :] + g * b_ref[i, at, :]
                    term = term - ((mus[v] * f) * c_ref[i, at, :] + (mus[v] * g) * d_ref[i, at, :])
                    acc = term if acc is None else acc + term
            held[v, at, :] = acc
            copies.append(pltpu.make_async_copy(held.at[v, at, :], out_ref.at[v, at, :], sems.at[2 * s + v]))
            copies[-1].start()
    for copy in copies:
        copy.wait()


def call(body, outs, kinds, scratch=(), flops=1_000_000, out_kind="v"):
    spaces = {"s": pltpu.SMEM, "v": pltpu.VMEM, "h": pltpu.HBM, "a": pl.ANY}
    return pl.pallas_call(
        body,
        out_shape=[pltpu.HBM(s, d) if out_kind == "h" else jax.ShapeDtypeStruct(s, d) for s, d in outs],
        in_specs=[pl.BlockSpec(memory_space=spaces[k]) for k in kinds],
        out_specs=[pl.BlockSpec(memory_space=spaces[out_kind]) for _ in outs],
        scratch_shapes=list(scratch),
        compiler_params=pltpu.CompilerParams(vmem_limit_bytes=32 * 1024 * 1024),
        cost_estimate=pl.CostEstimate(flops=flops, bytes_accessed=2_000_000, transcendentals=0),
    )


def per_device(vectors, prestress, thickness, foundation, patch_rows, matched, elem_row):
    owners = lax.axis_size("patch")
    inner = lax.axis_size(("sub", "half"))
    slots = patch_rows.shape[0]
    rows_dev, ncol = thickness.shape
    f32, bf16 = jnp.float32, jnp.bfloat16
    cells = float(owners * inner * rows_dev * ncol)
    field = ((2, rows_dev, ncol), f32)
    one = ((rows_dev, ncol), f32)
    sums = ((8 * len(FIRST), LANES), f32)
    tile = ((8, LANES), f32)

    width = 3 * ncol + LANES
    (payload,) = call(
        pack_kernel,
        [((rows_dev, width), bf16)],
        "hh",
        [
            pltpu.VMEM((1, rows_dev), jnp.int32),
            pltpu.VMEM((rows_dev, width), bf16),
            pltpu.SemaphoreType.DMA((8,)),
        ],
        out_kind="h",
    )(
        pltpu.with_memory_space_constraint(jnp.transpose(prestress, (1, 0, 2)), pltpu.HBM),
        pltpu.with_memory_space_constraint(elem_row.reshape(1, rows_dev), pltpu.HBM),
    )
    arrived = lax.all_to_all(
        payload, ("patch", "sub", "half"), split_axis=0, concat_axis=0, tiled=True
    )
    edge_rows = -(-10 * slots // 8) * 8
    (edges,) = call(edge_kernel, [((edge_rows, ncol), f32)], "ssv")(patch_rows, matched, vectors)
    below = passed_along(edges, "patch", 1)
    above = passed_along(edges, "patch", -1)
    k_x, u_k, k_uk, prec, part = call(stiff_kernel, [field, field, field, one, sums], "svvv")(
        patch_rows, vectors, thickness, foundation
    )
    sent_rows = (ncol // LANES) * 16 * slots + 8
    u_g, u_k, k_uk, stress, sent = call(
        gram_kernel,
        [field, field, field, ((3, rows_dev, ncol), f32), ((sent_rows, LANES), f32)],
        "ssvvvvvvvvvvvv",
        [pltpu.VMEM(field[0], f32), pltpu.VMEM(field[0], f32)],
    )(
        patch_rows, matched, arrived, vectors, thickness, foundation, prec, k_x, u_k, k_uk, part,
        edges, below, above,
    )
    line = [sent] + [passed_along(sent, "patch", by) for by in range(1, owners)]
    a, b, c, d = call(apply_kernel, [field] * 4, "svvvvvvvv")(
        patch_rows, vectors, thickness, foundation, prec, stress, u_g, u_k, k_uk
    )
    (total,) = call(functools.partial(line_kernel, slots), [tile], "v" * owners + "a")(*line, a)
    total = summed_over_both(total, "sub", "half")
    c, d = call(functools.partial(join_kernel, slots), [field, field], "ssv" + "v" * (owners + 2))(
        patch_rows, matched, prec, *line, c, d
    )
    (modes,) = call(
        functools.partial(final_kernel, cells),
        [field],
        "vvvvv",
        [pltpu.VMEM(field[0], f32), pltpu.SemaphoreType.DMA((4,))],
        out_kind="h",
    )(total, a, b, c, d)
    return modes


def solution(mesh):
    in_specs = (
        P(None, ("groups", "patch", "sub", "half"), None),
        P(("groups", "patch", "sub", "half"), None, None),
        P(("groups", "patch", "sub", "half"), None),
        P(("groups", "patch", "sub", "half"), None),
        P(("groups", "patch", "sub", "half")),
        P(("groups", "patch", "sub", "half")),
        P(("groups", "patch", "sub", "half")),
    )
    out_specs = P(None, ("groups", "patch", "sub", "half"), None)
    return jax.shard_map(
        per_device, mesh=mesh, in_specs=in_specs, out_specs=out_specs, check_vma=False
    )
```

```python
import functools

import jax
import jax.numpy as jnp
from jax import lax
from jax.experimental import pallas as pl
from jax.experimental.pallas import tpu as pltpu
from jax.sharding import PartitionSpec as P

norm_scale = 16.0
penalty_value = 8.0
penalty_slope = 4.0
LANES = 128

UU = [(a, b) for a in range(4) for b in range(a, 4)]
NAMES = (
    [("kuu", a, b) for a, b in UU]
    + [("guu", a, b) for a, b in UU]
    + [("kxx", 0, 0), ("kxx", 0, 1), ("kxx", 1, 1)]
    + [("gxx", 0, 0), ("gxx", 0, 1), ("gxx", 1, 1)]
    + [("kpk", 0, 0), ("kpk", 0, 1), ("kpk", 1, 1)]
    + [("kpg", a, b) for a in range(2) for b in range(2)]
    + [("gpg", 0, 0), ("gpg", 0, 1), ("gpg", 1, 1)]
)
AT = {name: k for k, name in enumerate(NAMES)}
SUMS = 40
TILES = SUMS // 8


def passed_along(array, axis, by):
    peers = lax.axis_size(axis)
    return lax.ppermute(array, axis, [(i, (i + by) % peers) for i in range(peers)])


def line_shared(array, axis):
    peers = lax.axis_size(axis)
    if peers == 4:
        shared = [lax.ppermute(array, axis, [(i, i ^ k) for i in range(4)]) for k in (1, 2, 3)]
        return [array] + shared, [(k ^ 1, k ^ 3) for k in range(4)]
    shared = [passed_along(array, axis, k) for k in range(1, peers)]
    return [array] + shared, [tuple(sorted({(k + 1) % peers, (k - 1) % peers})) for k in range(peers)]


def summed_over_both(array, outer, inner):
    across, within = lax.axis_size(outer), lax.axis_size(inner)
    shifts = [(o, i) for o in range(across) for i in range(within)]
    total = array
    for o, i in shifts[1:]:
        pairs = [
            (x * within + y, (x + o) % across * within + (y + i) % within) for x, y in shifts
        ]
        total = total + lax.ppermute(array, (outer, inner), pairs)
    return total


def iota(shape, axis):
    return lax.broadcasted_iota(jnp.int32, shape, axis)


def row_after(w):
    rows = w[0].shape[0]
    zero = jnp.zeros((8, LANES), jnp.float32)
    return [pltpu.roll(jnp.concatenate([p, zero], axis=0), rows + 7, 0)[:rows] for p in w]


def row_before(w):
    rows = w[0].shape[0]
    zero = jnp.zeros((8, LANES), jnp.float32)
    return [pltpu.roll(jnp.concatenate([p, zero], axis=0), 1, 0)[:rows] for p in w]


def col_after(w):
    at_end = iota(w[0].shape, 1) == LANES - 1
    turned = [pltpu.roll(p, LANES - 1, 1) for p in w]
    return [jnp.where(at_end, n, p) for p, n in zip(turned, turned[1:] + [0.0])]


def col_before(w):
    at_start = iota(w[0].shape, 1) == 0
    turned = [pltpu.roll(p, 1, 1) for p in w]
    return [jnp.where(at_start, n, p) for p, n in zip(turned, [0.0] + turned[:-1])]


def each(f, *fields):
    return [f(*parts) for parts in zip(*fields)]


def minus(u, w):
    return each(lambda a, b: a - b, u, w)


def times(u, w):
    return each(lambda a, b: a * b, u, w)


def second_rows(w):
    return each(lambda a, b, c: a + b - (c + c), row_before(w), row_after(w), w)


def second_cols(w):
    return each(lambda a, b, c: a + b - (c + c), col_before(w), col_after(w), w)


def stiffness(w, live_thick, thick, support):
    bend_rows = times(live_thick, second_rows(w))
    bend_cols = times(thick, second_cols(w))
    return each(
        lambda f, a, r, c: f * a + (r + c), support, w, second_rows(bend_rows), second_cols(bend_cols)
    )


def fluxes(w, stress):
    along_rows = minus(row_after(w), w)
    along_cols = minus(col_after(w), w)
    nuu, nvv, nuv = stress
    rows = each(lambda n, r, m, c: n * r + m * c, nuu, along_rows, nuv, along_cols)
    cols = each(lambda n, c, m, r: n * c + m * r, nvv, along_cols, nuv, along_rows)
    return along_rows, along_cols, rows, cols


def geometric(w, stress):
    _, _, rows, cols = fluxes(w, stress)
    return each(
        lambda rb, r, cb, c: (rb - r) + (cb - c), row_before(rows), rows, col_before(cols), cols
    )


def cut(value):
    return [value[:, h * LANES : (h + 1) * LANES] for h in range(value.shape[1] // LANES)]


def joined(w):
    return jnp.concatenate(w, axis=1)


def live_of(rows_ref, slot, shape):
    return iota(shape, 0) < rows_ref[slot]


def masked(live, value):
    return [jnp.where(live, p, 0.0) for p in cut(value)]


def column_sums(product):
    return jnp.sum(product, axis=0, keepdims=True)


def folded(w):
    total = sum(w[1:], w[0])
    return jnp.sum(total.reshape(total.shape[0] // 8, 8, LANES), axis=0)


def packed(rows):
    rows = list(rows)
    rows += [jnp.zeros_like(rows[0])] * (-len(rows) % 8)
    lane = iota((8, LANES), 1)
    out = jnp.zeros((8, LANES), jnp.float32)
    for tile in range(len(rows) // 8):
        total = jnp.sum(jnp.concatenate(rows[8 * tile : 8 * tile + 8], axis=0), axis=1, keepdims=True)
        out = jnp.where(lane == tile, total, out)
    return out


def place(rows_ref, matched_ref, slots):
    inner = lax.axis_size(("sub", "half"))
    mine = [lax.axis_index("patch") * slots + s for s in range(slots)]
    match = [
        matched_ref[s] // (inner * slots) * slots + lax.rem(matched_ref[s], slots) for s in range(slots)
    ]
    return mine, match


STACK = 8


def edge_row(rows_ref, slot, side, depth, prows):
    return slot * prows + (rows_ref[slot] - 1 - depth if side else depth)


def stacked(rows_ref, prows):
    return [(4 * s + 2 * v + side, v, s, side) for s in range(2) for v in range(2) for side in range(2)]


def labels_of(rows_ref, matched_ref):
    mine, match = place(rows_ref, matched_ref, 2)
    row = iota((STACK, LANES), 0)
    label = jnp.full((STACK, LANES), 0, jnp.int32)
    for s in range(2):
        for side, number in enumerate((mine[s], match[s])):
            label = jnp.where((row // 4 == s) & (row % 2 == side), number, label)
    return label.astype(jnp.float32)


def other_side(stack):
    row = iota(stack.shape, 0)
    return jnp.where(row % 2 == 0, pltpu.roll(stack, STACK - 1, 0), pltpu.roll(stack, 1, 0))


def other_vector(w):
    row = iota(w[0].shape, 0)
    return [jnp.where(row // 2 % 2 == 0, pltpu.roll(p, STACK - 2, 0), pltpu.roll(p, 2, 0)) for p in w]


def opposite(label, near):
    found = None
    for labels, stacks in near:
        turned, parts = other_side(labels), [[other_side(p) for p in w] for w in stacks]
        for shift in (0, 4):
            if shift:
                turned, parts = pltpu.roll(turned, 4, 0), [[pltpu.roll(p, 4, 0) for p in w] for w in parts]
            here = turned == label
            picked = [[jnp.where(here, p, 0.0) for p in w] for w in parts]
            found = picked if found is None else [each(lambda x, y: x + y, f, p) for f, p in zip(found, picked)]
    return found


def meeting(own, met):
    jump = minus(own[0], met[0])
    slope = each(lambda a, b, c, d: (a + b) - (c + d), own[0], met[0], own[1], met[1])
    return jump, slope


def interface_rows(own, met):
    jump, slope = meeting(own, met)
    return (
        each(lambda j, m: penalty_value * j + penalty_slope * m, jump, slope),
        [-penalty_slope * m for m in slope],
    )


def pack_kernel(stress_ref, elem_ref, pay_ref, elem, held, sems):
    rows_dev, ncol = stress_ref.shape[1:]
    get = pltpu.make_async_copy(elem_ref, elem, sems.at[0])
    get.start()
    planes = [
        pltpu.make_async_copy(stress_ref.at[j], held.at[:, pl.ds(j * ncol, ncol)], sems.at[1 + j])
        for j in range(3)
    ]
    for copy in planes:
        copy.start()
    get.wait()
    square = (rows_dev, rows_dev)
    if rows_dev & (rows_dev - 1) == 0:
        local = jnp.bitwise_and(elem[...], rows_dev - 1)
    else:
        local = lax.rem(elem[...], rows_dev)
    spread = jnp.broadcast_to(local.astype(jnp.float32), square)
    column = jnp.sum(
        jnp.where(iota(square, 0) == iota(square, 1), spread, 0.0), axis=1, keepdims=True
    )
    held[:, 3 * ncol :] = jnp.broadcast_to(column, (rows_dev, LANES)).astype(jnp.bfloat16)
    tail = pl.ds(3 * ncol, LANES)
    out = [pltpu.make_async_copy(held.at[:, tail], pay_ref.at[:, tail], sems.at[4])]
    out[0].start()
    for j in range(3):
        planes[j].wait()
        part = pl.ds(j * ncol, ncol)
        out.append(pltpu.make_async_copy(held.at[:, part], pay_ref.at[:, part], sems.at[5 + j]))
        out[-1].start()
    for copy in out:
        copy.wait()


def edge_kernel(rows_ref, matched_ref, vec_ref, edge_ref):
    rows_dev, ncol = vec_ref.shape[1:]
    halves = ncol // LANES
    for depth in range(2):
        for at, v, s, side in stacked(rows_ref, rows_dev // 2):
            row = vec_ref[v, pl.ds(edge_row(rows_ref, s, side, depth, rows_dev // 2), 1), :]
            for h, part in enumerate(cut(row)):
                to = STACK * (depth * halves + h) + at
                edge_ref[to : to + 1, :] = part
    edge_ref[2 * STACK * halves :, :] = labels_of(rows_ref, matched_ref)


FIRST = [("kxx", 0, 0), ("kxx", 0, 1), ("kxx", 1, 1), ("kpk", 0, 0), ("kpk", 0, 1), ("kpk", 1, 1)]
FIRST += [("kuu", 2, 2), ("kuu", 2, 3), ("kuu", 3, 3)]


RIM = [("prec", 2), ("thick", 3), ("support", 2), ("k", 2), ("uk", 2), ("kuk", 2)]
RIM_AT = {name: sum(n for _, n in RIM[:i]) for i, (name, _) in enumerate(RIM)}
RIM_STACKS = sum(n for _, n in RIM)


def stiff_kernel(rows_ref, vec_ref, thick_ref, support_ref, k_ref, uk_ref, kuk_ref, prec_ref, sums_ref, rim_ref):
    slots = rows_ref.shape[0]
    rows_dev, ncol = thick_ref.shape
    prows = rows_dev // slots
    totals = {}
    for s in range(slots):
        at = slice(s * prows, (s + 1) * prows)
        live = live_of(rows_ref, s, (prows, LANES))
        thick, support = cut(thick_ref[at, :]), cut(support_ref[at, :])
        live_thick = masked(live, thick_ref[at, :])
        prec = each(lambda f, t: jnp.where(live, 1.0 / (f + 12.0 * t), 0.0), support, thick)
        prec_ref[at, :] = joined(prec)
        for v in range(2):
            kw = stiffness(masked(live, vec_ref[v, at, :]), live_thick, thick, support)
            k_ref[v, at, :] = joined(kw)
            uk_ref[v, at, :] = joined(times(prec, kw))
        for v in range(2):
            kuk_ref[v, at, :] = joined(stiffness(cut(uk_ref[v, at, :]), live_thick, thick, support))
        for a in range(2):
            wa = masked(live, vec_ref[a, at, :])
            for b in range(a, 2):
                for name, product in (
                    (("kxx", a, b), times(wa, cut(k_ref[b, at, :]))),
                    (("kpk", a, b), times(cut(k_ref[a, at, :]), cut(uk_ref[b, at, :]))),
                    (("kuu", 2 + a, 2 + b), times(cut(uk_ref[a, at, :]), cut(kuk_ref[b, at, :]))),
                ):
                    part = folded(product)
                    totals[name] = totals[name] + part if s else part
    for k, name in enumerate(FIRST):
        sums_ref[8 * k : 8 * k + 8, :] = totals[name]
    sources = {"prec": prec_ref, "thick": thick_ref, "support": support_ref, "k": k_ref, "uk": uk_ref, "kuk": kuk_ref}
    for name, depths in RIM:
        for depth in range(depths):
            for at, v, s, side in stacked(rows_ref, prows):
                rows = pl.ds(edge_row(rows_ref, s, side, depth, prows), 1)
                to = STACK * (RIM_AT[name] + depth) + at
                ref = sources[name]
                rim_ref[to : to + 1, :] = ref[rows, :] if len(ref.shape) == 2 else ref[v, rows, :]


def rim_of(rim_ref, name, depth):
    at = STACK * (RIM_AT[name] + depth)
    return cut(rim_ref[at : at + STACK, :])


def sent_stack(ref, kind, depth, halves):
    at = (2 * kind + depth) * halves
    return [ref[STACK * (at + h) : STACK * (at + h + 1), :] for h in range(halves)]


def gram_kernel(
    rows_ref, arrived_ref, vec_ref, thick_ref, support_ref, prec_ref, k_in, uk_in, kuk_in, sums_in, rim_ref,
    edge_ref, below_ref, above_ref, ug_ref, uk_ref, kuk_ref, stress_ref, out_ref, g_ref, k_ref,
):
    slots = rows_ref.shape[0]
    rows_dev, ncol = prec_ref.shape
    prows = rows_dev // slots
    halves = ncol // LANES
    index = arrived_ref[:, 3 * ncol :].astype(jnp.float32)
    lane = iota(index.shape, 1).astype(jnp.float32)
    pick = jnp.concatenate(
        [
            jnp.where(index == lane + float(h * LANES), 1.0, 0.0).astype(jnp.bfloat16)
            for h in range(rows_dev // LANES)
        ],
        axis=1,
    )
    placed = lax.dot_general(
        pick, arrived_ref[:, : 3 * ncol], (((0,), (0,)), ((), ())), preferred_element_type=jnp.float32
    )
    for j in range(3):
        stress_ref[j] = placed[:, j * ncol : (j + 1) * ncol]
    totals = {name: sums_in[8 * k : 8 * k + 8, :] for k, name in enumerate(FIRST)}

    def add(name, product):
        part = folded(product)
        totals[name] = totals[name] + part if name in totals else part

    def add_stack(first, second, product):
        part = sum(product[1:], product[0])
        vector = iota(part.shape, 0) // 2 % 2
        totals[first] = totals[first] + jnp.where(vector == 0, part, 0.0)
        if second is not None:
            totals[second] = totals[second] + jnp.where(vector == 1, part, 0.0)

    k_ref[...] = k_in[...]
    uk_ref[...] = uk_in[...]
    kuk_ref[...] = kuk_in[...]
    label = edge_ref[2 * STACK * halves :, :]

    def depths_of(ref):
        return [[ref[STACK * (d * halves + h) : STACK * (d * halves + h + 1), :] for h in range(halves)] for d in range(2)]

    own = depths_of(edge_ref)
    met = opposite(label, [(ref[2 * STACK * halves :, :], depths_of(ref)) for ref in (below_ref, above_ref)])
    added = interface_rows(own, met)
    scaled = [times(rim_of(rim_ref, "prec", d), added[d]) for d in range(2)]
    bend = [
        each(lambda t, y, x: t * (y - (x + x)), rim_of(rim_ref, "thick", 0), scaled[1], scaled[0]),
        each(lambda t, y, x: t * (y - (x + x)), rim_of(rim_ref, "thick", 1), scaled[0], scaled[1]),
        times(rim_of(rim_ref, "thick", 2), scaled[1]),
    ]
    across = [second_cols(times(rim_of(rim_ref, "thick", d), second_cols(scaled[d]))) for d in range(2)]
    extra = [
        each(
            lambda f, z, p, q, c: f * z + (p - (q + q)) + c,
            rim_of(rim_ref, "support", 0), scaled[0], bend[1], bend[0], across[0],
        ),
        each(
            lambda f, z, p, q, r, c: f * z + (p - (q + q) + r) + c,
            rim_of(rim_ref, "support", 1), scaled[1], bend[0], bend[1], bend[2], across[1],
        ),
        each(lambda p, q: p - (q + q), bend[1], bend[2]),
        bend[2],
    ]
    for d in range(2):
        n, z, e, x = added[d], scaled[d], extra[d], own[d]
        k, kuk = rim_of(rim_ref, "k", d), rim_of(rim_ref, "kuk", d)
        add_stack(("kxx", 0, 0), ("kxx", 1, 1), times(x, n))
        add_stack(("kxx", 0, 1), None, times(x, other_vector(n)))
        z_turned = other_vector(z)
        for key, base, more in (("kpk", k, n), ("kuu", kuk, e)):
            lo = 2 if key == "kuu" else 0
            turned = other_vector(each(lambda p, q: p + q, base, more))
            add_stack((key, lo, lo), (key, lo + 1, lo + 1), each(lambda r, p, q: r * (p + p + q), z, base, more))
            add_stack((key, lo, lo + 1), None, each(lambda r, t, p, w: r * t + p * w, z, turned, base, z_turned))
    for d in range(4):
        for at, v, s, side in stacked(rows_ref, prows):
            rows = pl.ds(edge_row(rows_ref, s, side, d, prows), 1)
            kuk_ref[v, rows, :] += joined([p[at : at + 1] for p in extra[d]])
            if d < 2:
                k_ref[v, rows, :] += joined([p[at : at + 1] for p in added[d]])
                uk_ref[v, rows, :] += joined([p[at : at + 1] for p in scaled[d]])
    basis = [(ug_ref, 0), (ug_ref, 1), (uk_ref, 0), (uk_ref, 1)]
    for s in range(slots):
        at = slice(s * prows, (s + 1) * prows)
        live = live_of(rows_ref, s, (prows, LANES))
        stress = [cut(stress_ref[j, at, :]) for j in range(3)]
        prec = cut(prec_ref[at, :])
        gx = []
        for v in range(2):
            gx.append(geometric(masked(live, vec_ref[v, at, :]), stress))
            ug_ref[v, at, :] = joined(times(prec, gx[v]))
            g_ref[v, at, :] = joined(gx[v])
        for a in range(2):
            wa = masked(live, vec_ref[a, at, :])
            ga, ka, ua = cut(g_ref[a, at, :]), cut(k_ref[a, at, :]), cut(ug_ref[a, at, :])
            for b in range(2):
                ub = cut(ug_ref[b, at, :])
                if b >= a:
                    add(("gxx", a, b), times(wa, cut(g_ref[b, at, :])))
                    add(("gpg", a, b), times(ga, ub))
                add(("kpg", a, b), times(ka, ub))
                add(("kuu", a, 2 + b), times(ua, cut(kuk_ref[b, at, :])))
        thick, support = cut(thick_ref[at, :]), cut(support_ref[at, :])
        live_thick = masked(live, thick_ref[at, :])
        bends = []
        for v in range(2):
            w = cut(ug_ref[v, at, :])
            bends.append((w, second_rows(w), second_cols(w)))
        for b in range(2):
            w, r, c = bends[b]
            sw, tr, tc = times(support, w), times(live_thick, r), times(thick, c)
            for a in range(b + 1):
                add(
                    ("kuu", a, b),
                    each(lambda u, x, p, y, q, z: u * x + p * y + q * z, bends[a][0], sw, bends[a][1], tr, bends[a][2], tc),
                )
        first = []
        for b in range(4):
            ref, v = basis[b]
            r, c, fr, fc = fluxes(cut(ref[v, at, :]), stress)
            first.append((r, c))
            for a in range(b + 1):
                add(("guu", a, b), each(lambda p, x, q, y: p * x + q * y, first[a][0], fr, first[a][1], fc))
    for d in range(2):
        for at, v, s, side in stacked(rows_ref, prows):
            row = ug_ref[v, pl.ds(edge_row(rows_ref, s, side, d, prows), 1), :]
            for h, part in enumerate(cut(row)):
                to = STACK * (d * halves + h) + at
                out_ref[to : to + 1, :] = part
        for h, part in enumerate(each(lambda u, z: u + z, rim_of(rim_ref, "uk", d), scaled[d])):
            to = STACK * ((2 + d) * halves + h)
            out_ref[to : to + STACK, :] = part
    tile = packed([column_sums(totals[name]) for name in NAMES])
    out_ref[4 * STACK * halves :, :] = jnp.where(iota(tile.shape, 1) == LANES - 1, label, tile)


def apply_kernel(
    rows_ref, vec_ref, thick_ref, support_ref, prec_ref, stress_ref, ug_ref, uk_ref, kuk_ref,
    a_ref, b_ref, c_ref, d_ref,
):
    slots = rows_ref.shape[0]
    rows_dev, ncol = thick_ref.shape
    prows = rows_dev // slots
    for s in range(slots):
        at = slice(s * prows, (s + 1) * prows)
        live = live_of(rows_ref, s, (prows, LANES))
        thick, support = cut(thick_ref[at, :]), cut(support_ref[at, :])
        live_thick = masked(live, thick_ref[at, :])
        prec = cut(prec_ref[at, :])
        stress = [cut(stress_ref[j, at, :]) for j in range(3)]
        for v in range(2):
            x, ug, uk = masked(live, vec_ref[v, at, :]), cut(ug_ref[v, at, :]), cut(uk_ref[v, at, :])
            gg, gk = geometric(ug, stress), geometric(uk, stress)
            kg = stiffness(ug, live_thick, thick, support)
            a_ref[v, at, :] = joined(each(lambda w, u, p, g: w + (u + u) + p * g, x, ug, prec, gg))
            b_ref[v, at, :] = joined(each(lambda u, p, g: u + p * g, uk, prec, gk))
            c_ref[v, at, :] = joined(each(lambda u, p, k: u + p * k, uk, prec, kg))
            d_ref[v, at, :] = joined(times(prec, cut(kuk_ref[v, at, :])))


def line_parts(ref):
    halves = (ref.shape[0] // STACK - 1) // 4
    tag = 4 * STACK * halves
    return ref[tag:, LANES - 1 :], [sent_stack(ref, kind, d, halves) for kind in range(2) for d in range(2)]


def line_kernel(near, *refs):
    line, out_ref = refs[:-2], refs[-1]
    held = [line_parts(ref) for ref in line]
    sums = [None] * 6
    for (label, stacks), others in zip(held, near):
        met = opposite(label, [held[k] for k in others])
        g, k = (meeting(stacks[2 * i : 2 * i + 2], met[2 * i : 2 * i + 2]) for i in range(2))
        g_turned, k_turned = [other_vector(w) for w in g], [other_vector(w) for w in k]
        for i, (p, q) in enumerate(((g, g), (g, g_turned), (g, k), (g, k_turned), (k, k), (k, k_turned))):
            part = each(
                lambda a, b, c, d: penalty_value * (a * b) + penalty_slope * (c * d), p[0], q[0], p[1], q[1]
            )
            part = sum(part[1:], part[0])
            sums[i] = part if sums[i] is None else sums[i] + part
    total = line[0][-STACK:, :]
    for ref in line[1:]:
        total = total + ref[-STACK:, :]
    row = iota(total.shape, 0)
    masks = [(row % 2 == 1) & (row // 2 % 2 == v) for v in range(2)]
    rows = {
        (0, 0): (0, 0), (1, 1): (0, 1), (0, 1): (1, 0), (0, 2): (2, 0), (1, 3): (2, 1), (0, 3): (3, 0), (1, 2): (3, 1),
        (2, 2): (4, 0), (3, 3): (4, 1), (2, 3): (5, 0),
    }
    out_ref[...] = total + packed([column_sums(jnp.where(masks[rows[p][1]], sums[rows[p][0]], 0.0)) for p in UU])


def join_kernel(near, rows_ref, prec_ref, *refs):
    line, (c_in, d_in, c_ref, d_ref) = refs[:-4], refs[-4:]
    c_ref[...] = c_in[...]
    d_ref[...] = d_in[...]
    prows = c_in.shape[1] // 2
    label, stacks = line_parts(line[0])
    met = opposite(label, [line_parts(ref) for ref in line[1:]])
    for i, ref in enumerate((c_ref, d_ref)):
        added = interface_rows(stacks[2 * i : 2 * i + 2], met[2 * i : 2 * i + 2])
        for d in range(2):
            for at, v, s, side in stacked(rows_ref, prows):
                rows = pl.ds(edge_row(rows_ref, s, side, d, prows), 1)
                ref[v, rows, :] += prec_ref[rows, :] * joined([p[at : at + 1] for p in added[d]])


def form(table, left, right):
    total = None
    for i, c in left.items():
        row = None
        for j, d in right.items():
            term = d * table[i, j]
            row = term if row is None else row + term
        total = c * row if total is None else total + c * row
    return total


def final_kernel(cells, total_ref, a_ref, b_ref, c_ref, d_ref, out_ref, held, sems):
    rows_dev, ncol = a_ref.shape[1:]
    prows = rows_dev // 2
    total = total_ref[...]

    def value(*name):
        k = AT[name]
        return total[k % 8 : k % 8 + 1, k // 8 : k // 8 + 1]

    k_table, g_table = {}, {}

    def put(table, i, j, what):
        table[i, j] = what
        table[j, i] = what

    for a in range(2):
        for b in range(2):
            lo, hi = min(a, b), max(a, b)
            put(k_table, a, b, value("kxx", lo, hi))
            put(g_table, a, b, value("gxx", lo, hi))
            put(k_table, a, 2 + b, value("kpg", a, b))
            put(k_table, a, 4 + b, value("kpk", lo, hi))
            put(g_table, a, 2 + b, value("gpg", lo, hi))
            put(g_table, a, 4 + b, value("kpg", b, a))
    for a, b in UU:
        put(k_table, 2 + a, 2 + b, value("kuu", a, b))
        put(g_table, 2 + a, 2 + b, value("guu", a, b))

    first_a, cross_k, second_a = k_table[0, 0], k_table[0, 1], k_table[1, 1]
    first_g, cross_g, second_g = g_table[0, 0], g_table[0, 1], g_table[1, 1]
    ratio = cross_k / first_a
    other_a = second_a - ratio * cross_k
    other_q = second_g - 2.0 * ratio * cross_g + ratio * ratio * first_g
    mu_first = first_g / first_a
    mu_other = other_q / other_a
    scale_first = jnp.sqrt(norm_scale * cells / first_a)
    scale_other = jnp.sqrt(norm_scale * cells / other_a)
    new_first = {0: scale_first, 2: scale_first, 4: -scale_first * mu_first}
    new_second = {
        0: -scale_other * ratio,
        1: scale_other,
        2: -scale_other * ratio,
        3: scale_other,
        4: scale_other * mu_other * ratio,
        5: -scale_other * mu_other,
    }
    a1 = form(k_table, new_first, new_first)
    c = form(k_table, new_first, new_second)
    a2 = form(k_table, new_second, new_second)
    g1 = form(g_table, new_first, new_first)
    h = form(g_table, new_first, new_second)
    g2 = form(g_table, new_second, new_second)
    r = c / a1
    b2 = a2 - r * c
    q2 = g2 - 2.0 * r * h + r * r * g1
    mus = [g1 / a1, q2 / b2]
    scales = [jnp.sqrt(norm_scale * cells / a1), jnp.sqrt(norm_scale * cells / b2)]
    lead = [
        {i: scales[0] * f for i, f in new_first.items()},
        {i: scales[1] * (f - r * new_first[i] if i in new_first else f) for i, f in new_second.items()},
    ]
    copies = []
    for s in range(2):
        at = pl.ds(s * prows, prows)
        for v in range(2):
            acc = None
            for i in (0, 1):
                if i in lead[v]:
                    f, g = lead[v][i], lead[v][4 + i]
                    term = f * a_ref[i, at, :] + g * b_ref[i, at, :]
                    term = term - ((mus[v] * f) * c_ref[i, at, :] + (mus[v] * g) * d_ref[i, at, :])
                    acc = term if acc is None else acc + term
            held[v, at, :] = acc
            copies.append(pltpu.make_async_copy(held.at[v, at, :], out_ref.at[v, at, :], sems.at[2 * s + v]))
            copies[-1].start()
    for copy in copies:
        copy.wait()


def call(body, outs, kinds, scratch=(), flops=1_000_000, out_kind="v"):
    spaces = {"s": pltpu.SMEM, "v": pltpu.VMEM, "h": pltpu.HBM, "a": pl.ANY}
    return pl.pallas_call(
        body,
        out_shape=[pltpu.HBM(s, d) if out_kind == "h" else jax.ShapeDtypeStruct(s, d) for s, d in outs],
        in_specs=[pl.BlockSpec(memory_space=spaces[k]) for k in kinds],
        out_specs=[pl.BlockSpec(memory_space=spaces[out_kind]) for _ in outs],
        scratch_shapes=list(scratch),
        compiler_params=pltpu.CompilerParams(vmem_limit_bytes=32 * 1024 * 1024),
        cost_estimate=pl.CostEstimate(flops=flops, bytes_accessed=2_000_000, transcendentals=0),
    )


def per_device(vectors, prestress, thickness, foundation, patch_rows, matched, elem_row):
    owners = lax.axis_size("patch")
    inner = lax.axis_size(("sub", "half"))
    slots = patch_rows.shape[0]
    rows_dev, ncol = thickness.shape
    f32, bf16 = jnp.float32, jnp.bfloat16
    cells = float(owners * inner * rows_dev * ncol)
    field = ((2, rows_dev, ncol), f32)
    one = ((rows_dev, ncol), f32)
    sums = ((8 * len(FIRST), LANES), f32)
    tile = ((8, LANES), f32)

    width = 3 * ncol + LANES
    (payload,) = call(
        pack_kernel,
        [((rows_dev, width), bf16)],
        "hh",
        [
            pltpu.VMEM((1, rows_dev), jnp.int32),
            pltpu.VMEM((rows_dev, width), bf16),
            pltpu.SemaphoreType.DMA((8,)),
        ],
        out_kind="h",
    )(
        pltpu.with_memory_space_constraint(jnp.transpose(prestress, (1, 0, 2)), pltpu.HBM),
        pltpu.with_memory_space_constraint(elem_row.reshape(1, rows_dev), pltpu.HBM),
    )
    arrived = lax.all_to_all(
        payload, ("patch", "sub", "half"), split_axis=0, concat_axis=0, tiled=True
    )
    halves = ncol // LANES
    (edges,) = call(edge_kernel, [(((2 * halves + 1) * STACK, LANES), f32)], "ssv")(patch_rows, matched, vectors)
    below = passed_along(edges, "patch", 1)
    above = passed_along(edges, "patch", -1)
    k_x, u_k, k_uk, prec, part, rim = call(
        stiff_kernel, [field, field, field, one, sums, ((RIM_STACKS * STACK, ncol), f32)], "svvv"
    )(patch_rows, vectors, thickness, foundation)
    u_g, u_k, k_uk, stress, sent = call(
        gram_kernel,
        [field, field, field, ((3, rows_dev, ncol), f32), (((4 * halves + 1) * STACK, LANES), f32)],
        "svvvvvvvvvvvvv",
        [pltpu.VMEM(field[0], f32), pltpu.VMEM(field[0], f32)],
    )(
        patch_rows, arrived, vectors, thickness, foundation, prec, k_x, u_k, k_uk, part, rim,
        edges, below, above,
    )
    line, near = line_shared(sent, "patch")
    a, b, c, d = call(apply_kernel, [field] * 4, "svvvvvvvv")(
        patch_rows, vectors, thickness, foundation, prec, stress, u_g, u_k, k_uk
    )
    (total,) = call(functools.partial(line_kernel, near), [tile], "v" * owners + "a")(*line, a)
    total = summed_over_both(total, "sub", "half")
    c, d = call(functools.partial(join_kernel, near), [field, field], "sv" + "v" * (len(near[0]) + 3))(
        patch_rows, prec, line[0], *[line[k] for k in near[0]], c, d
    )
    (modes,) = call(
        functools.partial(final_kernel, cells),
        [field],
        "vvvvv",
        [pltpu.VMEM(field[0], f32), pltpu.SemaphoreType.DMA((4,))],
        out_kind="h",
    )(total, a, b, c, d)
    return modes


def solution(mesh):
    in_specs = (
        P(None, ("groups", "patch", "sub", "half"), None),
        P(("groups", "patch", "sub", "half"), None, None),
        P(("groups", "patch", "sub", "half"), None),
        P(("groups", "patch", "sub", "half"), None),
        P(("groups", "patch", "sub", "half")),
        P(("groups", "patch", "sub", "half")),
        P(("groups", "patch", "sub", "half")),
    )
    out_specs = P(None, ("groups", "patch", "sub", "half"), None)
    return jax.shard_map(
        per_device, mesh=mesh, in_specs=in_specs, out_specs=out_specs, check_vma=False
    )
```

```python
import functools

import jax
import jax.numpy as jnp
from jax import lax
from jax.experimental import pallas as pl
from jax.experimental.pallas import tpu as pltpu
from jax.sharding import PartitionSpec as P

norm_scale = 16.0
penalty_value = 8.0
penalty_slope = 4.0
LANES = 128

UU = [(a, b) for a in range(4) for b in range(a, 4)]
NAMES = (
    [("kuu", a, b) for a, b in UU]
    + [("guu", a, b) for a, b in UU]
    + [("kxx", 0, 0), ("kxx", 0, 1), ("kxx", 1, 1)]
    + [("gxx", 0, 0), ("gxx", 0, 1), ("gxx", 1, 1)]
    + [("kpk", 0, 0), ("kpk", 0, 1), ("kpk", 1, 1)]
    + [("kpg", a, b) for a in range(2) for b in range(2)]
    + [("gpg", 0, 0), ("gpg", 0, 1), ("gpg", 1, 1)]
)
AT = {name: k for k, name in enumerate(NAMES)}
SUMS = 40
TILES = SUMS // 8


def passed_along(array, axis, by):
    peers = lax.axis_size(axis)
    return lax.ppermute(array, axis, [(i, (i + by) % peers) for i in range(peers)])


def neighbours(array, axis):
    if lax.axis_size(axis) == 4:
        return [lax.ppermute(array, axis, [(i, i ^ k) for i in range(4)]) for k in (1, 3)]
    return [passed_along(array, axis, 1), passed_along(array, axis, -1)]


def line_shared(array, axis):
    peers = lax.axis_size(axis)
    if peers == 4:
        shared = [lax.ppermute(array, axis, [(i, i ^ k) for i in range(4)]) for k in (1, 2, 3)]
        return [array] + shared, [(k ^ 1, k ^ 3) for k in range(4)]
    shared = [passed_along(array, axis, k) for k in range(1, peers)]
    return [array] + shared, [tuple(sorted({(k + 1) % peers, (k - 1) % peers})) for k in range(peers)]


def summed_over_both(array, outer, inner):
    across, within = lax.axis_size(outer), lax.axis_size(inner)
    shifts = [(o, i) for o in range(across) for i in range(within)]
    total = array
    for o, i in shifts[1:]:
        pairs = [
            (x * within + y, (x + o) % across * within + (y + i) % within) for x, y in shifts
        ]
        total = total + lax.ppermute(array, (outer, inner), pairs)
    return total


def iota(shape, axis):
    return lax.broadcasted_iota(jnp.int32, shape, axis)


def row_after(w):
    rows = w[0].shape[0]
    zero = jnp.zeros((8, LANES), jnp.float32)
    return [pltpu.roll(jnp.concatenate([p, zero], axis=0), rows + 7, 0)[:rows] for p in w]


def row_before(w):
    rows = w[0].shape[0]
    zero = jnp.zeros((8, LANES), jnp.float32)
    return [pltpu.roll(jnp.concatenate([p, zero], axis=0), 1, 0)[:rows] for p in w]


def col_after(w):
    at_end = iota(w[0].shape, 1) == LANES - 1
    turned = [pltpu.roll(p, LANES - 1, 1) for p in w]
    return [jnp.where(at_end, n, p) for p, n in zip(turned, turned[1:] + [0.0])]


def col_before(w):
    at_start = iota(w[0].shape, 1) == 0
    turned = [pltpu.roll(p, 1, 1) for p in w]
    return [jnp.where(at_start, n, p) for p, n in zip(turned, [0.0] + turned[:-1])]


def each(f, *fields):
    return [f(*parts) for parts in zip(*fields)]


def minus(u, w):
    return each(lambda a, b: a - b, u, w)


def times(u, w):
    return each(lambda a, b: a * b, u, w)


def second_rows(w):
    return each(lambda a, b, c: a + b - (c + c), row_before(w), row_after(w), w)


def second_cols(w):
    return each(lambda a, b, c: a + b - (c + c), col_before(w), col_after(w), w)


def stiffness(w, live_thick, thick, support):
    bend_rows = times(live_thick, second_rows(w))
    bend_cols = times(thick, second_cols(w))
    return each(
        lambda f, a, r, c: f * a + (r + c), support, w, second_rows(bend_rows), second_cols(bend_cols)
    )


def fluxes(w, stress):
    along_rows = minus(row_after(w), w)
    along_cols = minus(col_after(w), w)
    nuu, nvv, nuv = stress
    rows = each(lambda n, r, m, c: n * r + m * c, nuu, along_rows, nuv, along_cols)
    cols = each(lambda n, c, m, r: n * c + m * r, nvv, along_cols, nuv, along_rows)
    return along_rows, along_cols, rows, cols


def geometric(w, stress):
    _, _, rows, cols = fluxes(w, stress)
    return each(
        lambda rb, r, cb, c: (rb - r) + (cb - c), row_before(rows), rows, col_before(cols), cols
    )


def cut(value):
    return [value[:, h * LANES : (h + 1) * LANES] for h in range(value.shape[1] // LANES)]


def joined(w):
    return jnp.concatenate(w, axis=1)


def live_of(rows_ref, slot, shape):
    return iota(shape, 0) < rows_ref[slot]


def masked(live, value):
    return [jnp.where(live, p, 0.0) for p in cut(value)]


def column_sums(product):
    return jnp.sum(product, axis=0, keepdims=True)


def folded(w):
    total = sum(w[1:], w[0])
    return jnp.sum(total.reshape(total.shape[0] // 8, 8, LANES), axis=0)


def packed(rows):
    rows = list(rows)
    rows += [jnp.zeros_like(rows[0])] * (-len(rows) % 8)
    lane = iota((8, LANES), 1)
    out = jnp.zeros((8, LANES), jnp.float32)
    for tile in range(len(rows) // 8):
        total = jnp.sum(jnp.concatenate(rows[8 * tile : 8 * tile + 8], axis=0), axis=1, keepdims=True)
        out = jnp.where(lane == tile, total, out)
    return out


def place(rows_ref, matched_ref, slots):
    inner = lax.axis_size(("sub", "half"))
    mine = [lax.axis_index("patch") * slots + s for s in range(slots)]
    match = [
        matched_ref[s] // (inner * slots) * slots + lax.rem(matched_ref[s], slots) for s in range(slots)
    ]
    return mine, match


STACK = 8


def edge_row(rows_ref, slot, side, depth, prows):
    return slot * prows + (rows_ref[slot] - 1 - depth if side else depth)


def stacked(rows_ref, prows):
    return [(4 * s + 2 * v + side, v, s, side) for s in range(2) for v in range(2) for side in range(2)]


def labels_of(rows_ref, matched_ref):
    mine, match = place(rows_ref, matched_ref, 2)
    row = iota((STACK, LANES), 0)
    label = jnp.full((STACK, LANES), 0, jnp.int32)
    for s in range(2):
        for side, number in enumerate((mine[s], match[s])):
            label = jnp.where((row // 4 == s) & (row % 2 == side), number, label)
    return label.astype(jnp.float32)


def other_side(stack):
    row = iota(stack.shape, 0)
    return jnp.where(row % 2 == 0, pltpu.roll(stack, STACK - 1, 0), pltpu.roll(stack, 1, 0))


def other_vector(w):
    row = iota(w[0].shape, 0)
    return [jnp.where(row // 2 % 2 == 0, pltpu.roll(p, STACK - 2, 0), pltpu.roll(p, 2, 0)) for p in w]


def opposite(label, near):
    found = None
    for labels, stacks in near:
        turned, parts = other_side(labels), [[other_side(p) for p in w] for w in stacks]
        for shift in (0, 4):
            if shift:
                turned, parts = pltpu.roll(turned, 4, 0), [[pltpu.roll(p, 4, 0) for p in w] for w in parts]
            here = turned == label
            picked = [[jnp.where(here, p, 0.0) for p in w] for w in parts]
            found = picked if found is None else [each(lambda x, y: x + y, f, p) for f, p in zip(found, picked)]
    return found


def meeting(own, met):
    jump = minus(own[0], met[0])
    slope = each(lambda a, b, c, d: (a + b) - (c + d), own[0], met[0], own[1], met[1])
    return jump, slope


def interface_rows(own, met):
    jump, slope = meeting(own, met)
    return (
        each(lambda j, m: penalty_value * j + penalty_slope * m, jump, slope),
        [-penalty_slope * m for m in slope],
    )


def local_rows(elem_ref, rows_dev):
    square = (rows_dev, rows_dev)
    if rows_dev & (rows_dev - 1) == 0:
        local = jnp.bitwise_and(elem_ref[...], rows_dev - 1)
    else:
        local = lax.rem(elem_ref[...], rows_dev)
    spread = jnp.broadcast_to(local.astype(jnp.float32), square)
    return jnp.sum(jnp.where(iota(square, 0) == iota(square, 1), spread, 0.0), axis=1, keepdims=True)


def pack_rows_kernel(stress_ref, elem_ref, pay_ref, elem, held, sems):
    rows_dev, ncol = stress_ref.shape[1:]
    get = pltpu.make_async_copy(elem_ref, elem, sems.at[0])
    get.start()
    planes = [
        pltpu.make_async_copy(stress_ref.at[j], held.at[:, pl.ds(j * ncol, ncol)], sems.at[1 + j])
        for j in range(3)
    ]
    for copy in planes:
        copy.start()
    get.wait()
    column = local_rows(elem, rows_dev)
    held[:, 3 * ncol :] = jnp.broadcast_to(column, (rows_dev, LANES)).astype(jnp.bfloat16)
    for copy in planes:
        copy.wait()
    put = pltpu.make_async_copy(held, pay_ref, sems.at[4])
    put.start()
    put.wait()


def pack_blocks_kernel(stress_ref, elem_ref, pay_ref, elem, held, get_sem, in_sems, out_sems):
    blocks, ncol = held.shape[0], stress_ref.shape[3]
    halves = ncol // LANES
    get = pltpu.make_async_copy(elem_ref, elem, get_sem)
    get.start()
    fetch, put = [], []
    for t in range(3 * halves):
        to = held.at[:, pl.ds(16 * t, 16), :]
        source = stress_ref.at[t // halves, :, :, pl.ds(t % halves * LANES, LANES)]
        fetch.append(pltpu.make_async_copy(source, to, in_sems.at[t]))
        put.append(pltpu.make_async_copy(to, pay_ref.at[:, pl.ds(16 * t, 16), :], out_sems.at[t]))
        fetch[-1].start()
    get.wait()
    column = jnp.broadcast_to(local_rows(elem, 16 * blocks), (16 * blocks, LANES))
    lane = iota((8, LANES), 1)
    for k in range(blocks):
        both = jnp.where(lane < LANES // 2, column[16 * k : 16 * k + 8], column[16 * k + 8 : 16 * k + 16])
        held[k, 48 * halves :, :] = both.astype(jnp.bfloat16)
    tail = pl.ds(48 * halves, 8)
    put.append(pltpu.make_async_copy(held.at[:, tail, :], pay_ref.at[:, tail, :], out_sems.at[3 * halves]))
    put[-1].start()
    for t in range(3 * halves):
        fetch[t].wait()
        put[t].start()
    for copy in put:
        copy.wait()


def unpacked(arrived_ref, ncol):
    if len(arrived_ref.shape) == 2:
        return arrived_ref[:, : 3 * ncol], arrived_ref[:, 3 * ncol :].astype(jnp.float32)
    blocks, halves = arrived_ref.shape[0], ncol // LANES
    forces = jnp.concatenate(
        [
            jnp.concatenate([arrived_ref[k, 16 * t : 16 * t + 16, :] for k in range(blocks)], axis=0)
            for t in range(3 * halves)
        ],
        axis=1,
    )
    tiles = [arrived_ref[k, 48 * halves :, :].astype(jnp.float32) for k in range(blocks)]
    half = LANES // 2
    column = jnp.concatenate([t[:, at : at + 1] for t in tiles for at in (0, half)], axis=0)
    return forces, jnp.broadcast_to(column, (16 * blocks, LANES))


def edge_kernel(rows_ref, matched_ref, vec_ref, edge_ref):
    rows_dev, ncol = vec_ref.shape[1:]
    halves = ncol // LANES
    for depth in range(2):
        for at, v, s, side in stacked(rows_ref, rows_dev // 2):
            row = vec_ref[v, pl.ds(edge_row(rows_ref, s, side, depth, rows_dev // 2), 1), :]
            for h, part in enumerate(cut(row)):
                to = STACK * (depth * halves + h) + at
                edge_ref[to : to + 1, :] = part
    edge_ref[2 * STACK * halves :, :] = labels_of(rows_ref, matched_ref)


FIRST = [("kxx", 0, 0), ("kxx", 0, 1), ("kxx", 1, 1), ("kpk", 0, 0), ("kpk", 0, 1), ("kpk", 1, 1)]
FIRST += [("kuu", 2, 2), ("kuu", 2, 3), ("kuu", 3, 3)]


RIM = [("prec", 2), ("thick", 3), ("support", 2), ("k", 2), ("uk", 2), ("kuk", 2)]
RIM_AT = {name: sum(n for _, n in RIM[:i]) for i, (name, _) in enumerate(RIM)}
RIM_STACKS = sum(n for _, n in RIM)


def stiff_kernel(rows_ref, vec_ref, thick_ref, support_ref, k_ref, uk_ref, kuk_ref, prec_ref, sums_ref, rim_ref):
    slots = rows_ref.shape[0]
    rows_dev, ncol = thick_ref.shape
    prows = rows_dev // slots
    totals = {}
    for s in range(slots):
        at = slice(s * prows, (s + 1) * prows)
        live = live_of(rows_ref, s, (prows, LANES))
        thick, support = cut(thick_ref[at, :]), cut(support_ref[at, :])
        live_thick = masked(live, thick_ref[at, :])
        prec = each(lambda f, t: jnp.where(live, 1.0 / (f + 12.0 * t), 0.0), support, thick)
        prec_ref[at, :] = joined(prec)
        for v in range(2):
            kw = stiffness(masked(live, vec_ref[v, at, :]), live_thick, thick, support)
            k_ref[v, at, :] = joined(kw)
            uk_ref[v, at, :] = joined(times(prec, kw))
        for v in range(2):
            kuk_ref[v, at, :] = joined(stiffness(cut(uk_ref[v, at, :]), live_thick, thick, support))
        for a in range(2):
            wa = masked(live, vec_ref[a, at, :])
            for b in range(a, 2):
                for name, product in (
                    (("kxx", a, b), times(wa, cut(k_ref[b, at, :]))),
                    (("kpk", a, b), times(cut(k_ref[a, at, :]), cut(uk_ref[b, at, :]))),
                    (("kuu", 2 + a, 2 + b), times(cut(uk_ref[a, at, :]), cut(kuk_ref[b, at, :]))),
                ):
                    part = folded(product)
                    totals[name] = totals[name] + part if s else part
    for k, name in enumerate(FIRST):
        sums_ref[8 * k : 8 * k + 8, :] = totals[name]
    sources = {"prec": prec_ref, "thick": thick_ref, "support": support_ref, "k": k_ref, "uk": uk_ref, "kuk": kuk_ref}
    for name, depths in RIM:
        for depth in range(depths):
            for at, v, s, side in stacked(rows_ref, prows):
                rows = pl.ds(edge_row(rows_ref, s, side, depth, prows), 1)
                to = STACK * (RIM_AT[name] + depth) + at
                ref = sources[name]
                rim_ref[to : to + 1, :] = ref[rows, :] if len(ref.shape) == 2 else ref[v, rows, :]


def rim_of(rim_ref, name, depth):
    at = STACK * (RIM_AT[name] + depth)
    return cut(rim_ref[at : at + STACK, :])


def sent_stack(ref, kind, depth, halves):
    at = (2 * kind + depth) * halves
    return [ref[STACK * (at + h) : STACK * (at + h + 1), :] for h in range(halves)]


def gram_kernel(
    rows_ref, arrived_ref, vec_ref, thick_ref, support_ref, prec_ref, k_in, uk_in, kuk_in, sums_in, rim_ref,
    edge_ref, below_ref, above_ref, ug_ref, uk_ref, kuk_ref, stress_ref, out_ref, g_ref, k_ref,
):
    slots = rows_ref.shape[0]
    rows_dev, ncol = prec_ref.shape
    prows = rows_dev // slots
    halves = ncol // LANES
    forces, index = unpacked(arrived_ref, ncol)
    lane = iota(index.shape, 1).astype(jnp.float32)
    pick = jnp.concatenate(
        [
            jnp.where(index == lane + float(h * LANES), 1.0, 0.0).astype(jnp.bfloat16)
            for h in range(rows_dev // LANES)
        ],
        axis=1,
    )
    placed = lax.dot_general(
        pick, forces, (((0,), (0,)), ((), ())), preferred_element_type=jnp.float32
    )
    for j in range(3):
        stress_ref[j] = placed[:, j * ncol : (j + 1) * ncol]
    totals = {name: sums_in[8 * k : 8 * k + 8, :] for k, name in enumerate(FIRST)}

    def add(name, product):
        part = folded(product)
        totals[name] = totals[name] + part if name in totals else part

    def add_stack(first, second, product):
        part = sum(product[1:], product[0])
        vector = iota(part.shape, 0) // 2 % 2
        totals[first] = totals[first] + jnp.where(vector == 0, part, 0.0)
        if second is not None:
            totals[second] = totals[second] + jnp.where(vector == 1, part, 0.0)

    k_ref[...] = k_in[...]
    uk_ref[...] = uk_in[...]
    kuk_ref[...] = kuk_in[...]
    label = edge_ref[2 * STACK * halves :, :]

    def depths_of(ref):
        return [[ref[STACK * (d * halves + h) : STACK * (d * halves + h + 1), :] for h in range(halves)] for d in range(2)]

    own = depths_of(edge_ref)
    met = opposite(label, [(ref[2 * STACK * halves :, :], depths_of(ref)) for ref in (below_ref, above_ref)])
    added = interface_rows(own, met)
    scaled = [times(rim_of(rim_ref, "prec", d), added[d]) for d in range(2)]
    bend = [
        each(lambda t, y, x: t * (y - (x + x)), rim_of(rim_ref, "thick", 0), scaled[1], scaled[0]),
        each(lambda t, y, x: t * (y - (x + x)), rim_of(rim_ref, "thick", 1), scaled[0], scaled[1]),
        times(rim_of(rim_ref, "thick", 2), scaled[1]),
    ]
    across = [second_cols(times(rim_of(rim_ref, "thick", d), second_cols(scaled[d]))) for d in range(2)]
    extra = [
        each(
            lambda f, z, p, q, c: f * z + (p - (q + q)) + c,
            rim_of(rim_ref, "support", 0), scaled[0], bend[1], bend[0], across[0],
        ),
        each(
            lambda f, z, p, q, r, c: f * z + (p - (q + q) + r) + c,
            rim_of(rim_ref, "support", 1), scaled[1], bend[0], bend[1], bend[2], across[1],
        ),
        each(lambda p, q: p - (q + q), bend[1], bend[2]),
        bend[2],
    ]
    for d in range(2):
        n, z, e, x = added[d], scaled[d], extra[d], own[d]
        k, kuk = rim_of(rim_ref, "k", d), rim_of(rim_ref, "kuk", d)
        add_stack(("kxx", 0, 0), ("kxx", 1, 1), times(x, n))
        add_stack(("kxx", 0, 1), None, times(x, other_vector(n)))
        z_turned = other_vector(z)
        for key, base, more in (("kpk", k, n), ("kuu", kuk, e)):
            lo = 2 if key == "kuu" else 0
            turned = other_vector(each(lambda p, q: p + q, base, more))
            add_stack((key, lo, lo), (key, lo + 1, lo + 1), each(lambda r, p, q: r * (p + p + q), z, base, more))
            add_stack((key, lo, lo + 1), None, each(lambda r, t, p, w: r * t + p * w, z, turned, base, z_turned))
    for d in range(4):
        for at, v, s, side in stacked(rows_ref, prows):
            rows = pl.ds(edge_row(rows_ref, s, side, d, prows), 1)
            kuk_ref[v, rows, :] += joined([p[at : at + 1] for p in extra[d]])
            if d < 2:
                k_ref[v, rows, :] += joined([p[at : at + 1] for p in added[d]])
                uk_ref[v, rows, :] += joined([p[at : at + 1] for p in scaled[d]])
    basis = [(ug_ref, 0), (ug_ref, 1), (uk_ref, 0), (uk_ref, 1)]
    for s in range(slots):
        at = slice(s * prows, (s + 1) * prows)
        live = live_of(rows_ref, s, (prows, LANES))
        stress = [cut(stress_ref[j, at, :]) for j in range(3)]
        prec = cut(prec_ref[at, :])
        gx = []
        for v in range(2):
            gx.append(geometric(masked(live, vec_ref[v, at, :]), stress))
            ug_ref[v, at, :] = joined(times(prec, gx[v]))
            g_ref[v, at, :] = joined(gx[v])
        for a in range(2):
            wa = masked(live, vec_ref[a, at, :])
            ga, ka, ua = cut(g_ref[a, at, :]), cut(k_ref[a, at, :]), cut(ug_ref[a, at, :])
            for b in range(2):
                ub = cut(ug_ref[b, at, :])
                if b >= a:
                    add(("gxx", a, b), times(wa, cut(g_ref[b, at, :])))
                    add(("gpg", a, b), times(ga, ub))
                add(("kpg", a, b), times(ka, ub))
                add(("kuu", a, 2 + b), times(ua, cut(kuk_ref[b, at, :])))
        thick, support = cut(thick_ref[at, :]), cut(support_ref[at, :])
        live_thick = masked(live, thick_ref[at, :])
        bends = []
        for v in range(2):
            w = cut(ug_ref[v, at, :])
            bends.append((w, second_rows(w), second_cols(w)))
        for b in range(2):
            w, r, c = bends[b]
            sw, tr, tc = times(support, w), times(live_thick, r), times(thick, c)
            for a in range(b + 1):
                add(
                    ("kuu", a, b),
                    each(lambda u, x, p, y, q, z: u * x + p * y + q * z, bends[a][0], sw, bends[a][1], tr, bends[a][2], tc),
                )
        first = []
        for b in range(4):
            ref, v = basis[b]
            r, c, fr, fc = fluxes(cut(ref[v, at, :]), stress)
            first.append((r, c))
            for a in range(b + 1):
                add(("guu", a, b), each(lambda p, x, q, y: p * x + q * y, first[a][0], fr, first[a][1], fc))
    for d in range(2):
        for at, v, s, side in stacked(rows_ref, prows):
            row = ug_ref[v, pl.ds(edge_row(rows_ref, s, side, d, prows), 1), :]
            for h, part in enumerate(cut(row)):
                to = STACK * (d * halves + h) + at
                out_ref[to : to + 1, :] = part
        for h, part in enumerate(each(lambda u, z: u + z, rim_of(rim_ref, "uk", d), scaled[d])):
            to = STACK * ((2 + d) * halves + h)
            out_ref[to : to + STACK, :] = part
    tile = packed([column_sums(totals[name]) for name in NAMES])
    out_ref[4 * STACK * halves :, :] = jnp.where(iota(tile.shape, 1) == LANES - 1, label, tile)


def apply_kernel(
    rows_ref, vec_ref, thick_ref, support_ref, prec_ref, stress_ref, ug_ref, uk_ref, kuk_ref, a_ref, c_ref, d_ref,
):
    slots = rows_ref.shape[0]
    rows_dev, ncol = thick_ref.shape
    prows = rows_dev // slots
    for s in range(slots):
        at = slice(s * prows, (s + 1) * prows)
        live = live_of(rows_ref, s, (prows, LANES))
        thick, support = cut(thick_ref[at, :]), cut(support_ref[at, :])
        live_thick = masked(live, thick_ref[at, :])
        prec = cut(prec_ref[at, :])
        stress = [cut(stress_ref[j, at, :]) for j in range(3)]
        for v in range(2):
            x, ug, uk = masked(live, vec_ref[v, at, :]), cut(ug_ref[v, at, :]), cut(uk_ref[v, at, :])
            gg = geometric(ug, stress)
            kg = stiffness(ug, live_thick, thick, support)
            a_ref[v, at, :] = joined(each(lambda w, u, p, g: w + (u + u) + p * g, x, ug, prec, gg))
            c_ref[v, at, :] = joined(each(lambda u, p, k: u + p * k, uk, prec, kg))
            d_ref[v, at, :] = joined(times(prec, cut(kuk_ref[v, at, :])))


def line_parts(ref):
    halves = (ref.shape[0] // STACK - 1) // 4
    tag = 4 * STACK * halves
    return ref[tag:, LANES - 1 :], [sent_stack(ref, kind, d, halves) for kind in range(2) for d in range(2)]


def line_kernel(near, *refs):
    line, out_ref = refs[:-2], refs[-1]
    held = [line_parts(ref) for ref in line]
    sums = [None] * 6
    for (label, stacks), others in zip(held, near):
        met = opposite(label, [held[k] for k in others])
        g, k = (meeting(stacks[2 * i : 2 * i + 2], met[2 * i : 2 * i + 2]) for i in range(2))
        g_turned, k_turned = [other_vector(w) for w in g], [other_vector(w) for w in k]
        for i, (p, q) in enumerate(((g, g), (g, g_turned), (g, k), (g, k_turned), (k, k), (k, k_turned))):
            part = each(
                lambda a, b, c, d: penalty_value * (a * b) + penalty_slope * (c * d), p[0], q[0], p[1], q[1]
            )
            part = sum(part[1:], part[0])
            sums[i] = part if sums[i] is None else sums[i] + part
    total = line[0][-STACK:, :]
    for ref in line[1:]:
        total = total + ref[-STACK:, :]
    row = iota(total.shape, 0)
    masks = [(row % 2 == 1) & (row // 2 % 2 == v) for v in range(2)]
    rows = {
        (0, 0): (0, 0), (1, 1): (0, 1), (0, 1): (1, 0), (0, 2): (2, 0), (1, 3): (2, 1), (0, 3): (3, 0), (1, 2): (3, 1),
        (2, 2): (4, 0), (3, 3): (4, 1), (2, 3): (5, 0),
    }
    out_ref[...] = total + packed([column_sums(jnp.where(masks[rows[p][1]], sums[rows[p][0]], 0.0)) for p in UU])


def join_kernel(near, rows_ref, prec_ref, stress_ref, uk_ref, c_in, d_in, *refs):
    line, (b_ref, c_ref, d_ref) = refs[:-3], refs[-3:]
    c_ref[...] = c_in[...]
    d_ref[...] = d_in[...]
    prows = c_in.shape[1] // 2
    for s in range(2):
        at = slice(s * prows, (s + 1) * prows)
        prec = cut(prec_ref[at, :])
        stress = [cut(stress_ref[j, at, :]) for j in range(3)]
        for v in range(2):
            uk = cut(uk_ref[v, at, :])
            gk = geometric(uk, stress)
            b_ref[v, at, :] = joined(each(lambda u, p, g: u + p * g, uk, prec, gk))
    label, stacks = line_parts(line[0])
    met = opposite(label, [line_parts(ref) for ref in line[1:]])
    for i, ref in enumerate((c_ref, d_ref)):
        added = interface_rows(stacks[2 * i : 2 * i + 2], met[2 * i : 2 * i + 2])
        for d in range(2):
            for at, v, s, side in stacked(rows_ref, prows):
                rows = pl.ds(edge_row(rows_ref, s, side, d, prows), 1)
                ref[v, rows, :] += prec_ref[rows, :] * joined([p[at : at + 1] for p in added[d]])


def form(table, left, right):
    total = None
    for i, c in left.items():
        row = None
        for j, d in right.items():
            term = d * table[i, j]
            row = term if row is None else row + term
        total = c * row if total is None else total + c * row
    return total


def final_kernel(cells, total_ref, a_ref, b_ref, c_ref, d_ref, out_ref, held, sems):
    rows_dev, ncol = a_ref.shape[1:]
    prows = rows_dev // 2
    total = total_ref[...]

    def value(*name):
        k = AT[name]
        return jnp.broadcast_to(total[k % 8 : k % 8 + 1, k // 8 : k // 8 + 1], (8, LANES))

    k_table, g_table = {}, {}

    def put(table, i, j, what):
        table[i, j] = what
        table[j, i] = what

    for a in range(2):
        for b in range(2):
            lo, hi = min(a, b), max(a, b)
            put(k_table, a, b, value("kxx", lo, hi))
            put(g_table, a, b, value("gxx", lo, hi))
            put(k_table, a, 2 + b, value("kpg", a, b))
            put(k_table, a, 4 + b, value("kpk", lo, hi))
            put(g_table, a, 2 + b, value("gpg", lo, hi))
            put(g_table, a, 4 + b, value("kpg", b, a))
    for a, b in UU:
        put(k_table, 2 + a, 2 + b, value("kuu", a, b))
        put(g_table, 2 + a, 2 + b, value("guu", a, b))

    first_a, cross_k, second_a = k_table[0, 0], k_table[0, 1], k_table[1, 1]
    first_g, cross_g, second_g = g_table[0, 0], g_table[0, 1], g_table[1, 1]
    ratio = cross_k / first_a
    other_a = second_a - ratio * cross_k
    other_q = second_g - 2.0 * ratio * cross_g + ratio * ratio * first_g
    mu_first = first_g / first_a
    mu_other = other_q / other_a
    scale_first = jnp.sqrt(norm_scale * cells / first_a)
    scale_other = jnp.sqrt(norm_scale * cells / other_a)
    new_first = {0: scale_first, 2: scale_first, 4: -scale_first * mu_first}
    new_second = {
        0: -scale_other * ratio,
        1: scale_other,
        2: -scale_other * ratio,
        3: scale_other,
        4: scale_other * mu_other * ratio,
        5: -scale_other * mu_other,
    }
    a1 = form(k_table, new_first, new_first)
    c = form(k_table, new_first, new_second)
    a2 = form(k_table, new_second, new_second)
    g1 = form(g_table, new_first, new_first)
    h = form(g_table, new_first, new_second)
    g2 = form(g_table, new_second, new_second)
    r = c / a1
    b2 = a2 - r * c
    q2 = g2 - 2.0 * r * h + r * r * g1
    mus = [g1 / a1, q2 / b2]
    scales = [jnp.sqrt(norm_scale * cells / a1), jnp.sqrt(norm_scale * cells / b2)]
    lead = [
        {i: scales[0] * f for i, f in new_first.items()},
        {i: scales[1] * (f - r * new_first[i] if i in new_first else f) for i, f in new_second.items()},
    ]
    copies = []
    tall = (prows // 8, 8, LANES)
    for s in range(2):
        at = pl.ds(s * prows, prows)
        for v in range(2):
            for h in range(ncol // LANES):
                cols = pl.ds(h * LANES, LANES)
                acc = None
                for i in (0, 1):
                    if i in lead[v]:
                        f, g = lead[v][i], lead[v][4 + i]
                        parts = [ref[i, at, cols].reshape(tall) for ref in (a_ref, b_ref, c_ref, d_ref)]
                        term = f * parts[0] + g * parts[1]
                        term = term - ((mus[v] * f) * parts[2] + (mus[v] * g) * parts[3])
                        acc = term if acc is None else acc + term
                held[v, at, cols] = acc.reshape(prows, LANES)
            copies.append(pltpu.make_async_copy(held.at[v, at, :], out_ref.at[v, at, :], sems.at[2 * s + v]))
            copies[-1].start()
    for copy in copies:
        copy.wait()


def call(body, outs, kinds, scratch=(), flops=1_000_000, out_kind="v"):
    spaces = {"s": pltpu.SMEM, "v": pltpu.VMEM, "h": pltpu.HBM, "a": pl.ANY}
    return pl.pallas_call(
        body,
        out_shape=[pltpu.HBM(s, d) if out_kind == "h" else jax.ShapeDtypeStruct(s, d) for s, d in outs],
        in_specs=[pl.BlockSpec(memory_space=spaces[k]) for k in kinds],
        out_specs=[pl.BlockSpec(memory_space=spaces[out_kind]) for _ in outs],
        scratch_shapes=list(scratch),
        compiler_params=pltpu.CompilerParams(vmem_limit_bytes=32 * 1024 * 1024),
        cost_estimate=pl.CostEstimate(flops=flops, bytes_accessed=2_000_000, transcendentals=0),
    )


def per_device(vectors, prestress, thickness, foundation, patch_rows, matched, elem_row):
    owners = lax.axis_size("patch")
    inner = lax.axis_size(("sub", "half"))
    slots = patch_rows.shape[0]
    rows_dev, ncol = thickness.shape
    f32, bf16 = jnp.float32, jnp.bfloat16
    cells = float(owners * inner * rows_dev * ncol)
    field = ((2, rows_dev, ncol), f32)
    one = ((rows_dev, ncol), f32)
    sums = ((8 * len(FIRST), LANES), f32)
    tile = ((8, LANES), f32)

    width = 3 * ncol + LANES
    elem = pltpu.VMEM((1, rows_dev), jnp.int32)
    planes = jnp.transpose(prestress, (1, 0, 2))
    if rows_dev == 16 * owners * inner:
        tiles = 3 * (ncol // LANES)
        shape = (owners * inner, 16 * tiles + 8, LANES)
        planes = planes.reshape(3, owners * inner, 16, ncol)
        sems = [pltpu.SemaphoreType.DMA, pltpu.SemaphoreType.DMA((tiles,)), pltpu.SemaphoreType.DMA((tiles + 1,))]
        pack = pack_blocks_kernel
    else:
        shape = (rows_dev, width)
        sems = [pltpu.SemaphoreType.DMA((5,))]
        pack = pack_rows_kernel
    (payload,) = call(pack, [(shape, bf16)], "hh", [elem, pltpu.VMEM(shape, bf16), *sems], out_kind="h")(
        pltpu.with_memory_space_constraint(planes, pltpu.HBM),
        pltpu.with_memory_space_constraint(elem_row.reshape(1, rows_dev), pltpu.HBM),
    )
    arrived = lax.all_to_all(
        payload, ("patch", "sub", "half"), split_axis=0, concat_axis=0, tiled=True
    )
    halves = ncol // LANES
    (edges,) = call(edge_kernel, [(((2 * halves + 1) * STACK, LANES), f32)], "ssv")(patch_rows, matched, vectors)
    below, above = neighbours(edges, "patch")
    k_x, u_k, k_uk, prec, part, rim = call(
        stiff_kernel, [field, field, field, one, sums, ((RIM_STACKS * STACK, ncol), f32)], "svvv"
    )(patch_rows, vectors, thickness, foundation)
    u_g, u_k, k_uk, stress, sent = call(
        gram_kernel,
        [field, field, field, ((3, rows_dev, ncol), f32), (((4 * halves + 1) * STACK, LANES), f32)],
        "svvvvvvvvvvvvv",
        [pltpu.VMEM(field[0], f32), pltpu.VMEM(field[0], f32)],
    )(
        patch_rows, arrived, vectors, thickness, foundation, prec, k_x, u_k, k_uk, part, rim,
        edges, below, above,
    )
    line, near = line_shared(sent, "patch")
    a, c, d = call(apply_kernel, [field] * 3, "svvvvvvvv")(
        patch_rows, vectors, thickness, foundation, prec, stress, u_g, u_k, k_uk
    )
    (total,) = call(functools.partial(line_kernel, near), [tile], "v" * owners + "a")(*line, a)
    total = summed_over_both(total, "sub", "half")
    b, c, d = call(functools.partial(join_kernel, near), [field] * 3, "sv" + "v" * (len(near[0]) + 5))(
        patch_rows, prec, stress, u_k, c, d, line[0], *[line[k] for k in near[0]]
    )
    (modes,) = call(
        functools.partial(final_kernel, cells),
        [field],
        "vvvvv",
        [pltpu.VMEM(field[0], f32), pltpu.SemaphoreType.DMA((4,))],
        out_kind="h",
    )(total, a, b, c, d)
    return modes


def solution(mesh):
    in_specs = (
        P(None, ("groups", "patch", "sub", "half"), None),
        P(("groups", "patch", "sub", "half"), None, None),
        P(("groups", "patch", "sub", "half"), None),
        P(("groups", "patch", "sub", "half"), None),
        P(("groups", "patch", "sub", "half")),
        P(("groups", "patch", "sub", "half")),
        P(("groups", "patch", "sub", "half")),
    )
    out_specs = P(None, ("groups", "patch", "sub", "half"), None)
    return jax.shard_map(
        per_device, mesh=mesh, in_specs=in_specs, out_specs=out_specs, check_vma=False
    )
```

```python
import functools

import jax
import jax.numpy as jnp
from jax import lax
from jax.experimental import pallas as pl
from jax.experimental.pallas import tpu as pltpu
from jax.sharding import PartitionSpec as P

norm_scale = 16.0
penalty_value = 8.0
penalty_slope = 4.0
LANES = 128

UU = [(a, b) for a in range(4) for b in range(a, 4)]
XX = [(0, 0), (0, 1), (1, 1)]
NAMES = [(kind,) + pair for kind, pairs in (("kuu", UU), ("guu", UU), ("kxx", XX), ("gxx", XX)) for pair in pairs]
AT = {name: k for k, name in enumerate(NAMES)}


def passed_along(array, axis, by):
    peers = lax.axis_size(axis)
    return lax.ppermute(array, axis, [(i, (i + by) % peers) for i in range(peers)])


def neighbours(array, axis):
    if lax.axis_size(axis) == 4:
        return [lax.ppermute(array, axis, [(i, i ^ k) for i in range(4)]) for k in (1, 3)]
    return [passed_along(array, axis, 1), passed_along(array, axis, -1)]


def line_shared(array, axis):
    peers = lax.axis_size(axis)
    if peers == 4:
        shared = [lax.ppermute(array, axis, [(i, i ^ k) for i in range(4)]) for k in (3, 2, 1)]
        return [array] + shared[::-1], [(k ^ 1, k ^ 3) for k in range(4)]
    shared = [passed_along(array, axis, k) for k in range(1, peers)]
    return [array] + shared, [tuple(sorted({(k + 1) % peers, (k - 1) % peers})) for k in range(peers)]


def summed_over_both(array, outer, inner):
    across, within = lax.axis_size(outer), lax.axis_size(inner)
    shifts = [(o, i) for o in range(across) for i in range(within)]
    total = array
    for o, i in shifts[1:]:
        pairs = [
            (x * within + y, (x + o) % across * within + (y + i) % within) for x, y in shifts
        ]
        total = total + lax.ppermute(array, (outer, inner), pairs)
    return total


def iota(shape, axis):
    return lax.broadcasted_iota(jnp.int32, shape, axis)


def row_after(w):
    rows = w[0].shape[0]
    zero = jnp.zeros((8, LANES), jnp.float32)
    return [pltpu.roll(jnp.concatenate([p, zero], axis=0), rows + 7, 0)[:rows] for p in w]


def row_before(w):
    rows = w[0].shape[0]
    zero = jnp.zeros((8, LANES), jnp.float32)
    return [pltpu.roll(jnp.concatenate([p, zero], axis=0), 1, 0)[:rows] for p in w]


def col_after(w):
    at_end = iota(w[0].shape, 1) == LANES - 1
    turned = [pltpu.roll(p, LANES - 1, 1) for p in w]
    return [jnp.where(at_end, n, p) for p, n in zip(turned, turned[1:] + [0.0])]


def col_before(w):
    at_start = iota(w[0].shape, 1) == 0
    turned = [pltpu.roll(p, 1, 1) for p in w]
    return [jnp.where(at_start, n, p) for p, n in zip(turned, [0.0] + turned[:-1])]


def each(f, *fields):
    return [f(*parts) for parts in zip(*fields)]


def minus(u, w):
    return each(lambda a, b: a - b, u, w)


def times(u, w):
    return each(lambda a, b: a * b, u, w)


def second_rows(w):
    return each(lambda a, b, c: a + b - (c + c), row_before(w), row_after(w), w)


def second_cols(w):
    return each(lambda a, b, c: a + b - (c + c), col_before(w), col_after(w), w)


def stiffness(w, live_thick, thick, support):
    bend_rows = times(live_thick, second_rows(w))
    bend_cols = times(thick, second_cols(w))
    return each(
        lambda f, a, r, c: f * a + (r + c), support, w, second_rows(bend_rows), second_cols(bend_cols)
    )


def differences(w):
    return minus(row_after(w), w), minus(col_after(w), w)


def membrane(along_rows, along_cols, stress):
    nuu, nvv, nuv = stress
    rows = each(lambda n, r, m, c: n * r + m * c, nuu, along_rows, nuv, along_cols)
    cols = each(lambda n, c, m, r: n * c + m * r, nvv, along_cols, nuv, along_rows)
    return rows, cols


def geometric(w, stress):
    rows, cols = membrane(*differences(w), stress)
    return each(
        lambda rb, r, cb, c: (rb - r) + (cb - c), row_before(rows), rows, col_before(cols), cols
    )


def cut(value):
    return [value[:, h * LANES : (h + 1) * LANES] for h in range(value.shape[1] // LANES)]


def joined(w):
    return jnp.concatenate(w, axis=1)


def live_of(rows_ref, slot, shape):
    return iota(shape, 0) < rows_ref[slot]


def masked(live, value):
    return [jnp.where(live, p, 0.0) for p in cut(value)]


def column_sums(product):
    return jnp.sum(product, axis=0, keepdims=True)


def folded(w):
    total = sum(w[1:], w[0])
    return jnp.sum(total.reshape(total.shape[0] // 8, 8, LANES), axis=0)


def packed(rows):
    rows = list(rows)
    rows += [jnp.zeros_like(rows[0])] * (-len(rows) % 8)
    lane = iota((8, LANES), 1)
    out = jnp.zeros((8, LANES), jnp.float32)
    for tile in range(len(rows) // 8):
        total = jnp.sum(jnp.concatenate(rows[8 * tile : 8 * tile + 8], axis=0), axis=1, keepdims=True)
        out = jnp.where(lane == tile, total, out)
    return out


def place(rows_ref, matched_ref, slots):
    inner = lax.axis_size(("sub", "half"))
    mine = [lax.axis_index("patch") * slots + s for s in range(slots)]
    match = [
        matched_ref[s] // (inner * slots) * slots + lax.rem(matched_ref[s], slots) for s in range(slots)
    ]
    return mine, match


STACK = 8


def edge_row(rows_ref, slot, side, depth, prows):
    return slot * prows + (rows_ref[slot] - 1 - depth if side else depth)


def stacked(rows_ref, prows):
    return [(4 * s + 2 * v + side, v, s, side) for s in range(2) for v in range(2) for side in range(2)]


def labels_of(rows_ref, matched_ref):
    mine, match = place(rows_ref, matched_ref, 2)
    row = iota((STACK, LANES), 0)
    label = jnp.full((STACK, LANES), 0, jnp.int32)
    for s in range(2):
        for side, number in enumerate((mine[s], match[s])):
            label = jnp.where((row // 4 == s) & (row % 2 == side), number, label)
    return label.astype(jnp.float32)


def other_side(stack):
    row = iota(stack.shape, 0)
    return jnp.where(row % 2 == 0, pltpu.roll(stack, STACK - 1, 0), pltpu.roll(stack, 1, 0))


def other_vector(w):
    row = iota(w[0].shape, 0)
    return [jnp.where(row // 2 % 2 == 0, pltpu.roll(p, STACK - 2, 0), pltpu.roll(p, 2, 0)) for p in w]


def opposite(label, near):
    found = None
    for labels, stacks in near:
        turned, parts = other_side(labels), [[other_side(p) for p in w] for w in stacks]
        for shift in (0, 4):
            if shift:
                turned, parts = pltpu.roll(turned, 4, 0), [[pltpu.roll(p, 4, 0) for p in w] for w in parts]
            here = turned == label
            picked = [[jnp.where(here, p, 0.0) for p in w] for w in parts]
            found = picked if found is None else [each(lambda x, y: x + y, f, p) for f, p in zip(found, picked)]
    return found


def meeting(own, met):
    jump = minus(own[0], met[0])
    slope = each(lambda a, b, c, d: (a + b) - (c + d), own[0], met[0], own[1], met[1])
    return jump, slope


def interface_rows(own, met):
    jump, slope = meeting(own, met)
    return (
        each(lambda j, m: penalty_value * j + penalty_slope * m, jump, slope),
        [-penalty_slope * m for m in slope],
    )


def local_rows(elem_ref, rows_dev):
    square = (rows_dev, rows_dev)
    if rows_dev & (rows_dev - 1) == 0:
        local = jnp.bitwise_and(elem_ref[...], rows_dev - 1)
    else:
        local = lax.rem(elem_ref[...], rows_dev)
    spread = jnp.broadcast_to(local.astype(jnp.float32), square)
    return jnp.sum(jnp.where(iota(square, 0) == iota(square, 1), spread, 0.0), axis=1, keepdims=True)


def pack_rows_kernel(stress_ref, elem_ref, pay_ref, elem, held, sems):
    rows_dev, ncol = stress_ref.shape[1:]
    get = pltpu.make_async_copy(elem_ref, elem, sems.at[0])
    get.start()
    planes = [
        pltpu.make_async_copy(stress_ref.at[j], held.at[:, pl.ds(j * ncol, ncol)], sems.at[1 + j])
        for j in range(3)
    ]
    for copy in planes:
        copy.start()
    get.wait()
    column = local_rows(elem, rows_dev)
    held[:, 3 * ncol :] = jnp.broadcast_to(column, (rows_dev, LANES)).astype(jnp.bfloat16)
    for copy in planes:
        copy.wait()
    put = pltpu.make_async_copy(held, pay_ref, sems.at[4])
    put.start()
    put.wait()


def pack_blocks_kernel(stress_ref, elem_ref, pay_ref, elem, held, get_sem, in_sems, out_sems):
    blocks, ncol = held.shape[0], stress_ref.shape[3]
    halves = ncol // LANES
    get = pltpu.make_async_copy(elem_ref, elem, get_sem)
    get.start()
    fetch, put = [], []
    for t in range(3 * halves):
        to = held.at[:, pl.ds(16 * t, 16), :]
        source = stress_ref.at[t // halves, :, :, pl.ds(t % halves * LANES, LANES)]
        fetch.append(pltpu.make_async_copy(source, to, in_sems.at[t]))
        put.append(pltpu.make_async_copy(to, pay_ref.at[:, pl.ds(16 * t, 16), :], out_sems.at[t]))
        fetch[-1].start()
    get.wait()
    column = jnp.broadcast_to(local_rows(elem, 16 * blocks), (16 * blocks, LANES))
    lane = iota((8, LANES), 1)
    for k in range(blocks):
        both = jnp.where(lane < LANES // 2, column[16 * k : 16 * k + 8], column[16 * k + 8 : 16 * k + 16])
        held[k, 48 * halves :, :] = both.astype(jnp.bfloat16)
    tail = pl.ds(48 * halves, 8)
    put.append(pltpu.make_async_copy(held.at[:, tail, :], pay_ref.at[:, tail, :], out_sems.at[3 * halves]))
    put[-1].start()
    for t in range(3 * halves):
        fetch[t].wait()
        put[t].start()
    for copy in put:
        copy.wait()


def unpacked(arrived_ref, ncol):
    if len(arrived_ref.shape) == 2:
        return arrived_ref[:, : 3 * ncol], arrived_ref[:, 3 * ncol :].astype(jnp.float32)
    blocks, halves = arrived_ref.shape[0], ncol // LANES
    forces = jnp.concatenate(
        [
            jnp.concatenate([arrived_ref[k, 16 * t : 16 * t + 16, :] for k in range(blocks)], axis=0)
            for t in range(3 * halves)
        ],
        axis=1,
    )
    tiles = [arrived_ref[k, 48 * halves :, :].astype(jnp.float32) for k in range(blocks)]
    half = LANES // 2
    column = jnp.concatenate([t[:, at : at + 1] for t in tiles for at in (0, half)], axis=0)
    return forces, jnp.broadcast_to(column, (16 * blocks, LANES))


def edge_kernel(rows_ref, matched_ref, vec_ref, edge_ref):
    rows_dev, ncol = vec_ref.shape[1:]
    halves = ncol // LANES
    for depth in range(2):
        for at, v, s, side in stacked(rows_ref, rows_dev // 2):
            row = vec_ref[v, pl.ds(edge_row(rows_ref, s, side, depth, rows_dev // 2), 1), :]
            for h, part in enumerate(cut(row)):
                to = STACK * (depth * halves + h) + at
                edge_ref[to : to + 1, :] = part
    edge_ref[2 * STACK * halves :, :] = labels_of(rows_ref, matched_ref)


FIRST = [("kxx", 0, 0), ("kxx", 0, 1), ("kxx", 1, 1), ("kuu", 2, 2), ("kuu", 2, 3), ("kuu", 3, 3)]


RIM = [("prec", 2), ("thick", 3), ("support", 2), ("uk", 2), ("kuk", 2)]
RIM_AT = {name: sum(n for _, n in RIM[:i]) for i, (name, _) in enumerate(RIM)}
RIM_STACKS = sum(n for _, n in RIM)


def stiff_kernel(rows_ref, vec_ref, thick_ref, support_ref, uk_ref, kuk_ref, prec_ref, sums_ref, rim_ref, k_ref):
    slots = rows_ref.shape[0]
    rows_dev, ncol = thick_ref.shape
    prows = rows_dev // slots
    totals = {}
    for s in range(slots):
        at = slice(s * prows, (s + 1) * prows)
        live = live_of(rows_ref, s, (prows, LANES))
        thick, support = cut(thick_ref[at, :]), cut(support_ref[at, :])
        live_thick = masked(live, thick_ref[at, :])
        prec = each(lambda f, t: jnp.where(live, 1.0 / (f + 12.0 * t), 0.0), support, thick)
        prec_ref[at, :] = joined(prec)
        for v in range(2):
            kw = stiffness(masked(live, vec_ref[v, at, :]), live_thick, thick, support)
            k_ref[v, at, :] = joined(kw)
            uk_ref[v, at, :] = joined(times(prec, kw))
        for v in range(2):
            kuk_ref[v, at, :] = joined(stiffness(cut(uk_ref[v, at, :]), live_thick, thick, support))
        for a in range(2):
            wa = masked(live, vec_ref[a, at, :])
            for b in range(a, 2):
                for name, product in (
                    (("kxx", a, b), times(wa, cut(k_ref[b, at, :]))),
                    (("kuu", 2 + a, 2 + b), times(cut(uk_ref[a, at, :]), cut(kuk_ref[b, at, :]))),
                ):
                    part = folded(product)
                    totals[name] = totals[name] + part if s else part
    for k, name in enumerate(FIRST):
        sums_ref[8 * k : 8 * k + 8, :] = totals[name]
    sources = {"prec": prec_ref, "thick": thick_ref, "support": support_ref, "uk": uk_ref, "kuk": kuk_ref}
    for name, depths in RIM:
        for depth in range(depths):
            for at, v, s, side in stacked(rows_ref, prows):
                rows = pl.ds(edge_row(rows_ref, s, side, depth, prows), 1)
                to = STACK * (RIM_AT[name] + depth) + at
                ref = sources[name]
                rim_ref[to : to + 1, :] = ref[rows, :] if len(ref.shape) == 2 else ref[v, rows, :]


def rim_of(rim_ref, name, depth):
    at = STACK * (RIM_AT[name] + depth)
    return cut(rim_ref[at : at + STACK, :])


def sent_stack(ref, kind, depth, halves):
    at = (2 * kind + depth) * halves
    return [ref[STACK * (at + h) : STACK * (at + h + 1), :] for h in range(halves)]


PIECE = 16


def gram_kernel(
    rows_ref, arrived_ref, vec_ref, thick_ref, support_ref, prec_ref, uk_in, kuk_in, sums_in, rim_ref,
    edge_ref, below_ref, above_ref, v_ref, uk_ref, kuk_ref, stress_ref, out_ref,
):
    slots = rows_ref.shape[0]
    rows_dev, ncol = prec_ref.shape
    prows = rows_dev // slots
    halves = ncol // LANES
    forces, index = unpacked(arrived_ref, ncol)
    lane = iota(index.shape, 1).astype(jnp.float32)
    pick = jnp.concatenate(
        [
            jnp.where(index == lane + float(h * LANES), 1.0, 0.0).astype(jnp.bfloat16)
            for h in range(rows_dev // LANES)
        ],
        axis=1,
    )
    placed = lax.dot_general(
        pick, forces, (((0,), (0,)), ((), ())), preferred_element_type=jnp.float32
    )
    for j in range(3):
        stress_ref[j] = placed[:, j * ncol : (j + 1) * ncol]
    totals = {name: sums_in[8 * k : 8 * k + 8, :] for k, name in enumerate(FIRST)}

    def add(name, product):
        part = folded(product)
        totals[name] = totals[name] + part if name in totals else part

    def add_stack(first, second, product):
        part = sum(product[1:], product[0])
        vector = iota(part.shape, 0) // 2 % 2
        totals[first] = totals[first] + jnp.where(vector == 0, part, 0.0)
        if second is not None:
            totals[second] = totals[second] + jnp.where(vector == 1, part, 0.0)

    uk_ref[...] = uk_in[...]
    kuk_ref[...] = kuk_in[...]
    label = edge_ref[2 * STACK * halves :, :]

    def depths_of(ref):
        return [[ref[STACK * (d * halves + h) : STACK * (d * halves + h + 1), :] for h in range(halves)] for d in range(2)]

    own = depths_of(edge_ref)
    met = opposite(label, [(ref[2 * STACK * halves :, :], depths_of(ref)) for ref in (below_ref, above_ref)])
    added = interface_rows(own, met)
    scaled = [times(rim_of(rim_ref, "prec", d), added[d]) for d in range(2)]
    bend = [
        each(lambda t, y, x: t * (y - (x + x)), rim_of(rim_ref, "thick", 0), scaled[1], scaled[0]),
        each(lambda t, y, x: t * (y - (x + x)), rim_of(rim_ref, "thick", 1), scaled[0], scaled[1]),
        times(rim_of(rim_ref, "thick", 2), scaled[1]),
    ]
    across = [second_cols(times(rim_of(rim_ref, "thick", d), second_cols(scaled[d]))) for d in range(2)]
    extra = [
        each(
            lambda f, z, p, q, c: f * z + (p - (q + q)) + c,
            rim_of(rim_ref, "support", 0), scaled[0], bend[1], bend[0], across[0],
        ),
        each(
            lambda f, z, p, q, r, c: f * z + (p - (q + q) + r) + c,
            rim_of(rim_ref, "support", 1), scaled[1], bend[0], bend[1], bend[2], across[1],
        ),
        each(lambda p, q: p - (q + q), bend[1], bend[2]),
        bend[2],
    ]
    for d in range(2):
        n, z, e, x = added[d], scaled[d], extra[d], own[d]
        kuk = rim_of(rim_ref, "kuk", d)
        add_stack(("kxx", 0, 0), ("kxx", 1, 1), times(x, n))
        add_stack(("kxx", 0, 1), None, times(x, other_vector(n)))
        add_stack(("kuu", 2, 2), ("kuu", 3, 3), each(lambda r, p, q: r * (p + p + q), z, kuk, e))
        turned, z_turned = other_vector(each(lambda p, q: p + q, kuk, e)), other_vector(z)
        add_stack(("kuu", 2, 3), None, each(lambda r, t, p, w: r * t + p * w, z, turned, kuk, z_turned))
    for d in range(4):
        for at, v, s, side in stacked(rows_ref, prows):
            rows = pl.ds(edge_row(rows_ref, s, side, d, prows), 1)
            kuk_ref[v, rows, :] += joined([p[at : at + 1] for p in extra[d]])
            if d < 2:
                uk_ref[v, rows, :] += joined([p[at : at + 1] for p in scaled[d]])
    for s in range(slots):
        at = slice(s * prows, (s + 1) * prows)
        live = live_of(rows_ref, s, (prows, LANES))
        stress = [cut(stress_ref[j, at, :]) for j in range(3)]
        prec = cut(prec_ref[at, :])
        x = [masked(live, vec_ref[v, at, :]) for v in range(2)]
        for b in range(2):
            gx = geometric(x[b], stress)
            v_ref[b, at, :] = joined(each(lambda w, p, g: w + p * g, x[b], prec, gx))
            for a in range(b + 1):
                add(("gxx", a, b), times(x[a], gx))
    basis = [(v_ref, 0), (v_ref, 1), (uk_ref, 0), (uk_ref, 1)]
    pieces = [(s, c) for s in range(slots) for c in range(0, prows, PIECE)]

    def piece(ref, v, s, c, low=0, high=0):
        start, stop = max(c - low, 0), min(c + PIECE + high, prows)
        parts = cut(ref[v, s * prows + start : s * prows + stop, :])
        zero = [jnp.zeros((8, LANES), jnp.float32)]
        head, tail = zero * ((start - c + low) // 8), zero * ((c + PIECE + high - stop) // 8)
        return [jnp.concatenate([*head, p, *tail], axis=0) if head or tail else p for p in parts]

    for s, c in pieces:
        stress = [piece(stress_ref, j, s, c) for j in range(3)]
        first = []
        for b in range(4):
            held = piece(*basis[b], s, c, high=8)
            w = [p[:PIECE] for p in held]
            along_rows = [pltpu.roll(p, PIECE + 7, 0)[:PIECE] - q for p, q in zip(held, w)]
            along_cols = minus(col_after(w), w)
            first.append((along_rows, along_cols))
            fr, fc = membrane(along_rows, along_cols, stress)
            for a in range(b + 1):
                add(("guu", a, b), each(lambda p, x, q, y: p * x + q * y, first[a][0], fr, first[a][1], fc))
    for s, c in pieces:
        at = slice(s * prows + c, s * prows + c + PIECE)
        live = iota((PIECE, LANES), 0) < rows_ref[s] - c
        thick, support = cut(thick_ref[at, :]), cut(support_ref[at, :])
        live_thick = masked(live, thick_ref[at, :])
        bends = []
        for v in range(2):
            held = piece(v_ref, v, s, c, 8, 8)
            w = [p[8 : 8 + PIECE] for p in held]
            rows = [
                pltpu.roll(p, PIECE + 15, 0)[8 : 8 + PIECE] + pltpu.roll(p, 1, 0)[8 : 8 + PIECE] - (q + q)
                for p, q in zip(held, w)
            ]
            bends.append((w, rows, second_cols(w)))
        for b in range(2):
            w, rows, cols = bends[b]
            sw, tr, tc = times(support, w), times(live_thick, rows), times(thick, cols)
            for a in range(b + 1):
                add(
                    ("kuu", a, b),
                    each(lambda u, x, p, y, q, z: u * x + p * y + q * z, bends[a][0], sw, bends[a][1], tr, bends[a][2], tc),
                )
        for b in range(2):
            kuk = piece(kuk_ref, b, s, c)
            for a in range(2):
                add(("kuu", a, 2 + b), times(bends[a][0], kuk))
    for d in range(2):
        for at, v, s, side in stacked(rows_ref, prows):
            row = v_ref[v, pl.ds(edge_row(rows_ref, s, side, d, prows), 1), :]
            for h, part in enumerate(cut(row)):
                to = STACK * (d * halves + h) + at
                out_ref[to : to + 1, :] = part
        for h, part in enumerate(each(lambda u, z: u + z, rim_of(rim_ref, "uk", d), scaled[d])):
            to = STACK * ((2 + d) * halves + h)
            out_ref[to : to + STACK, :] = part
    tile = packed([column_sums(totals[name]) for name in NAMES])
    out_ref[4 * STACK * halves :, :] = jnp.where(iota(tile.shape, 1) == LANES - 1, label, tile)


def apply_kernel(rows_ref, thick_ref, support_ref, prec_ref, stress_ref, v_ref, kuk_ref, a_ref, c_ref, d_ref):
    slots = rows_ref.shape[0]
    rows_dev, ncol = thick_ref.shape
    prows = rows_dev // slots
    for s in range(slots):
        at = slice(s * prows, (s + 1) * prows)
        live = live_of(rows_ref, s, (prows, LANES))
        thick, support = cut(thick_ref[at, :]), cut(support_ref[at, :])
        live_thick = masked(live, thick_ref[at, :])
        prec = cut(prec_ref[at, :])
        stress = [cut(stress_ref[j, at, :]) for j in range(3)]
        for v in range(2):
            w = cut(v_ref[v, at, :])
            a_ref[v, at, :] = joined(each(lambda u, p, g: u + p * g, w, prec, geometric(w, stress)))
            c_ref[v, at, :] = joined(times(prec, stiffness(w, live_thick, thick, support)))
            d_ref[v, at, :] = joined(times(prec, cut(kuk_ref[v, at, :])))


def line_parts(ref):
    halves = (ref.shape[0] // STACK - 1) // 4
    tag = 4 * STACK * halves
    return ref[tag:, LANES - 1 :], [sent_stack(ref, kind, d, halves) for kind in range(2) for d in range(2)]


def line_kernel(near, *refs):
    line, out_ref = refs[:-2], refs[-1]
    held = [line_parts(ref) for ref in line]
    sums = [None] * 6
    for (label, stacks), others in zip(held, near):
        met = opposite(label, [held[k] for k in others])
        g, k = (meeting(stacks[2 * i : 2 * i + 2], met[2 * i : 2 * i + 2]) for i in range(2))
        g_turned, k_turned = [other_vector(w) for w in g], [other_vector(w) for w in k]
        for i, (p, q) in enumerate(((g, g), (g, g_turned), (g, k), (g, k_turned), (k, k), (k, k_turned))):
            part = each(
                lambda a, b, c, d: penalty_value * (a * b) + penalty_slope * (c * d), p[0], q[0], p[1], q[1]
            )
            part = sum(part[1:], part[0])
            sums[i] = part if sums[i] is None else sums[i] + part
    total = line[0][-STACK:, :]
    for ref in line[1:]:
        total = total + ref[-STACK:, :]
    row = iota(total.shape, 0)
    masks = [(row % 2 == 1) & (row // 2 % 2 == v) for v in range(2)]
    rows = {
        (0, 0): (0, 0), (1, 1): (0, 1), (0, 1): (1, 0), (0, 2): (2, 0), (1, 3): (2, 1), (0, 3): (3, 0), (1, 2): (3, 1),
        (2, 2): (4, 0), (3, 3): (4, 1), (2, 3): (5, 0),
    }
    out_ref[...] = total + packed([column_sums(jnp.where(masks[rows[p][1]], sums[rows[p][0]], 0.0)) for p in UU])


def join_kernel(near, rows_ref, prec_ref, stress_ref, uk_ref, c_in, d_in, *refs):
    line, (b_ref, c_ref, d_ref) = refs[:-4], refs[-3:]
    c_ref[...] = c_in[...]
    d_ref[...] = d_in[...]
    prows = c_in.shape[1] // 2
    for s in range(2):
        at = slice(s * prows, (s + 1) * prows)
        prec = cut(prec_ref[at, :])
        stress = [cut(stress_ref[j, at, :]) for j in range(3)]
        for v in range(2):
            uk = cut(uk_ref[v, at, :])
            gk = geometric(uk, stress)
            b_ref[v, at, :] = joined(each(lambda u, p, g: u + p * g, uk, prec, gk))
    label, stacks = line_parts(line[0])
    met = opposite(label, [line_parts(ref) for ref in line[1:]])
    for i, ref in enumerate((c_ref, d_ref)):
        added = interface_rows(stacks[2 * i : 2 * i + 2], met[2 * i : 2 * i + 2])
        for d in range(2):
            for at, v, s, side in stacked(rows_ref, prows):
                rows = pl.ds(edge_row(rows_ref, s, side, d, prows), 1)
                ref[v, rows, :] += prec_ref[rows, :] * joined([p[at : at + 1] for p in added[d]])


def form(table, left, right):
    total = None
    for i, c in left.items():
        row = None
        for j, d in right.items():
            term = d * table[i, j]
            row = term if row is None else row + term
        total = c * row if total is None else total + c * row
    return total


def final_kernel(cells, total_ref, a_ref, b_ref, c_ref, d_ref, out_ref, held, sems):
    rows_dev, ncol = a_ref.shape[1:]
    prows = rows_dev // 2
    total = total_ref[...]

    def value(*name):
        k = AT[name]
        return jnp.broadcast_to(total[k % 8 : k % 8 + 1, k // 8 : k // 8 + 1], (8, LANES))

    k_table, g_table = {}, {}
    for a, b in UU:
        k_table[a, b] = k_table[b, a] = value("kuu", a, b)
        g_table[a, b] = g_table[b, a] = value("guu", a, b)
    first_a, cross_k, second_a = (value("kxx", a, b) for a, b in XX)
    first_g, cross_g, second_g = (value("gxx", a, b) for a, b in XX)
    ratio = cross_k / first_a
    other_a = second_a - ratio * cross_k
    other_q = second_g - 2.0 * ratio * cross_g + ratio * ratio * first_g
    mu_first = first_g / first_a
    mu_other = other_q / other_a
    one = jnp.ones_like(ratio)
    new_first = {0: one, 2: -mu_first}
    new_second = {0: -ratio, 1: one, 2: mu_other * ratio, 3: -mu_other}
    a1 = form(k_table, new_first, new_first)
    c = form(k_table, new_first, new_second)
    a2 = form(k_table, new_second, new_second)
    g1 = form(g_table, new_first, new_first)
    h = form(g_table, new_first, new_second)
    g2 = form(g_table, new_second, new_second)
    r = c / a1
    b2 = a2 - r * c
    q2 = g2 - 2.0 * r * h + r * r * g1
    mus = [g1 / a1, q2 / b2]
    scales = [jnp.sqrt(norm_scale * cells / a1), jnp.sqrt(norm_scale * cells / b2)]
    lead = [
        {i: scales[0] * f for i, f in new_first.items()},
        {i: scales[1] * (f - r * new_first[i] if i in new_first else f) for i, f in new_second.items()},
    ]
    copies = []
    tall = (prows // 8, 8, LANES)
    for s in range(2):
        at = pl.ds(s * prows, prows)
        for v in range(2):
            for h in range(ncol // LANES):
                cols = pl.ds(h * LANES, LANES)
                acc = None
                for i in (0, 1):
                    if i in lead[v]:
                        f, g = lead[v][i], lead[v][2 + i]
                        parts = [ref[i, at, cols].reshape(tall) for ref in (a_ref, b_ref, c_ref, d_ref)]
                        term = f * parts[0] + g * parts[1]
                        term = term - ((mus[v] * f) * parts[2] + (mus[v] * g) * parts[3])
                        acc = term if acc is None else acc + term
                held[v, at, cols] = acc.reshape(prows, LANES)
            copies.append(pltpu.make_async_copy(held.at[v, at, :], out_ref.at[v, at, :], sems.at[2 * s + v]))
            copies[-1].start()
    for copy in copies:
        copy.wait()


def call(body, outs, kinds, scratch=(), flops=1_000_000, out_kind="v"):
    spaces = {"s": pltpu.SMEM, "v": pltpu.VMEM, "h": pltpu.HBM, "a": pl.ANY}
    return pl.pallas_call(
        body,
        out_shape=[pltpu.HBM(s, d) if out_kind == "h" else jax.ShapeDtypeStruct(s, d) for s, d in outs],
        in_specs=[pl.BlockSpec(memory_space=spaces[k]) for k in kinds],
        out_specs=[pl.BlockSpec(memory_space=spaces[out_kind]) for _ in outs],
        scratch_shapes=list(scratch),
        compiler_params=pltpu.CompilerParams(vmem_limit_bytes=32 * 1024 * 1024),
        cost_estimate=pl.CostEstimate(flops=flops, bytes_accessed=2_000_000, transcendentals=0),
    )


def per_device(vectors, prestress, thickness, foundation, patch_rows, matched, elem_row):
    owners = lax.axis_size("patch")
    inner = lax.axis_size(("sub", "half"))
    slots = patch_rows.shape[0]
    rows_dev, ncol = thickness.shape
    f32, bf16 = jnp.float32, jnp.bfloat16
    cells = float(owners * inner * rows_dev * ncol)
    field = ((2, rows_dev, ncol), f32)
    one = ((rows_dev, ncol), f32)
    sums = ((8 * len(FIRST), LANES), f32)
    tile = ((8, LANES), f32)

    width = 3 * ncol + LANES
    elem = pltpu.VMEM((1, rows_dev), jnp.int32)
    planes = jnp.transpose(prestress, (1, 0, 2))
    if rows_dev == 16 * owners * inner:
        tiles = 3 * (ncol // LANES)
        shape = (owners * inner, 16 * tiles + 8, LANES)
        planes = planes.reshape(3, owners * inner, 16, ncol)
        sems = [pltpu.SemaphoreType.DMA, pltpu.SemaphoreType.DMA((tiles,)), pltpu.SemaphoreType.DMA((tiles + 1,))]
        pack = pack_blocks_kernel
    else:
        shape = (rows_dev, width)
        sems = [pltpu.SemaphoreType.DMA((5,))]
        pack = pack_rows_kernel
    (payload,) = call(pack, [(shape, bf16)], "hh", [elem, pltpu.VMEM(shape, bf16), *sems], out_kind="h")(
        pltpu.with_memory_space_constraint(planes, pltpu.HBM),
        pltpu.with_memory_space_constraint(elem_row.reshape(1, rows_dev), pltpu.HBM),
    )
    arrived = lax.all_to_all(
        payload, ("patch", "sub", "half"), split_axis=0, concat_axis=0, tiled=True
    )
    halves = ncol // LANES
    (edges,) = call(edge_kernel, [(((2 * halves + 1) * STACK, LANES), f32)], "ssv")(patch_rows, matched, vectors)
    below, above = neighbours(edges, "patch")
    u_k, k_uk, prec, part, rim = call(
        stiff_kernel,
        [field, field, one, sums, ((RIM_STACKS * STACK, ncol), f32)],
        "svvv",
        [pltpu.VMEM(field[0], f32)],
    )(patch_rows, vectors, thickness, foundation)
    v, u_k, k_uk, stress, sent = call(
        gram_kernel,
        [field, field, field, ((3, rows_dev, ncol), f32), (((4 * halves + 1) * STACK, LANES), f32)],
        "svvvvvvvvvvvv",
    )(
        patch_rows, arrived, vectors, thickness, foundation, prec, u_k, k_uk, part, rim,
        edges, below, above,
    )
    line, near = line_shared(sent, "patch")
    a, c, d = call(apply_kernel, [field] * 3, "svvvvvv")(
        patch_rows, thickness, foundation, prec, stress, v, k_uk
    )
    (total,) = call(functools.partial(line_kernel, near), [tile], "v" * owners + "a")(*line, a)
    total = summed_over_both(total, "sub", "half")
    b, c, d = call(functools.partial(join_kernel, near), [field] * 3, "sv" + "v" * (len(near[0]) + 5) + "a")(
        patch_rows, prec, stress, u_k, c, d, line[0], *[line[k] for k in near[0]], line[2]
    )
    (modes,) = call(
        functools.partial(final_kernel, cells),
        [field],
        "vvvvv",
        [pltpu.VMEM(field[0], f32), pltpu.SemaphoreType.DMA((4,))],
        out_kind="h",
    )(total, a, b, c, d)
    return modes


def solution(mesh):
    in_specs = (
        P(None, ("groups", "patch", "sub", "half"), None),
        P(("groups", "patch", "sub", "half"), None, None),
        P(("groups", "patch", "sub", "half"), None),
        P(("groups", "patch", "sub", "half"), None),
        P(("groups", "patch", "sub", "half")),
        P(("groups", "patch", "sub", "half")),
        P(("groups", "patch", "sub", "half")),
    )
    out_specs = P(None, ("groups", "patch", "sub", "half"), None)
    return jax.shard_map(
        per_device, mesh=mesh, in_specs=in_specs, out_specs=out_specs, check_vma=False
    )
```

```python
import functools

import jax
import jax.numpy as jnp
from jax import lax
from jax.experimental import pallas as pl
from jax.experimental.pallas import tpu as pltpu
from jax.sharding import PartitionSpec as P

norm_scale = 16.0
penalty_value = 8.0
penalty_slope = 4.0
LANES = 128

UU = [(a, b) for a in range(4) for b in range(a, 4)]
XX = [(0, 0), (0, 1), (1, 1)]
NAMES = [(kind,) + pair for kind, pairs in (("kuu", UU), ("guu", UU), ("kxx", XX), ("gxx", XX)) for pair in pairs]
AT = {name: k for k, name in enumerate(NAMES)}


def passed_along(array, axis, by):
    peers = lax.axis_size(axis)
    return lax.ppermute(array, axis, [(i, (i + by) % peers) for i in range(peers)])


def neighbours(array, axis):
    if lax.axis_size(axis) == 4:
        return [lax.ppermute(array, axis, [(i, i ^ k) for i in range(4)]) for k in (1, 3)]
    return [passed_along(array, axis, 1), passed_along(array, axis, -1)]


def line_shared(array, axis):
    peers = lax.axis_size(axis)
    if peers == 4:
        shared = [lax.ppermute(array, axis, [(i, i ^ k) for i in range(4)]) for k in (3, 2, 1)]
        return [array] + shared[::-1], [(k ^ 1, k ^ 3) for k in range(4)]
    shared = [passed_along(array, axis, k) for k in range(1, peers)]
    return [array] + shared, [tuple(sorted({(k + 1) % peers, (k - 1) % peers})) for k in range(peers)]


def summed_over_both(array, outer, inner):
    across, within = lax.axis_size(outer), lax.axis_size(inner)
    shifts = [(o, i) for o in range(across) for i in range(within)]
    total = array
    for o, i in shifts[1:]:
        pairs = [
            (x * within + y, (x + o) % across * within + (y + i) % within) for x, y in shifts
        ]
        total = total + lax.ppermute(array, (outer, inner), pairs)
    return total


def iota(shape, axis):
    return lax.broadcasted_iota(jnp.int32, shape, axis)


def row_after(w):
    rows = w[0].shape[0]
    zero = jnp.zeros((8, LANES), jnp.float32)
    return [pltpu.roll(jnp.concatenate([p, zero], axis=0), rows + 7, 0)[:rows] for p in w]


def row_before(w):
    rows = w[0].shape[0]
    zero = jnp.zeros((8, LANES), jnp.float32)
    return [pltpu.roll(jnp.concatenate([p, zero], axis=0), 1, 0)[:rows] for p in w]


def col_after(w):
    at_end = iota(w[0].shape, 1) == LANES - 1
    turned = [pltpu.roll(p, LANES - 1, 1) for p in w]
    return [jnp.where(at_end, n, p) for p, n in zip(turned, turned[1:] + [0.0])]


def col_before(w):
    at_start = iota(w[0].shape, 1) == 0
    turned = [pltpu.roll(p, 1, 1) for p in w]
    return [jnp.where(at_start, n, p) for p, n in zip(turned, [0.0] + turned[:-1])]


def each(f, *fields):
    return [f(*parts) for parts in zip(*fields)]


def minus(u, w):
    return each(lambda a, b: a - b, u, w)


def times(u, w):
    return each(lambda a, b: a * b, u, w)


def second_rows(w):
    return each(lambda a, b, c: a + b - (c + c), row_before(w), row_after(w), w)


def second_cols(w):
    return each(lambda a, b, c: a + b - (c + c), col_before(w), col_after(w), w)


def stiffness(w, live_thick, thick, support):
    bend_rows = times(live_thick, second_rows(w))
    bend_cols = times(thick, second_cols(w))
    return each(
        lambda f, a, r, c: f * a + (r + c), support, w, second_rows(bend_rows), second_cols(bend_cols)
    )


def differences(w):
    return minus(row_after(w), w), minus(col_after(w), w)


def membrane(along_rows, along_cols, stress):
    nuu, nvv, nuv = stress
    rows = each(lambda n, r, m, c: n * r + m * c, nuu, along_rows, nuv, along_cols)
    cols = each(lambda n, c, m, r: n * c + m * r, nvv, along_cols, nuv, along_rows)
    return rows, cols


def geometric(w, stress):
    rows, cols = membrane(*differences(w), stress)
    return each(
        lambda rb, r, cb, c: (rb - r) + (cb - c), row_before(rows), rows, col_before(cols), cols
    )


def cut(value):
    return [value[:, h * LANES : (h + 1) * LANES] for h in range(value.shape[1] // LANES)]


def joined(w):
    return jnp.concatenate(w, axis=1)


def live_of(rows_ref, slot, shape):
    return iota(shape, 0) < rows_ref[slot]


def masked(live, value):
    return [jnp.where(live, p, 0.0) for p in cut(value)]


def column_sums(product):
    return jnp.sum(product, axis=0, keepdims=True)


def folded(w):
    total = sum(w[1:], w[0])
    return jnp.sum(total.reshape(total.shape[0] // 8, 8, LANES), axis=0)


def packed(rows):
    rows = list(rows)
    rows += [jnp.zeros_like(rows[0])] * (-len(rows) % 8)
    lane = iota((8, LANES), 1)
    out = jnp.zeros((8, LANES), jnp.float32)
    for tile in range(len(rows) // 8):
        total = jnp.sum(jnp.concatenate(rows[8 * tile : 8 * tile + 8], axis=0), axis=1, keepdims=True)
        out = jnp.where(lane == tile, total, out)
    return out


def place(rows_ref, matched_ref, slots):
    inner = lax.axis_size(("sub", "half"))
    mine = [lax.axis_index("patch") * slots + s for s in range(slots)]
    match = [
        matched_ref[s] // (inner * slots) * slots + lax.rem(matched_ref[s], slots) for s in range(slots)
    ]
    return mine, match


STACK = 8


def edge_row(rows_ref, slot, side, depth, prows):
    return slot * prows + (rows_ref[slot] - 1 - depth if side else depth)


def stacked(rows_ref, prows):
    return [(4 * s + 2 * v + side, v, s, side) for s in range(2) for v in range(2) for side in range(2)]


def labels_of(rows_ref, matched_ref):
    mine, match = place(rows_ref, matched_ref, 2)
    row = iota((STACK, LANES), 0)
    label = jnp.full((STACK, LANES), 0, jnp.int32)
    for s in range(2):
        for side, number in enumerate((mine[s], match[s])):
            label = jnp.where((row // 4 == s) & (row % 2 == side), number, label)
    return label.astype(jnp.float32)


def other_side(stack):
    row = iota(stack.shape, 0)
    return jnp.where(row % 2 == 0, pltpu.roll(stack, STACK - 1, 0), pltpu.roll(stack, 1, 0))


def other_vector(w):
    row = iota(w[0].shape, 0)
    return [jnp.where(row // 2 % 2 == 0, pltpu.roll(p, STACK - 2, 0), pltpu.roll(p, 2, 0)) for p in w]


def opposite(label, near):
    found = None
    for labels, stacks in near:
        turned, parts = other_side(labels), [[other_side(p) for p in w] for w in stacks]
        for shift in (0, 4):
            if shift:
                turned, parts = pltpu.roll(turned, 4, 0), [[pltpu.roll(p, 4, 0) for p in w] for w in parts]
            here = turned == label
            picked = [[jnp.where(here, p, 0.0) for p in w] for w in parts]
            found = picked if found is None else [each(lambda x, y: x + y, f, p) for f, p in zip(found, picked)]
    return found


def meeting(own, met):
    jump = minus(own[0], met[0])
    slope = each(lambda a, b, c, d: (a + b) - (c + d), own[0], met[0], own[1], met[1])
    return jump, slope


def interface_rows(own, met):
    jump, slope = meeting(own, met)
    return (
        each(lambda j, m: penalty_value * j + penalty_slope * m, jump, slope),
        [-penalty_slope * m for m in slope],
    )


def local_rows(elem_ref, rows_dev):
    square = (rows_dev, rows_dev)
    if rows_dev & (rows_dev - 1) == 0:
        local = jnp.bitwise_and(elem_ref[...], rows_dev - 1)
    else:
        local = lax.rem(elem_ref[...], rows_dev)
    spread = jnp.broadcast_to(local.astype(jnp.float32), square)
    return jnp.sum(jnp.where(iota(square, 0) == iota(square, 1), spread, 0.0), axis=1, keepdims=True)


def pack_rows_kernel(stress_ref, elem_ref, pay_ref, elem, held, sems):
    rows_dev, ncol = stress_ref.shape[1:]
    get = pltpu.make_async_copy(elem_ref, elem, sems.at[0])
    get.start()
    planes = [
        pltpu.make_async_copy(stress_ref.at[j], held.at[:, pl.ds(j * ncol, ncol)], sems.at[1 + j])
        for j in range(3)
    ]
    for copy in planes:
        copy.start()
    get.wait()
    column = local_rows(elem, rows_dev)
    held[:, 3 * ncol :] = jnp.broadcast_to(column, (rows_dev, LANES)).astype(jnp.bfloat16)
    for copy in planes:
        copy.wait()
    put = pltpu.make_async_copy(held, pay_ref, sems.at[4])
    put.start()
    put.wait()


def pack_blocks_kernel(stress_ref, elem_ref, pay_ref, elem, planes, held, get_sem, in_sems, out_sems):
    blocks, ncol = held.shape[0], stress_ref.shape[3]
    halves = ncol // LANES
    get = pltpu.make_async_copy(elem_ref, elem, get_sem)
    get.start()
    fetch = [pltpu.make_async_copy(stress_ref.at[j], planes.at[j], in_sems.at[j]) for j in range(3)]
    for copy in fetch:
        copy.start()
    put = []
    get.wait()
    column = jnp.broadcast_to(local_rows(elem, 16 * blocks), (16 * blocks, LANES))
    lane = iota((8, LANES), 1)
    for k in range(blocks):
        both = jnp.where(lane < LANES // 2, column[16 * k : 16 * k + 8], column[16 * k + 8 : 16 * k + 16])
        held[k] = both.astype(jnp.bfloat16)
    put.append(pltpu.make_async_copy(held, pay_ref.at[:, pl.ds(48 * halves, 8), :], out_sems.at[3 * halves]))
    put[0].start()
    for t in range(3 * halves):
        if t % halves == 0:
            fetch[t // halves].wait()
        source = planes.at[t // halves, :, :, pl.ds(t % halves * LANES, LANES)]
        put.append(pltpu.make_async_copy(source, pay_ref.at[:, pl.ds(16 * t, 16), :], out_sems.at[t]))
        put[-1].start()
    for copy in put:
        copy.wait()


def unpacked(arrived_ref, ncol):
    if len(arrived_ref.shape) == 2:
        return arrived_ref[:, : 3 * ncol], arrived_ref[:, 3 * ncol :].astype(jnp.float32)
    blocks, halves = arrived_ref.shape[0], ncol // LANES
    forces = jnp.concatenate(
        [
            jnp.concatenate([arrived_ref[k, 16 * t : 16 * t + 16, :] for k in range(blocks)], axis=0)
            for t in range(3 * halves)
        ],
        axis=1,
    )
    tiles = [arrived_ref[k, 48 * halves :, :].astype(jnp.float32) for k in range(blocks)]
    half = LANES // 2
    column = jnp.concatenate([t[:, at : at + 1] for t in tiles for at in (0, half)], axis=0)
    return forces, jnp.broadcast_to(column, (16 * blocks, LANES))


def edge_kernel(rows_ref, matched_ref, vec_ref, edge_ref):
    rows_dev, ncol = vec_ref.shape[1:]
    halves = ncol // LANES
    for depth in range(2):
        for at, v, s, side in stacked(rows_ref, rows_dev // 2):
            row = vec_ref[v, pl.ds(edge_row(rows_ref, s, side, depth, rows_dev // 2), 1), :]
            for h, part in enumerate(cut(row)):
                to = STACK * (depth * halves + h) + at
                edge_ref[to : to + 1, :] = part
    edge_ref[2 * STACK * halves :, :] = labels_of(rows_ref, matched_ref)


FIRST = [("kxx", 0, 0), ("kxx", 0, 1), ("kxx", 1, 1), ("kuu", 2, 2), ("kuu", 2, 3), ("kuu", 3, 3)]


RIM = [("prec", 2), ("thick", 3), ("support", 2), ("uk", 2), ("kuk", 2)]
RIM_AT = {name: sum(n for _, n in RIM[:i]) for i, (name, _) in enumerate(RIM)}
RIM_STACKS = sum(n for _, n in RIM)


def stiff_kernel(rows_ref, vec_ref, thick_ref, support_ref, uk_ref, kuk_ref, prec_ref, sums_ref, rim_ref, k_ref):
    slots = rows_ref.shape[0]
    rows_dev, ncol = thick_ref.shape
    prows = rows_dev // slots
    totals = {}
    for s in range(slots):
        at = slice(s * prows, (s + 1) * prows)
        live = live_of(rows_ref, s, (prows, LANES))
        thick, support = cut(thick_ref[at, :]), cut(support_ref[at, :])
        live_thick = masked(live, thick_ref[at, :])
        prec = each(lambda f, t: jnp.where(live, 1.0 / (f + 12.0 * t), 0.0), support, thick)
        prec_ref[at, :] = joined(prec)
        for v in range(2):
            kw = stiffness(masked(live, vec_ref[v, at, :]), live_thick, thick, support)
            k_ref[v, at, :] = joined(kw)
            uk_ref[v, at, :] = joined(times(prec, kw))
        for v in range(2):
            kuk_ref[v, at, :] = joined(stiffness(cut(uk_ref[v, at, :]), live_thick, thick, support))
        for a in range(2):
            wa = masked(live, vec_ref[a, at, :])
            for b in range(a, 2):
                for name, product in (
                    (("kxx", a, b), times(wa, cut(k_ref[b, at, :]))),
                    (("kuu", 2 + a, 2 + b), times(cut(uk_ref[a, at, :]), cut(kuk_ref[b, at, :]))),
                ):
                    part = folded(product)
                    totals[name] = totals[name] + part if s else part
    for k, name in enumerate(FIRST):
        sums_ref[8 * k : 8 * k + 8, :] = totals[name]
    sources = {"prec": prec_ref, "thick": thick_ref, "support": support_ref, "uk": uk_ref, "kuk": kuk_ref}
    for name, depths in RIM:
        for depth in range(depths):
            for at, v, s, side in stacked(rows_ref, prows):
                rows = pl.ds(edge_row(rows_ref, s, side, depth, prows), 1)
                to = STACK * (RIM_AT[name] + depth) + at
                ref = sources[name]
                rim_ref[to : to + 1, :] = ref[rows, :] if len(ref.shape) == 2 else ref[v, rows, :]


def rim_of(rim_ref, name, depth):
    at = STACK * (RIM_AT[name] + depth)
    return cut(rim_ref[at : at + STACK, :])


def sent_stack(ref, kind, depth, halves):
    at = (2 * kind + depth) * halves
    return [ref[STACK * (at + h) : STACK * (at + h + 1), :] for h in range(halves)]


PIECE = 16


def gram_kernel(
    rows_ref, arrived_ref, vec_ref, thick_ref, support_ref, prec_ref, uk_in, kuk_in, sums_in, rim_ref,
    edge_ref, below_ref, above_ref, v_ref, uk_ref, kuk_ref, stress_ref, out_ref,
):
    slots = rows_ref.shape[0]
    rows_dev, ncol = prec_ref.shape
    prows = rows_dev // slots
    halves = ncol // LANES
    forces, index = unpacked(arrived_ref, ncol)
    lane = iota(index.shape, 1).astype(jnp.float32)
    pick = jnp.concatenate(
        [
            jnp.where(index == lane + float(h * LANES), 1.0, 0.0).astype(jnp.bfloat16)
            for h in range(rows_dev // LANES)
        ],
        axis=1,
    )
    placed = lax.dot_general(
        pick, forces, (((0,), (0,)), ((), ())), preferred_element_type=jnp.float32
    )
    for j in range(3):
        stress_ref[j] = placed[:, j * ncol : (j + 1) * ncol]
    totals = {name: sums_in[8 * k : 8 * k + 8, :] for k, name in enumerate(FIRST)}

    def add(name, product):
        part = folded(product)
        totals[name] = totals[name] + part if name in totals else part

    def add_stack(first, second, product):
        part = sum(product[1:], product[0])
        vector = iota(part.shape, 0) // 2 % 2
        totals[first] = totals[first] + jnp.where(vector == 0, part, 0.0)
        if second is not None:
            totals[second] = totals[second] + jnp.where(vector == 1, part, 0.0)

    uk_ref[...] = uk_in[...]
    kuk_ref[...] = kuk_in[...]
    label = edge_ref[2 * STACK * halves :, :]

    def depths_of(ref):
        return [[ref[STACK * (d * halves + h) : STACK * (d * halves + h + 1), :] for h in range(halves)] for d in range(2)]

    own = depths_of(edge_ref)
    met = opposite(label, [(ref[2 * STACK * halves :, :], depths_of(ref)) for ref in (below_ref, above_ref)])
    added = interface_rows(own, met)
    scaled = [times(rim_of(rim_ref, "prec", d), added[d]) for d in range(2)]
    bend = [
        each(lambda t, y, x: t * (y - (x + x)), rim_of(rim_ref, "thick", 0), scaled[1], scaled[0]),
        each(lambda t, y, x: t * (y - (x + x)), rim_of(rim_ref, "thick", 1), scaled[0], scaled[1]),
        times(rim_of(rim_ref, "thick", 2), scaled[1]),
    ]
    across = [second_cols(times(rim_of(rim_ref, "thick", d), second_cols(scaled[d]))) for d in range(2)]
    extra = [
        each(
            lambda f, z, p, q, c: f * z + (p - (q + q)) + c,
            rim_of(rim_ref, "support", 0), scaled[0], bend[1], bend[0], across[0],
        ),
        each(
            lambda f, z, p, q, r, c: f * z + (p - (q + q) + r) + c,
            rim_of(rim_ref, "support", 1), scaled[1], bend[0], bend[1], bend[2], across[1],
        ),
        each(lambda p, q: p - (q + q), bend[1], bend[2]),
        bend[2],
    ]
    for d in range(2):
        n, z, e, x = added[d], scaled[d], extra[d], own[d]
        kuk = rim_of(rim_ref, "kuk", d)
        add_stack(("kxx", 0, 0), ("kxx", 1, 1), times(x, n))
        add_stack(("kxx", 0, 1), None, times(x, other_vector(n)))
        add_stack(("kuu", 2, 2), ("kuu", 3, 3), each(lambda r, p, q: r * (p + p + q), z, kuk, e))
        turned, z_turned = other_vector(each(lambda p, q: p + q, kuk, e)), other_vector(z)
        add_stack(("kuu", 2, 3), None, each(lambda r, t, p, w: r * t + p * w, z, turned, kuk, z_turned))
    for d in range(4):
        for at, v, s, side in stacked(rows_ref, prows):
            rows = pl.ds(edge_row(rows_ref, s, side, d, prows), 1)
            kuk_ref[v, rows, :] += joined([p[at : at + 1] for p in extra[d]])
            if d < 2:
                uk_ref[v, rows, :] += joined([p[at : at + 1] for p in scaled[d]])
    for s in range(slots):
        at = slice(s * prows, (s + 1) * prows)
        live = live_of(rows_ref, s, (prows, LANES))
        stress = [cut(stress_ref[j, at, :]) for j in range(3)]
        prec = cut(prec_ref[at, :])
        x = [masked(live, vec_ref[v, at, :]) for v in range(2)]
        for b in range(2):
            gx = geometric(x[b], stress)
            v_ref[b, at, :] = joined(each(lambda w, p, g: w + p * g, x[b], prec, gx))
            for a in range(b + 1):
                add(("gxx", a, b), times(x[a], gx))
    basis = [(v_ref, 0), (v_ref, 1), (uk_ref, 0), (uk_ref, 1)]
    pieces = [(s, c) for s in range(slots) for c in range(0, prows, PIECE)]

    def piece(ref, v, s, c, low=0, high=0):
        start, stop = max(c - low, 0), min(c + PIECE + high, prows)
        parts = cut(ref[v, s * prows + start : s * prows + stop, :])
        zero = [jnp.zeros((8, LANES), jnp.float32)]
        head, tail = zero * ((start - c + low) // 8), zero * ((c + PIECE + high - stop) // 8)
        return [jnp.concatenate([*head, p, *tail], axis=0) if head or tail else p for p in parts]

    for s, c in pieces:
        stress = [piece(stress_ref, j, s, c) for j in range(3)]
        first = []
        for b in range(4):
            held = piece(*basis[b], s, c, high=8)
            w = [p[:PIECE] for p in held]
            along_rows = [pltpu.roll(p, PIECE + 7, 0)[:PIECE] - q for p, q in zip(held, w)]
            along_cols = minus(col_after(w), w)
            first.append((along_rows, along_cols))
            fr, fc = membrane(along_rows, along_cols, stress)
            for a in range(b + 1):
                add(("guu", a, b), each(lambda p, x, q, y: p * x + q * y, first[a][0], fr, first[a][1], fc))
    for s, c in pieces:
        at = slice(s * prows + c, s * prows + c + PIECE)
        live = iota((PIECE, LANES), 0) < rows_ref[s] - c
        thick, support = cut(thick_ref[at, :]), cut(support_ref[at, :])
        live_thick = masked(live, thick_ref[at, :])
        bends = []
        for v in range(2):
            held = piece(v_ref, v, s, c, 8, 8)
            w = [p[8 : 8 + PIECE] for p in held]
            rows = [
                pltpu.roll(p, PIECE + 15, 0)[8 : 8 + PIECE] + pltpu.roll(p, 1, 0)[8 : 8 + PIECE] - (q + q)
                for p, q in zip(held, w)
            ]
            bends.append((w, rows, second_cols(w)))
        for b in range(2):
            w, rows, cols = bends[b]
            sw, tr, tc = times(support, w), times(live_thick, rows), times(thick, cols)
            for a in range(b + 1):
                add(
                    ("kuu", a, b),
                    each(lambda u, x, p, y, q, z: u * x + p * y + q * z, bends[a][0], sw, bends[a][1], tr, bends[a][2], tc),
                )
        for b in range(2):
            kuk = piece(kuk_ref, b, s, c)
            for a in range(2):
                add(("kuu", a, 2 + b), times(bends[a][0], kuk))
    for d in range(2):
        for at, v, s, side in stacked(rows_ref, prows):
            row = v_ref[v, pl.ds(edge_row(rows_ref, s, side, d, prows), 1), :]
            for h, part in enumerate(cut(row)):
                to = STACK * (d * halves + h) + at
                out_ref[to : to + 1, :] = part
        for h, part in enumerate(each(lambda u, z: u + z, rim_of(rim_ref, "uk", d), scaled[d])):
            to = STACK * ((2 + d) * halves + h)
            out_ref[to : to + STACK, :] = part
    tile = packed([column_sums(totals[name]) for name in NAMES])
    out_ref[4 * STACK * halves :, :] = jnp.where(iota(tile.shape, 1) == LANES - 1, label, tile)


def apply_kernel(rows_ref, thick_ref, support_ref, prec_ref, stress_ref, v_ref, kuk_ref, a_ref, c_ref, d_ref):
    slots = rows_ref.shape[0]
    rows_dev, ncol = thick_ref.shape
    prows = rows_dev // slots
    for s in range(slots):
        at = slice(s * prows, (s + 1) * prows)
        live = live_of(rows_ref, s, (prows, LANES))
        thick, support = cut(thick_ref[at, :]), cut(support_ref[at, :])
        live_thick = masked(live, thick_ref[at, :])
        prec = cut(prec_ref[at, :])
        stress = [cut(stress_ref[j, at, :]) for j in range(3)]
        for v in range(2):
            w = cut(v_ref[v, at, :])
            a_ref[v, at, :] = joined(each(lambda u, p, g: u + p * g, w, prec, geometric(w, stress)))
            c_ref[v, at, :] = joined(times(prec, stiffness(w, live_thick, thick, support)))
            d_ref[v, at, :] = joined(times(prec, cut(kuk_ref[v, at, :])))


def line_parts(ref):
    halves = (ref.shape[0] // STACK - 1) // 4
    tag = 4 * STACK * halves
    return ref[tag:, LANES - 1 :], [sent_stack(ref, kind, d, halves) for kind in range(2) for d in range(2)]


def line_kernel(near, *refs):
    line, out_ref = refs[:-2], refs[-1]
    held = [line_parts(ref) for ref in line]
    sums = [None] * 6
    for (label, stacks), others in zip(held, near):
        met = opposite(label, [held[k] for k in others])
        g, k = (meeting(stacks[2 * i : 2 * i + 2], met[2 * i : 2 * i + 2]) for i in range(2))
        g_turned, k_turned = [other_vector(w) for w in g], [other_vector(w) for w in k]
        for i, (p, q) in enumerate(((g, g), (g, g_turned), (g, k), (g, k_turned), (k, k), (k, k_turned))):
            part = each(
                lambda a, b, c, d: penalty_value * (a * b) + penalty_slope * (c * d), p[0], q[0], p[1], q[1]
            )
            part = sum(part[1:], part[0])
            sums[i] = part if sums[i] is None else sums[i] + part
    total = line[0][-STACK:, :]
    for ref in line[1:]:
        total = total + ref[-STACK:, :]
    row = iota(total.shape, 0)
    masks = [(row % 2 == 1) & (row // 2 % 2 == v) for v in range(2)]
    rows = {
        (0, 0): (0, 0), (1, 1): (0, 1), (0, 1): (1, 0), (0, 2): (2, 0), (1, 3): (2, 1), (0, 3): (3, 0), (1, 2): (3, 1),
        (2, 2): (4, 0), (3, 3): (4, 1), (2, 3): (5, 0),
    }
    out_ref[...] = total + packed([column_sums(jnp.where(masks[rows[p][1]], sums[rows[p][0]], 0.0)) for p in UU])


def join_kernel(near, rows_ref, prec_ref, stress_ref, uk_ref, c_in, d_in, *refs):
    line, (b_ref, c_ref, d_ref) = refs[:-4], refs[-3:]
    c_ref[...] = c_in[...]
    d_ref[...] = d_in[...]
    prows = c_in.shape[1] // 2
    for s in range(2):
        at = slice(s * prows, (s + 1) * prows)
        prec = cut(prec_ref[at, :])
        stress = [cut(stress_ref[j, at, :]) for j in range(3)]
        for v in range(2):
            uk = cut(uk_ref[v, at, :])
            gk = geometric(uk, stress)
            b_ref[v, at, :] = joined(each(lambda u, p, g: u + p * g, uk, prec, gk))
    label, stacks = line_parts(line[0])
    met = opposite(label, [line_parts(ref) for ref in line[1:]])
    for i, ref in enumerate((c_ref, d_ref)):
        added = interface_rows(stacks[2 * i : 2 * i + 2], met[2 * i : 2 * i + 2])
        for d in range(2):
            for at, v, s, side in stacked(rows_ref, prows):
                rows = pl.ds(edge_row(rows_ref, s, side, d, prows), 1)
                ref[v, rows, :] += prec_ref[rows, :] * joined([p[at : at + 1] for p in added[d]])


def form(table, left, right):
    total = None
    for i, c in left.items():
        row = None
        for j, d in right.items():
            term = d * table[i, j]
            row = term if row is None else row + term
        total = c * row if total is None else total + c * row
    return total


def final_kernel(cells, total_ref, a_ref, b_ref, c_ref, d_ref, out_ref, held, sems):
    rows_dev, ncol = a_ref.shape[1:]
    prows = rows_dev // 2
    total = total_ref[...]

    def value(*name):
        k = AT[name]
        return jnp.broadcast_to(total[k % 8 : k % 8 + 1, k // 8 : k // 8 + 1], (8, LANES))

    k_table, g_table = {}, {}
    for a, b in UU:
        k_table[a, b] = k_table[b, a] = value("kuu", a, b)
        g_table[a, b] = g_table[b, a] = value("guu", a, b)
    first_a, cross_k, second_a = (value("kxx", a, b) for a, b in XX)
    first_g, cross_g, second_g = (value("gxx", a, b) for a, b in XX)
    ratio = cross_k / first_a
    other_a = second_a - ratio * cross_k
    other_q = second_g - 2.0 * ratio * cross_g + ratio * ratio * first_g
    mu_first = first_g / first_a
    mu_other = other_q / other_a
    one = jnp.ones_like(ratio)
    new_first = {0: one, 2: -mu_first}
    new_second = {0: -ratio, 1: one, 2: mu_other * ratio, 3: -mu_other}
    a1 = form(k_table, new_first, new_first)
    c = form(k_table, new_first, new_second)
    a2 = form(k_table, new_second, new_second)
    g1 = form(g_table, new_first, new_first)
    h = form(g_table, new_first, new_second)
    g2 = form(g_table, new_second, new_second)
    r = c / a1
    b2 = a2 - r * c
    q2 = g2 - 2.0 * r * h + r * r * g1
    mus = [g1 / a1, q2 / b2]
    scales = [jnp.sqrt(norm_scale * cells / a1), jnp.sqrt(norm_scale * cells / b2)]
    lead = [
        {i: scales[0] * f for i, f in new_first.items()},
        {i: scales[1] * (f - r * new_first[i] if i in new_first else f) for i, f in new_second.items()},
    ]
    copies = []
    tall = (prows // 8, 8, LANES)
    for s in range(2):
        at = pl.ds(s * prows, prows)
        for v in range(2):
            for h in range(ncol // LANES):
                cols = pl.ds(h * LANES, LANES)
                acc = None
                for i in (0, 1):
                    if i in lead[v]:
                        f, g = lead[v][i], lead[v][2 + i]
                        parts = [ref[i, at, cols].reshape(tall) for ref in (a_ref, b_ref, c_ref, d_ref)]
                        term = f * parts[0] + g * parts[1]
                        term = term - ((mus[v] * f) * parts[2] + (mus[v] * g) * parts[3])
                        acc = term if acc is None else acc + term
                held[v, at, cols] = acc.reshape(prows, LANES)
            copies.append(pltpu.make_async_copy(held.at[v, at, :], out_ref.at[v, at, :], sems.at[2 * s + v]))
            copies[-1].start()
    for copy in copies:
        copy.wait()


def call(body, outs, kinds, scratch=(), flops=1_000_000, out_kind="v"):
    spaces = {"s": pltpu.SMEM, "v": pltpu.VMEM, "h": pltpu.HBM, "a": pl.ANY}
    return pl.pallas_call(
        body,
        out_shape=[pltpu.HBM(s, d) if out_kind == "h" else jax.ShapeDtypeStruct(s, d) for s, d in outs],
        in_specs=[pl.BlockSpec(memory_space=spaces[k]) for k in kinds],
        out_specs=[pl.BlockSpec(memory_space=spaces[out_kind]) for _ in outs],
        scratch_shapes=list(scratch),
        compiler_params=pltpu.CompilerParams(vmem_limit_bytes=32 * 1024 * 1024),
        cost_estimate=pl.CostEstimate(flops=flops, bytes_accessed=2_000_000, transcendentals=0),
    )


def per_device(vectors, prestress, thickness, foundation, patch_rows, matched, elem_row):
    owners = lax.axis_size("patch")
    inner = lax.axis_size(("sub", "half"))
    slots = patch_rows.shape[0]
    rows_dev, ncol = thickness.shape
    f32, bf16 = jnp.float32, jnp.bfloat16
    cells = float(owners * inner * rows_dev * ncol)
    field = ((2, rows_dev, ncol), f32)
    one = ((rows_dev, ncol), f32)
    sums = ((8 * len(FIRST), LANES), f32)
    tile = ((8, LANES), f32)

    width = 3 * ncol + LANES
    elem = pltpu.VMEM((1, rows_dev), jnp.int32)
    planes = jnp.transpose(prestress, (1, 0, 2))
    if rows_dev == 16 * owners * inner:
        tiles = 3 * (ncol // LANES)
        shape = (owners * inner, 16 * tiles + 8, LANES)
        planes = planes.reshape(3, owners * inner, 16, ncol)
        sems = [pltpu.SemaphoreType.DMA, pltpu.SemaphoreType.DMA((tiles,)), pltpu.SemaphoreType.DMA((tiles + 1,))]
        pack = pack_blocks_kernel
        scratch = [pltpu.VMEM(planes.shape, bf16), pltpu.VMEM((owners * inner, 8, LANES), bf16)]
    else:
        shape = (rows_dev, width)
        sems = [pltpu.SemaphoreType.DMA((5,))]
        pack = pack_rows_kernel
        scratch = [pltpu.VMEM(shape, bf16)]
    (payload,) = call(pack, [(shape, bf16)], "hh", [elem, *scratch, *sems], out_kind="h")(
        pltpu.with_memory_space_constraint(planes, pltpu.HBM),
        pltpu.with_memory_space_constraint(elem_row.reshape(1, rows_dev), pltpu.HBM),
    )
    arrived = lax.all_to_all(
        payload, ("patch", "sub", "half"), split_axis=0, concat_axis=0, tiled=True
    )
    halves = ncol // LANES
    (edges,) = call(edge_kernel, [(((2 * halves + 1) * STACK, LANES), f32)], "ssv")(patch_rows, matched, vectors)
    below, above = neighbours(edges, "patch")
    u_k, k_uk, prec, part, rim = call(
        stiff_kernel,
        [field, field, one, sums, ((RIM_STACKS * STACK, ncol), f32)],
        "svvv",
        [pltpu.VMEM(field[0], f32)],
    )(patch_rows, vectors, thickness, foundation)
    v, u_k, k_uk, stress, sent = call(
        gram_kernel,
        [field, field, field, ((3, rows_dev, ncol), f32), (((4 * halves + 1) * STACK, LANES), f32)],
        "svvvvvvvvvvvv",
    )(
        patch_rows, arrived, vectors, thickness, foundation, prec, u_k, k_uk, part, rim,
        edges, below, above,
    )
    line, near = line_shared(sent, "patch")
    a, c, d = call(apply_kernel, [field] * 3, "svvvvvv")(
        patch_rows, thickness, foundation, prec, stress, v, k_uk
    )
    (total,) = call(functools.partial(line_kernel, near), [tile], "v" * owners + "a")(*line, a)
    total = summed_over_both(total, "sub", "half")
    b, c, d = call(functools.partial(join_kernel, near), [field] * 3, "sv" + "v" * (len(near[0]) + 5) + "a")(
        patch_rows, prec, stress, u_k, c, d, line[0], *[line[k] for k in near[0]], line[2]
    )
    (modes,) = call(
        functools.partial(final_kernel, cells),
        [field],
        "vvvvv",
        [pltpu.VMEM(field[0], f32), pltpu.SemaphoreType.DMA((4,))],
        out_kind="h",
    )(total, a, b, c, d)
    return modes


def solution(mesh):
    in_specs = (
        P(None, ("groups", "patch", "sub", "half"), None),
        P(("groups", "patch", "sub", "half"), None, None),
        P(("groups", "patch", "sub", "half"), None),
        P(("groups", "patch", "sub", "half"), None),
        P(("groups", "patch", "sub", "half")),
        P(("groups", "patch", "sub", "half")),
        P(("groups", "patch", "sub", "half")),
    )
    out_specs = P(None, ("groups", "patch", "sub", "half"), None)
    return jax.shard_map(
        per_device, mesh=mesh, in_specs=in_specs, out_specs=out_specs, check_vma=False
    )
```

```python
import functools

import jax
import jax.numpy as jnp
from jax import lax
from jax.experimental import pallas as pl
from jax.experimental.pallas import tpu as pltpu
from jax.sharding import PartitionSpec as P

norm_scale = 16.0
penalty_value = 8.0
penalty_slope = 4.0
LANES = 128

UU = [(a, b) for a in range(4) for b in range(a, 4)]
XX = [(0, 0), (0, 1), (1, 1)]
NAMES = [(kind,) + pair for kind, pairs in (("kuu", UU), ("guu", UU), ("kxx", XX), ("gxx", XX)) for pair in pairs]
AT = {name: k for k, name in enumerate(NAMES)}


def passed_along(array, axis, by):
    peers = lax.axis_size(axis)
    return lax.ppermute(array, axis, [(i, (i + by) % peers) for i in range(peers)])


def neighbours(array, axis):
    if lax.axis_size(axis) == 4:
        return [lax.ppermute(array, axis, [(i, i ^ k) for i in range(4)]) for k in (1, 3)]
    return [passed_along(array, axis, 1), passed_along(array, axis, -1)]


def line_shared(array, axis):
    peers = lax.axis_size(axis)
    if peers == 4:
        shared = [lax.ppermute(array, axis, [(i, i ^ k) for i in range(4)]) for k in (3, 2, 1)]
        return [array] + shared[::-1], [(k ^ 1, k ^ 3) for k in range(4)]
    shared = [passed_along(array, axis, k) for k in range(1, peers)]
    return [array] + shared, [tuple(sorted({(k + 1) % peers, (k - 1) % peers})) for k in range(peers)]


def summed_over_both(array, outer, inner):
    across, within = lax.axis_size(outer), lax.axis_size(inner)
    shifts = [(o, i) for o in range(across) for i in range(within)]
    total = array
    for o, i in shifts[1:]:
        pairs = [
            (x * within + y, (x + o) % across * within + (y + i) % within) for x, y in shifts
        ]
        total = total + lax.ppermute(array, (outer, inner), pairs)
    return total


def iota(shape, axis):
    return lax.broadcasted_iota(jnp.int32, shape, axis)


def row_after(w):
    rows = w[0].shape[0]
    zero = jnp.zeros((8, LANES), jnp.float32)
    return [pltpu.roll(jnp.concatenate([p, zero], axis=0), rows + 7, 0)[:rows] for p in w]


def row_before(w):
    rows = w[0].shape[0]
    zero = jnp.zeros((8, LANES), jnp.float32)
    return [pltpu.roll(jnp.concatenate([p, zero], axis=0), 1, 0)[:rows] for p in w]


def col_after(w):
    at_end = iota(w[0].shape, 1) == LANES - 1
    turned = [pltpu.roll(p, LANES - 1, 1) for p in w]
    return [jnp.where(at_end, n, p) for p, n in zip(turned, turned[1:] + [0.0])]


def col_before(w):
    at_start = iota(w[0].shape, 1) == 0
    turned = [pltpu.roll(p, 1, 1) for p in w]
    return [jnp.where(at_start, n, p) for p, n in zip(turned, [0.0] + turned[:-1])]


def each(f, *fields):
    return [f(*parts) for parts in zip(*fields)]


def minus(u, w):
    return each(lambda a, b: a - b, u, w)


def times(u, w):
    return each(lambda a, b: a * b, u, w)


def second_rows(w):
    return each(lambda a, b, c: a + b - (c + c), row_before(w), row_after(w), w)


def second_cols(w):
    return each(lambda a, b, c: a + b - (c + c), col_before(w), col_after(w), w)


def stiffness(w, live_thick, thick, support):
    bend_rows = times(live_thick, second_rows(w))
    bend_cols = times(thick, second_cols(w))
    return each(
        lambda f, a, r, c: f * a + (r + c), support, w, second_rows(bend_rows), second_cols(bend_cols)
    )


def differences(w):
    return minus(row_after(w), w), minus(col_after(w), w)


def membrane(along_rows, along_cols, stress):
    nuu, nvv, nuv = stress
    rows = each(lambda n, r, m, c: n * r + m * c, nuu, along_rows, nuv, along_cols)
    cols = each(lambda n, c, m, r: n * c + m * r, nvv, along_cols, nuv, along_rows)
    return rows, cols


def geometric(w, stress):
    rows, cols = membrane(*differences(w), stress)
    return each(
        lambda rb, r, cb, c: (rb - r) + (cb - c), row_before(rows), rows, col_before(cols), cols
    )


def cut(value):
    return [value[:, h * LANES : (h + 1) * LANES] for h in range(value.shape[1] // LANES)]


def joined(w):
    return jnp.concatenate(w, axis=1)


def live_of(rows_ref, slot, shape):
    return iota(shape, 0) < rows_ref[slot]


def masked(live, value):
    return [jnp.where(live, p, 0.0) for p in cut(value)]


def column_sums(product):
    return jnp.sum(product, axis=0, keepdims=True)


def folded(w):
    total = sum(w[1:], w[0])
    return jnp.sum(total.reshape(total.shape[0] // 8, 8, LANES), axis=0)


def packed(rows):
    rows = list(rows)
    rows += [jnp.zeros_like(rows[0])] * (-len(rows) % 8)
    lane = iota((8, LANES), 1)
    out = jnp.zeros((8, LANES), jnp.float32)
    for tile in range(len(rows) // 8):
        total = jnp.sum(jnp.concatenate(rows[8 * tile : 8 * tile + 8], axis=0), axis=1, keepdims=True)
        out = jnp.where(lane == tile, total, out)
    return out


def place(rows_ref, matched_ref, slots):
    inner = lax.axis_size(("sub", "half"))
    mine = [lax.axis_index("patch") * slots + s for s in range(slots)]
    match = [
        matched_ref[s] // (inner * slots) * slots + lax.rem(matched_ref[s], slots) for s in range(slots)
    ]
    return mine, match


STACK = 8


def edge_row(rows_ref, slot, side, depth, prows):
    return slot * prows + (rows_ref[slot] - 1 - depth if side else depth)


def stacked(rows_ref, prows):
    return [(4 * s + 2 * v + side, v, s, side) for s in range(2) for v in range(2) for side in range(2)]


def labels_of(rows_ref, matched_ref):
    mine, match = place(rows_ref, matched_ref, 2)
    row = iota((STACK, LANES), 0)
    label = jnp.full((STACK, LANES), 0, jnp.int32)
    for s in range(2):
        for side, number in enumerate((mine[s], match[s])):
            label = jnp.where((row // 4 == s) & (row % 2 == side), number, label)
    return label.astype(jnp.float32)


def other_side(stack):
    row = iota(stack.shape, 0)
    return jnp.where(row % 2 == 0, pltpu.roll(stack, STACK - 1, 0), pltpu.roll(stack, 1, 0))


def other_vector(w):
    row = iota(w[0].shape, 0)
    return [jnp.where(row // 2 % 2 == 0, pltpu.roll(p, STACK - 2, 0), pltpu.roll(p, 2, 0)) for p in w]


def opposite(label, near):
    found = None
    for labels, stacks in near:
        turned, parts = other_side(labels), [[other_side(p) for p in w] for w in stacks]
        for shift in (0, 4):
            if shift:
                turned, parts = pltpu.roll(turned, 4, 0), [[pltpu.roll(p, 4, 0) for p in w] for w in parts]
            here = turned == label
            picked = [[jnp.where(here, p, 0.0) for p in w] for w in parts]
            found = picked if found is None else [each(lambda x, y: x + y, f, p) for f, p in zip(found, picked)]
    return found


def meeting(own, met):
    jump = minus(own[0], met[0])
    slope = each(lambda a, b, c, d: (a + b) - (c + d), own[0], met[0], own[1], met[1])
    return jump, slope


def interface_rows(own, met):
    jump, slope = meeting(own, met)
    return (
        each(lambda j, m: penalty_value * j + penalty_slope * m, jump, slope),
        [-penalty_slope * m for m in slope],
    )


def local_rows(elem_ref, rows_dev):
    square = (rows_dev, rows_dev)
    if rows_dev & (rows_dev - 1) == 0:
        local = jnp.bitwise_and(elem_ref[...], rows_dev - 1)
    else:
        local = lax.rem(elem_ref[...], rows_dev)
    spread = jnp.broadcast_to(local.astype(jnp.float32), square)
    return jnp.sum(jnp.where(iota(square, 0) == iota(square, 1), spread, 0.0), axis=1, keepdims=True)


def pack_rows_kernel(stress_ref, elem_ref, pay_ref, elem, held, sems):
    rows_dev, ncol = stress_ref.shape[1:]
    get = pltpu.make_async_copy(elem_ref, elem, sems.at[0])
    get.start()
    planes = [
        pltpu.make_async_copy(stress_ref.at[j], held.at[:, pl.ds(j * ncol, ncol)], sems.at[1 + j])
        for j in range(3)
    ]
    for copy in planes:
        copy.start()
    get.wait()
    column = local_rows(elem, rows_dev)
    held[:, 3 * ncol :] = jnp.broadcast_to(column, (rows_dev, LANES)).astype(jnp.bfloat16)
    for copy in planes:
        copy.wait()
    put = pltpu.make_async_copy(held, pay_ref, sems.at[4])
    put.start()
    put.wait()


LABEL_LANE = 32


def neighbour_labels(arrived_ref, back, halves):
    me, peers, inner = lax.axis_index("patch"), lax.axis_size("patch"), lax.axis_size(("sub", "half"))
    there = jnp.bitwise_xor(me, back) if peers == 4 else lax.rem(me - back + peers, peers)
    block = there * inner + lax.axis_index(("sub", "half"))
    return arrived_ref[block, 48 * halves :, :].astype(jnp.float32)[:, LABEL_LANE : LABEL_LANE + 1]


def pack_blocks_kernel(stress_ref, elem_ref, matched_ref, pay_ref, elem, planes, held, match, get_sem, in_sems, out_sems):
    blocks, ncol = held.shape[0], stress_ref.shape[3]
    halves = ncol // LANES
    get = pltpu.make_async_copy(elem_ref, elem, get_sem)
    get.start()
    ask = pltpu.make_async_copy(matched_ref, match, out_sems.at[0])
    ask.start()
    fetch = [pltpu.make_async_copy(stress_ref.at[j], planes.at[j], in_sems.at[j]) for j in range(3)]
    for copy in fetch:
        copy.start()
    put = []
    get.wait()
    column = jnp.broadcast_to(local_rows(elem, 16 * blocks), (16 * blocks, LANES))
    ask.wait()
    labels = labels_of(None, match)
    lane = iota((8, LANES), 1)
    for k in range(blocks):
        both = jnp.where(lane < LANES // 2, column[16 * k : 16 * k + 8], column[16 * k + 8 : 16 * k + 16])
        held[k] = jnp.where(lane == LABEL_LANE, labels, both).astype(jnp.bfloat16)
    put.append(pltpu.make_async_copy(held, pay_ref.at[:, pl.ds(48 * halves, 8), :], out_sems.at[3 * halves]))
    put[0].start()
    for t in range(3 * halves):
        if t % halves == 0:
            fetch[t // halves].wait()
        source = planes.at[t // halves, :, :, pl.ds(t % halves * LANES, LANES)]
        put.append(pltpu.make_async_copy(source, pay_ref.at[:, pl.ds(16 * t, 16), :], out_sems.at[t]))
        put[-1].start()
    for copy in put:
        copy.wait()


def unpacked(arrived_ref, ncol):
    if len(arrived_ref.shape) == 2:
        return arrived_ref[:, : 3 * ncol], arrived_ref[:, 3 * ncol :].astype(jnp.float32)
    blocks, halves = arrived_ref.shape[0], ncol // LANES
    forces = jnp.concatenate(
        [
            jnp.concatenate([arrived_ref[k, 16 * t : 16 * t + 16, :] for k in range(blocks)], axis=0)
            for t in range(3 * halves)
        ],
        axis=1,
    )
    tiles = [arrived_ref[k, 48 * halves :, :].astype(jnp.float32) for k in range(blocks)]
    half = LANES // 2
    column = jnp.concatenate([t[:, at : at + 1] for t in tiles for at in (0, half)], axis=0)
    return forces, jnp.broadcast_to(column, (16 * blocks, LANES))


def edge_kernel(rows_ref, matched_ref, vec_ref, edge_ref):
    rows_dev, ncol = vec_ref.shape[1:]
    halves = ncol // LANES
    for depth in range(2):
        for at, v, s, side in stacked(rows_ref, rows_dev // 2):
            row = vec_ref[v, pl.ds(edge_row(rows_ref, s, side, depth, rows_dev // 2), 1), :]
            for h, part in enumerate(cut(row)):
                to = STACK * (depth * halves + h) + at
                edge_ref[to : to + 1, :] = part
    edge_ref[2 * STACK * halves :, :] = labels_of(rows_ref, matched_ref)


FIRST = [("kxx", 0, 0), ("kxx", 0, 1), ("kxx", 1, 1), ("kuu", 2, 2), ("kuu", 2, 3), ("kuu", 3, 3)]


RIM = [("prec", 2), ("thick", 3), ("support", 2), ("uk", 2), ("kuk", 2)]
RIM_AT = {name: sum(n for _, n in RIM[:i]) for i, (name, _) in enumerate(RIM)}
RIM_STACKS = sum(n for _, n in RIM)


def stiff_kernel(rows_ref, vec_ref, thick_ref, support_ref, uk_ref, kuk_ref, prec_ref, sums_ref, rim_ref, k_ref):
    slots = rows_ref.shape[0]
    rows_dev, ncol = thick_ref.shape
    prows = rows_dev // slots
    totals = {}
    for s in range(slots):
        at = slice(s * prows, (s + 1) * prows)
        live = live_of(rows_ref, s, (prows, LANES))
        thick, support = cut(thick_ref[at, :]), cut(support_ref[at, :])
        live_thick = masked(live, thick_ref[at, :])
        prec = each(lambda f, t: jnp.where(live, 1.0 / (f + 12.0 * t), 0.0), support, thick)
        prec_ref[at, :] = joined(prec)
        for v in range(2):
            kw = stiffness(masked(live, vec_ref[v, at, :]), live_thick, thick, support)
            k_ref[v, at, :] = joined(kw)
            uk_ref[v, at, :] = joined(times(prec, kw))
        for v in range(2):
            kuk_ref[v, at, :] = joined(stiffness(cut(uk_ref[v, at, :]), live_thick, thick, support))
        for a in range(2):
            wa = masked(live, vec_ref[a, at, :])
            for b in range(a, 2):
                for name, product in (
                    (("kxx", a, b), times(wa, cut(k_ref[b, at, :]))),
                    (("kuu", 2 + a, 2 + b), times(cut(uk_ref[a, at, :]), cut(kuk_ref[b, at, :]))),
                ):
                    part = folded(product)
                    totals[name] = totals[name] + part if s else part
    for k, name in enumerate(FIRST):
        sums_ref[8 * k : 8 * k + 8, :] = totals[name]
    sources = {"prec": prec_ref, "thick": thick_ref, "support": support_ref, "uk": uk_ref, "kuk": kuk_ref}
    for name, depths in RIM:
        for depth in range(depths):
            for at, v, s, side in stacked(rows_ref, prows):
                rows = pl.ds(edge_row(rows_ref, s, side, depth, prows), 1)
                to = STACK * (RIM_AT[name] + depth) + at
                ref = sources[name]
                rim_ref[to : to + 1, :] = ref[rows, :] if len(ref.shape) == 2 else ref[v, rows, :]


def rim_of(rim_ref, name, depth):
    at = STACK * (RIM_AT[name] + depth)
    return cut(rim_ref[at : at + STACK, :])


def sent_stack(ref, kind, depth, halves):
    at = (2 * kind + depth) * halves
    return [ref[STACK * (at + h) : STACK * (at + h + 1), :] for h in range(halves)]


PIECE = 16


def gram_kernel(
    rows_ref, arrived_ref, vec_ref, thick_ref, support_ref, prec_ref, uk_in, kuk_in, sums_in, rim_ref,
    edge_ref, below_ref, above_ref, v_ref, uk_ref, kuk_ref, stress_ref, out_ref,
):
    slots = rows_ref.shape[0]
    rows_dev, ncol = prec_ref.shape
    prows = rows_dev // slots
    halves = ncol // LANES
    forces, index = unpacked(arrived_ref, ncol)
    lane = iota(index.shape, 1).astype(jnp.float32)
    pick = jnp.concatenate(
        [
            jnp.where(index == lane + float(h * LANES), 1.0, 0.0).astype(jnp.bfloat16)
            for h in range(rows_dev // LANES)
        ],
        axis=1,
    )
    placed = lax.dot_general(
        pick, forces, (((0,), (0,)), ((), ())), preferred_element_type=jnp.float32
    )
    for j in range(3):
        stress_ref[j] = placed[:, j * ncol : (j + 1) * ncol]
    totals = {name: sums_in[8 * k : 8 * k + 8, :] for k, name in enumerate(FIRST)}

    def add(name, product):
        part = folded(product)
        totals[name] = totals[name] + part if name in totals else part

    def add_stack(first, second, product):
        part = sum(product[1:], product[0])
        vector = iota(part.shape, 0) // 2 % 2
        totals[first] = totals[first] + jnp.where(vector == 0, part, 0.0)
        if second is not None:
            totals[second] = totals[second] + jnp.where(vector == 1, part, 0.0)

    uk_ref[...] = uk_in[...]
    kuk_ref[...] = kuk_in[...]
    label = edge_ref[2 * STACK * halves :, :]

    def depths_of(ref):
        return [[ref[STACK * (d * halves + h) : STACK * (d * halves + h + 1), :] for h in range(halves)] for d in range(2)]

    own = depths_of(edge_ref)
    if len(arrived_ref.shape) == 2:
        labels = [ref[2 * STACK * halves :, :] for ref in (below_ref, above_ref)]
    else:
        backs = (1, 3) if lax.axis_size("patch") == 4 else (1, -1)
        labels = [neighbour_labels(arrived_ref, back, halves) for back in backs]
    met = opposite(label, [(near, depths_of(ref)) for near, ref in zip(labels, (below_ref, above_ref))])
    added = interface_rows(own, met)
    scaled = [times(rim_of(rim_ref, "prec", d), added[d]) for d in range(2)]
    bend = [
        each(lambda t, y, x: t * (y - (x + x)), rim_of(rim_ref, "thick", 0), scaled[1], scaled[0]),
        each(lambda t, y, x: t * (y - (x + x)), rim_of(rim_ref, "thick", 1), scaled[0], scaled[1]),
        times(rim_of(rim_ref, "thick", 2), scaled[1]),
    ]
    across = [second_cols(times(rim_of(rim_ref, "thick", d), second_cols(scaled[d]))) for d in range(2)]
    extra = [
        each(
            lambda f, z, p, q, c: f * z + (p - (q + q)) + c,
            rim_of(rim_ref, "support", 0), scaled[0], bend[1], bend[0], across[0],
        ),
        each(
            lambda f, z, p, q, r, c: f * z + (p - (q + q) + r) + c,
            rim_of(rim_ref, "support", 1), scaled[1], bend[0], bend[1], bend[2], across[1],
        ),
        each(lambda p, q: p - (q + q), bend[1], bend[2]),
        bend[2],
    ]
    for d in range(2):
        n, z, e, x = added[d], scaled[d], extra[d], own[d]
        kuk = rim_of(rim_ref, "kuk", d)
        add_stack(("kxx", 0, 0), ("kxx", 1, 1), times(x, n))
        add_stack(("kxx", 0, 1), None, times(x, other_vector(n)))
        add_stack(("kuu", 2, 2), ("kuu", 3, 3), each(lambda r, p, q: r * (p + p + q), z, kuk, e))
        turned, z_turned = other_vector(each(lambda p, q: p + q, kuk, e)), other_vector(z)
        add_stack(("kuu", 2, 3), None, each(lambda r, t, p, w: r * t + p * w, z, turned, kuk, z_turned))
    for d in range(4):
        for at, v, s, side in stacked(rows_ref, prows):
            rows = pl.ds(edge_row(rows_ref, s, side, d, prows), 1)
            kuk_ref[v, rows, :] += joined([p[at : at + 1] for p in extra[d]])
            if d < 2:
                uk_ref[v, rows, :] += joined([p[at : at + 1] for p in scaled[d]])
    for s in range(slots):
        at = slice(s * prows, (s + 1) * prows)
        live = live_of(rows_ref, s, (prows, LANES))
        stress = [cut(stress_ref[j, at, :]) for j in range(3)]
        prec = cut(prec_ref[at, :])
        x = [masked(live, vec_ref[v, at, :]) for v in range(2)]
        for b in range(2):
            gx = geometric(x[b], stress)
            v_ref[b, at, :] = joined(each(lambda w, p, g: w + p * g, x[b], prec, gx))
            for a in range(b + 1):
                add(("gxx", a, b), times(x[a], gx))
    basis = [(v_ref, 0), (v_ref, 1), (uk_ref, 0), (uk_ref, 1)]
    pieces = [(s, c) for s in range(slots) for c in range(0, prows, PIECE)]

    def piece(ref, v, s, c, low=0, high=0):
        start, stop = max(c - low, 0), min(c + PIECE + high, prows)
        parts = cut(ref[v, s * prows + start : s * prows + stop, :])
        zero = [jnp.zeros((8, LANES), jnp.float32)]
        head, tail = zero * ((start - c + low) // 8), zero * ((c + PIECE + high - stop) // 8)
        return [jnp.concatenate([*head, p, *tail], axis=0) if head or tail else p for p in parts]

    for s, c in pieces:
        stress = [piece(stress_ref, j, s, c) for j in range(3)]
        first = []
        for b in range(4):
            held = piece(*basis[b], s, c, high=8)
            w = [p[:PIECE] for p in held]
            along_rows = [pltpu.roll(p, PIECE + 7, 0)[:PIECE] - q for p, q in zip(held, w)]
            along_cols = minus(col_after(w), w)
            first.append((along_rows, along_cols))
            fr, fc = membrane(along_rows, along_cols, stress)
            for a in range(b + 1):
                add(("guu", a, b), each(lambda p, x, q, y: p * x + q * y, first[a][0], fr, first[a][1], fc))
    for s, c in pieces:
        at = slice(s * prows + c, s * prows + c + PIECE)
        live = iota((PIECE, LANES), 0) < rows_ref[s] - c
        thick, support = cut(thick_ref[at, :]), cut(support_ref[at, :])
        live_thick = masked(live, thick_ref[at, :])
        bends = []
        for v in range(2):
            held = piece(v_ref, v, s, c, 8, 8)
            w = [p[8 : 8 + PIECE] for p in held]
            rows = [
                pltpu.roll(p, PIECE + 15, 0)[8 : 8 + PIECE] + pltpu.roll(p, 1, 0)[8 : 8 + PIECE] - (q + q)
                for p, q in zip(held, w)
            ]
            bends.append((w, rows, second_cols(w)))
        for b in range(2):
            w, rows, cols = bends[b]
            sw, tr, tc = times(support, w), times(live_thick, rows), times(thick, cols)
            for a in range(b + 1):
                add(
                    ("kuu", a, b),
                    each(lambda u, x, p, y, q, z: u * x + p * y + q * z, bends[a][0], sw, bends[a][1], tr, bends[a][2], tc),
                )
        for b in range(2):
            kuk = piece(kuk_ref, b, s, c)
            for a in range(2):
                add(("kuu", a, 2 + b), times(bends[a][0], kuk))
    for d in range(2):
        for at, v, s, side in stacked(rows_ref, prows):
            row = v_ref[v, pl.ds(edge_row(rows_ref, s, side, d, prows), 1), :]
            for h, part in enumerate(cut(row)):
                to = STACK * (d * halves + h) + at
                out_ref[to : to + 1, :] = part
        for h, part in enumerate(each(lambda u, z: u + z, rim_of(rim_ref, "uk", d), scaled[d])):
            to = STACK * ((2 + d) * halves + h)
            out_ref[to : to + STACK, :] = part
    tile = packed([column_sums(totals[name]) for name in NAMES])
    out_ref[4 * STACK * halves :, :] = jnp.where(iota(tile.shape, 1) == LANES - 1, label, tile)


def apply_kernel(rows_ref, thick_ref, support_ref, prec_ref, stress_ref, v_ref, kuk_ref, a_ref, c_ref, d_ref):
    slots = rows_ref.shape[0]
    rows_dev, ncol = thick_ref.shape
    prows = rows_dev // slots
    for s in range(slots):
        at = slice(s * prows, (s + 1) * prows)
        live = live_of(rows_ref, s, (prows, LANES))
        thick, support = cut(thick_ref[at, :]), cut(support_ref[at, :])
        live_thick = masked(live, thick_ref[at, :])
        prec = cut(prec_ref[at, :])
        stress = [cut(stress_ref[j, at, :]) for j in range(3)]
        for v in range(2):
            w = cut(v_ref[v, at, :])
            a_ref[v, at, :] = joined(each(lambda u, p, g: u + p * g, w, prec, geometric(w, stress)))
            c_ref[v, at, :] = joined(times(prec, stiffness(w, live_thick, thick, support)))
            d_ref[v, at, :] = joined(times(prec, cut(kuk_ref[v, at, :])))


def line_parts(ref):
    halves = (ref.shape[0] // STACK - 1) // 4
    tag = 4 * STACK * halves
    return ref[tag:, LANES - 1 :], [sent_stack(ref, kind, d, halves) for kind in range(2) for d in range(2)]


def line_kernel(near, *refs):
    line, out_ref = refs[:-2], refs[-1]
    held = [line_parts(ref) for ref in line]
    sums = [None] * 6
    for (label, stacks), others in zip(held, near):
        met = opposite(label, [held[k] for k in others])
        g, k = (meeting(stacks[2 * i : 2 * i + 2], met[2 * i : 2 * i + 2]) for i in range(2))
        g_turned, k_turned = [other_vector(w) for w in g], [other_vector(w) for w in k]
        for i, (p, q) in enumerate(((g, g), (g, g_turned), (g, k), (g, k_turned), (k, k), (k, k_turned))):
            part = each(
                lambda a, b, c, d: penalty_value * (a * b) + penalty_slope * (c * d), p[0], q[0], p[1], q[1]
            )
            part = sum(part[1:], part[0])
            sums[i] = part if sums[i] is None else sums[i] + part
    total = line[0][-STACK:, :]
    for ref in line[1:]:
        total = total + ref[-STACK:, :]
    row = iota(total.shape, 0)
    masks = [(row % 2 == 1) & (row // 2 % 2 == v) for v in range(2)]
    rows = {
        (0, 0): (0, 0), (1, 1): (0, 1), (0, 1): (1, 0), (0, 2): (2, 0), (1, 3): (2, 1), (0, 3): (3, 0), (1, 2): (3, 1),
        (2, 2): (4, 0), (3, 3): (4, 1), (2, 3): (5, 0),
    }
    out_ref[...] = total + packed([column_sums(jnp.where(masks[rows[p][1]], sums[rows[p][0]], 0.0)) for p in UU])


def join_kernel(near, rows_ref, prec_ref, stress_ref, uk_ref, c_in, d_in, *refs):
    line, (b_ref, c_ref, d_ref) = refs[:-4], refs[-3:]
    c_ref[...] = c_in[...]
    d_ref[...] = d_in[...]
    prows = c_in.shape[1] // 2
    for s in range(2):
        at = slice(s * prows, (s + 1) * prows)
        prec = cut(prec_ref[at, :])
        stress = [cut(stress_ref[j, at, :]) for j in range(3)]
        for v in range(2):
            uk = cut(uk_ref[v, at, :])
            gk = geometric(uk, stress)
            b_ref[v, at, :] = joined(each(lambda u, p, g: u + p * g, uk, prec, gk))
    label, stacks = line_parts(line[0])
    met = opposite(label, [line_parts(ref) for ref in line[1:]])
    for i, ref in enumerate((c_ref, d_ref)):
        added = interface_rows(stacks[2 * i : 2 * i + 2], met[2 * i : 2 * i + 2])
        for d in range(2):
            for at, v, s, side in stacked(rows_ref, prows):
                rows = pl.ds(edge_row(rows_ref, s, side, d, prows), 1)
                ref[v, rows, :] += prec_ref[rows, :] * joined([p[at : at + 1] for p in added[d]])


def form(table, left, right):
    total = None
    for i, c in left.items():
        row = None
        for j, d in right.items():
            term = d * table[i, j]
            row = term if row is None else row + term
        total = c * row if total is None else total + c * row
    return total


def final_kernel(cells, total_ref, a_ref, b_ref, c_ref, d_ref, out_ref, held, sems):
    rows_dev, ncol = a_ref.shape[1:]
    prows = rows_dev // 2
    total = total_ref[...]

    def value(*name):
        k = AT[name]
        return jnp.broadcast_to(total[k % 8 : k % 8 + 1, k // 8 : k // 8 + 1], (8, LANES))

    k_table, g_table = {}, {}
    for a, b in UU:
        k_table[a, b] = k_table[b, a] = value("kuu", a, b)
        g_table[a, b] = g_table[b, a] = value("guu", a, b)
    first_a, cross_k, second_a = (value("kxx", a, b) for a, b in XX)
    first_g, cross_g, second_g = (value("gxx", a, b) for a, b in XX)
    ratio = cross_k / first_a
    other_a = second_a - ratio * cross_k
    other_q = second_g - 2.0 * ratio * cross_g + ratio * ratio * first_g
    mu_first = first_g / first_a
    mu_other = other_q / other_a
    one = jnp.ones_like(ratio)
    new_first = {0: one, 2: -mu_first}
    new_second = {0: -ratio, 1: one, 2: mu_other * ratio, 3: -mu_other}
    a1 = form(k_table, new_first, new_first)
    c = form(k_table, new_first, new_second)
    a2 = form(k_table, new_second, new_second)
    g1 = form(g_table, new_first, new_first)
    h = form(g_table, new_first, new_second)
    g2 = form(g_table, new_second, new_second)
    r = c / a1
    b2 = a2 - r * c
    q2 = g2 - 2.0 * r * h + r * r * g1
    mus = [g1 / a1, q2 / b2]
    scales = [jnp.sqrt(norm_scale * cells / a1), jnp.sqrt(norm_scale * cells / b2)]
    lead = [
        {i: scales[0] * f for i, f in new_first.items()},
        {i: scales[1] * (f - r * new_first[i] if i in new_first else f) for i, f in new_second.items()},
    ]
    copies = []
    tall = (prows // 8, 8, LANES)
    for s in range(2):
        at = pl.ds(s * prows, prows)
        for v in range(2):
            for h in range(ncol // LANES):
                cols = pl.ds(h * LANES, LANES)
                acc = None
                for i in (0, 1):
                    if i in lead[v]:
                        f, g = lead[v][i], lead[v][2 + i]
                        parts = [ref[i, at, cols].reshape(tall) for ref in (a_ref, b_ref, c_ref, d_ref)]
                        term = f * parts[0] + g * parts[1]
                        term = term - ((mus[v] * f) * parts[2] + (mus[v] * g) * parts[3])
                        acc = term if acc is None else acc + term
                held[v, at, cols] = acc.reshape(prows, LANES)
            copies.append(pltpu.make_async_copy(held.at[v, at, :], out_ref.at[v, at, :], sems.at[2 * s + v]))
            copies[-1].start()
    for copy in copies:
        copy.wait()


def call(body, outs, kinds, scratch=(), flops=1_000_000, out_kind="v"):
    spaces = {"s": pltpu.SMEM, "v": pltpu.VMEM, "h": pltpu.HBM, "a": pl.ANY}
    return pl.pallas_call(
        body,
        out_shape=[pltpu.HBM(s, d) if out_kind == "h" else jax.ShapeDtypeStruct(s, d) for s, d in outs],
        in_specs=[pl.BlockSpec(memory_space=spaces[k]) for k in kinds],
        out_specs=[pl.BlockSpec(memory_space=spaces[out_kind]) for _ in outs],
        scratch_shapes=list(scratch),
        compiler_params=pltpu.CompilerParams(vmem_limit_bytes=32 * 1024 * 1024),
        cost_estimate=pl.CostEstimate(flops=flops, bytes_accessed=2_000_000, transcendentals=0),
    )


def per_device(vectors, prestress, thickness, foundation, patch_rows, matched, elem_row):
    owners = lax.axis_size("patch")
    inner = lax.axis_size(("sub", "half"))
    slots = patch_rows.shape[0]
    rows_dev, ncol = thickness.shape
    f32, bf16 = jnp.float32, jnp.bfloat16
    cells = float(owners * inner * rows_dev * ncol)
    field = ((2, rows_dev, ncol), f32)
    one = ((rows_dev, ncol), f32)
    sums = ((8 * len(FIRST), LANES), f32)
    tile = ((8, LANES), f32)

    width = 3 * ncol + LANES
    elem = pltpu.VMEM((1, rows_dev), jnp.int32)
    planes = jnp.transpose(prestress, (1, 0, 2))
    if rows_dev == 16 * owners * inner:
        tiles = 3 * (ncol // LANES)
        shape = (owners * inner, 16 * tiles + 8, LANES)
        planes = planes.reshape(3, owners * inner, 16, ncol)
        sems = [pltpu.SemaphoreType.DMA, pltpu.SemaphoreType.DMA((tiles,)), pltpu.SemaphoreType.DMA((tiles + 1,))]
        pack = pack_blocks_kernel
        scratch = [pltpu.VMEM(planes.shape, bf16), pltpu.VMEM((owners * inner, 8, LANES), bf16), pltpu.SMEM(matched.shape, jnp.int32)]
        extra = [pltpu.with_memory_space_constraint(matched, pltpu.HBM)]
    else:
        shape = (rows_dev, width)
        sems = [pltpu.SemaphoreType.DMA((5,))]
        pack = pack_rows_kernel
        scratch, extra = [pltpu.VMEM(shape, bf16)], []
    (payload,) = call(pack, [(shape, bf16)], "h" * (2 + len(extra)), [elem, *scratch, *sems], out_kind="h")(
        pltpu.with_memory_space_constraint(planes, pltpu.HBM),
        pltpu.with_memory_space_constraint(elem_row.reshape(1, rows_dev), pltpu.HBM),
        *extra,
    )
    arrived = lax.all_to_all(
        payload, ("patch", "sub", "half"), split_axis=0, concat_axis=0, tiled=True
    )
    halves = ncol // LANES
    (edges,) = call(edge_kernel, [(((2 * halves + 1) * STACK, LANES), f32)], "ssv")(patch_rows, matched, vectors)
    below, above = neighbours(edges[: 2 * STACK * halves] if extra else edges, "patch")
    u_k, k_uk, prec, part, rim = call(
        stiff_kernel,
        [field, field, one, sums, ((RIM_STACKS * STACK, ncol), f32)],
        "svvv",
        [pltpu.VMEM(field[0], f32)],
    )(patch_rows, vectors, thickness, foundation)
    v, u_k, k_uk, stress, sent = call(
        gram_kernel,
        [field, field, field, ((3, rows_dev, ncol), f32), (((4 * halves + 1) * STACK, LANES), f32)],
        "svvvvvvvvvvvv",
    )(
        patch_rows, arrived, vectors, thickness, foundation, prec, u_k, k_uk, part, rim,
        edges, below, above,
    )
    line, near = line_shared(sent, "patch")
    a, c, d = call(apply_kernel, [field] * 3, "svvvvvv")(
        patch_rows, thickness, foundation, prec, stress, v, k_uk
    )
    (total,) = call(functools.partial(line_kernel, near), [tile], "v" * owners + "a")(*line, a)
    total = summed_over_both(total, "sub", "half")
    b, c, d = call(functools.partial(join_kernel, near), [field] * 3, "sv" + "v" * (len(near[0]) + 5) + "a")(
        patch_rows, prec, stress, u_k, c, d, line[0], *[line[k] for k in near[0]], line[2]
    )
    (modes,) = call(
        functools.partial(final_kernel, cells),
        [field],
        "vvvvv",
        [pltpu.VMEM(field[0], f32), pltpu.SemaphoreType.DMA((4,))],
        out_kind="h",
    )(total, a, b, c, d)
    return modes


def solution(mesh):
    in_specs = (
        P(None, ("groups", "patch", "sub", "half"), None),
        P(("groups", "patch", "sub", "half"), None, None),
        P(("groups", "patch", "sub", "half"), None),
        P(("groups", "patch", "sub", "half"), None),
        P(("groups", "patch", "sub", "half")),
        P(("groups", "patch", "sub", "half")),
        P(("groups", "patch", "sub", "half")),
    )
    out_specs = P(None, ("groups", "patch", "sub", "half"), None)
    return jax.shard_map(
        per_device, mesh=mesh, in_specs=in_specs, out_specs=out_specs, check_vma=False
    )
```

```python
import functools

import jax
import jax.numpy as jnp
from jax import lax
from jax.experimental import pallas as pl
from jax.experimental.pallas import tpu as pltpu
from jax.sharding import PartitionSpec as P

norm_scale = 16.0
penalty_value = 8.0
penalty_slope = 4.0
LANES = 128

UU = [(a, b) for a in range(4) for b in range(a, 4)]
XX = [(0, 0), (0, 1), (1, 1)]
NAMES = [(kind,) + pair for kind, pairs in (("kuu", UU), ("guu", UU), ("kxx", XX), ("gxx", XX)) for pair in pairs]
AT = {name: k for k, name in enumerate(NAMES)}


def passed_along(array, axis, by):
    peers = lax.axis_size(axis)
    return lax.ppermute(array, axis, [(i, (i + by) % peers) for i in range(peers)])


def neighbours(array, axis):
    if lax.axis_size(axis) == 4:
        return [lax.ppermute(array, axis, [(i, i ^ k) for i in range(4)]) for k in (1, 3)]
    return [passed_along(array, axis, 1), passed_along(array, axis, -1)]


def line_shared(array, axis):
    peers = lax.axis_size(axis)
    if peers == 4:
        shared = [lax.ppermute(array, axis, [(i, i ^ k) for i in range(4)]) for k in (3, 2, 1)]
        return [array] + shared[::-1], [(k ^ 1, k ^ 3) for k in range(4)]
    shared = [passed_along(array, axis, k) for k in range(1, peers)]
    return [array] + shared, [tuple(sorted({(k + 1) % peers, (k - 1) % peers})) for k in range(peers)]


def summed_over_both(array, outer, inner):
    across, within = lax.axis_size(outer), lax.axis_size(inner)
    shifts = [(o, i) for o in range(across) for i in range(within)]
    total = array
    for o, i in shifts[1:]:
        pairs = [
            (x * within + y, (x + o) % across * within + (y + i) % within) for x, y in shifts
        ]
        total = total + lax.ppermute(array, (outer, inner), pairs)
    return total


def iota(shape, axis):
    return lax.broadcasted_iota(jnp.int32, shape, axis)


def row_after(w):
    rows = w[0].shape[0]
    zero = jnp.zeros((8, LANES), jnp.float32)
    return [pltpu.roll(jnp.concatenate([p, zero], axis=0), rows + 7, 0)[:rows] for p in w]


def row_before(w):
    rows = w[0].shape[0]
    zero = jnp.zeros((8, LANES), jnp.float32)
    return [pltpu.roll(jnp.concatenate([p, zero], axis=0), 1, 0)[:rows] for p in w]


def col_after(w):
    at_end = iota(w[0].shape, 1) == LANES - 1
    turned = [pltpu.roll(p, LANES - 1, 1) for p in w]
    return [jnp.where(at_end, n, p) for p, n in zip(turned, turned[1:] + [0.0])]


def col_before(w):
    at_start = iota(w[0].shape, 1) == 0
    turned = [pltpu.roll(p, 1, 1) for p in w]
    return [jnp.where(at_start, n, p) for p, n in zip(turned, [0.0] + turned[:-1])]


def each(f, *fields):
    return [f(*parts) for parts in zip(*fields)]


def minus(u, w):
    return each(lambda a, b: a - b, u, w)


def times(u, w):
    return each(lambda a, b: a * b, u, w)


def second_rows(w):
    return each(lambda a, b, c: a + b - (c + c), row_before(w), row_after(w), w)


def second_cols(w):
    return each(lambda a, b, c: a + b - (c + c), col_before(w), col_after(w), w)


def stiffness(w, live_thick, thick, support):
    bend_rows = times(live_thick, second_rows(w))
    bend_cols = times(thick, second_cols(w))
    return each(
        lambda f, a, r, c: f * a + (r + c), support, w, second_rows(bend_rows), second_cols(bend_cols)
    )


def differences(w):
    return minus(row_after(w), w), minus(col_after(w), w)


def membrane(along_rows, along_cols, stress):
    nuu, nvv, nuv = stress
    rows = each(lambda n, r, m, c: n * r + m * c, nuu, along_rows, nuv, along_cols)
    cols = each(lambda n, c, m, r: n * c + m * r, nvv, along_cols, nuv, along_rows)
    return rows, cols


def geometric(w, stress):
    rows, cols = membrane(*differences(w), stress)
    return each(
        lambda rb, r, cb, c: (rb - r) + (cb - c), row_before(rows), rows, col_before(cols), cols
    )


def cut(value):
    return [value[:, h * LANES : (h + 1) * LANES] for h in range(value.shape[1] // LANES)]


def joined(w):
    return jnp.concatenate(w, axis=1)


def live_of(rows_ref, slot, shape):
    return iota(shape, 0) < rows_ref[slot]


def masked(live, value):
    return [jnp.where(live, p, 0.0) for p in cut(value)]


def column_sums(product):
    return jnp.sum(product, axis=0, keepdims=True)


def folded(w):
    total = sum(w[1:], w[0])
    return jnp.sum(total.reshape(total.shape[0] // 8, 8, LANES), axis=0)


def packed(rows):
    rows = list(rows)
    rows += [jnp.zeros_like(rows[0])] * (-len(rows) % 8)
    lane = iota((8, LANES), 1)
    out = jnp.zeros((8, LANES), jnp.float32)
    for tile in range(len(rows) // 8):
        total = jnp.sum(jnp.concatenate(rows[8 * tile : 8 * tile + 8], axis=0), axis=1, keepdims=True)
        out = jnp.where(lane == tile, total, out)
    return out


def place(rows_ref, matched_ref, slots):
    inner = lax.axis_size(("sub", "half"))
    mine = [lax.axis_index("patch") * slots + s for s in range(slots)]
    match = [
        matched_ref[s] // (inner * slots) * slots + lax.rem(matched_ref[s], slots) for s in range(slots)
    ]
    return mine, match


STACK = 8


def edge_row(rows_ref, slot, side, depth, prows):
    return slot * prows + (rows_ref[slot] - 1 - depth if side else depth)


def stacked(rows_ref, prows):
    return [(4 * s + 2 * v + side, v, s, side) for s in range(2) for v in range(2) for side in range(2)]


def labels_of(rows_ref, matched_ref):
    mine, match = place(rows_ref, matched_ref, 2)
    row = iota((STACK, LANES), 0)
    label = jnp.full((STACK, LANES), 0, jnp.int32)
    for s in range(2):
        for side, number in enumerate((mine[s], match[s])):
            label = jnp.where((row // 4 == s) & (row % 2 == side), number, label)
    return label.astype(jnp.float32)


def other_side(stack):
    row = iota(stack.shape, 0)
    return jnp.where(row % 2 == 0, pltpu.roll(stack, STACK - 1, 0), pltpu.roll(stack, 1, 0))


def other_vector(w):
    row = iota(w[0].shape, 0)
    return [jnp.where(row // 2 % 2 == 0, pltpu.roll(p, STACK - 2, 0), pltpu.roll(p, 2, 0)) for p in w]


def opposite(label, near):
    found = None
    for labels, stacks in near:
        turned, parts = other_side(labels), [[other_side(p) for p in w] for w in stacks]
        for shift in (0, 4):
            if shift:
                turned, parts = pltpu.roll(turned, 4, 0), [[pltpu.roll(p, 4, 0) for p in w] for w in parts]
            here = turned == label
            picked = [[jnp.where(here, p, 0.0) for p in w] for w in parts]
            found = picked if found is None else [each(lambda x, y: x + y, f, p) for f, p in zip(found, picked)]
    return found


def meeting(own, met):
    jump = minus(own[0], met[0])
    slope = each(lambda a, b, c, d: (a + b) - (c + d), own[0], met[0], own[1], met[1])
    return jump, slope


def interface_rows(own, met):
    jump, slope = meeting(own, met)
    return (
        each(lambda j, m: penalty_value * j + penalty_slope * m, jump, slope),
        [-penalty_slope * m for m in slope],
    )


def local_rows(elem_ref, rows_dev):
    square = (rows_dev, rows_dev)
    if rows_dev & (rows_dev - 1) == 0:
        local = jnp.bitwise_and(elem_ref[...], rows_dev - 1)
    else:
        local = lax.rem(elem_ref[...], rows_dev)
    spread = jnp.broadcast_to(local.astype(jnp.float32), square)
    return jnp.sum(jnp.where(iota(square, 0) == iota(square, 1), spread, 0.0), axis=1, keepdims=True)


def pack_rows_kernel(stress_ref, elem_ref, pay_ref, elem, held, sems):
    rows_dev, ncol = stress_ref.shape[1:]
    get = pltpu.make_async_copy(elem_ref, elem, sems.at[0])
    get.start()
    planes = [
        pltpu.make_async_copy(stress_ref.at[j], held.at[:, pl.ds(j * ncol, ncol)], sems.at[1 + j])
        for j in range(3)
    ]
    for copy in planes:
        copy.start()
    get.wait()
    column = local_rows(elem, rows_dev)
    held[:, 3 * ncol :] = jnp.broadcast_to(column, (rows_dev, LANES)).astype(jnp.bfloat16)
    for copy in planes:
        copy.wait()
    put = pltpu.make_async_copy(held, pay_ref, sems.at[4])
    put.start()
    put.wait()


LABEL_LANE = 32


def neighbour_labels(arrived_ref, back, halves):
    me, peers, inner = lax.axis_index("patch"), lax.axis_size("patch"), lax.axis_size(("sub", "half"))
    there = jnp.bitwise_xor(me, back) if peers == 4 else lax.rem(me - back + peers, peers)
    block = there * inner + lax.axis_index(("sub", "half"))
    return arrived_ref[block, 48 * halves :, :].astype(jnp.float32)[:, LABEL_LANE : LABEL_LANE + 1]


def pack_blocks_kernel(stress_ref, elem_ref, matched_ref, pay_ref, elem, planes, held, match, get_sem, in_sems, out_sems):
    blocks, ncol = held.shape[0], stress_ref.shape[3]
    halves = ncol // LANES
    get = pltpu.make_async_copy(elem_ref, elem, get_sem)
    get.start()
    ask = pltpu.make_async_copy(matched_ref, match, out_sems.at[0])
    ask.start()
    fetch = [pltpu.make_async_copy(stress_ref.at[j], planes.at[j], in_sems.at[j]) for j in range(3)]
    for copy in fetch:
        copy.start()
    put = []
    get.wait()
    column = jnp.broadcast_to(local_rows(elem, 16 * blocks), (16 * blocks, LANES))
    ask.wait()
    labels = labels_of(None, match)
    lane = iota((8, LANES), 1)
    for k in range(blocks):
        both = jnp.where(lane < LANES // 2, column[16 * k : 16 * k + 8], column[16 * k + 8 : 16 * k + 16])
        held[k] = jnp.where(lane == LABEL_LANE, labels, both).astype(jnp.bfloat16)
    put.append(pltpu.make_async_copy(held, pay_ref.at[:, pl.ds(48 * halves, 8), :], out_sems.at[3 * halves]))
    put[0].start()
    for t in range(3 * halves):
        if t % halves == 0:
            fetch[t // halves].wait()
        source = planes.at[t // halves, :, :, pl.ds(t % halves * LANES, LANES)]
        put.append(pltpu.make_async_copy(source, pay_ref.at[:, pl.ds(16 * t, 16), :], out_sems.at[t]))
        put[-1].start()
    for copy in put:
        copy.wait()


def unpacked(arrived_ref, ncol):
    if len(arrived_ref.shape) == 2:
        return arrived_ref[:, : 3 * ncol], arrived_ref[:, 3 * ncol :].astype(jnp.float32)
    blocks, halves = arrived_ref.shape[0], ncol // LANES
    forces = jnp.concatenate(
        [
            jnp.concatenate([arrived_ref[k, 16 * t : 16 * t + 16, :] for k in range(blocks)], axis=0)
            for t in range(3 * halves)
        ],
        axis=1,
    )
    tiles = [arrived_ref[k, 48 * halves :, :].astype(jnp.float32) for k in range(blocks)]
    half = LANES // 2
    column = jnp.concatenate([t[:, at : at + 1] for t in tiles for at in (0, half)], axis=0)
    return forces, jnp.broadcast_to(column, (16 * blocks, LANES))


def edge_kernel(rows_ref, matched_ref, vec_ref, edge_ref):
    rows_dev, ncol = vec_ref.shape[1:]
    halves = ncol // LANES
    for depth in range(2):
        for at, v, s, side in stacked(rows_ref, rows_dev // 2):
            row = vec_ref[v, pl.ds(edge_row(rows_ref, s, side, depth, rows_dev // 2), 1), :]
            for h, part in enumerate(cut(row)):
                to = STACK * (depth * halves + h) + at
                edge_ref[to : to + 1, :] = part
    edge_ref[2 * STACK * halves :, :] = labels_of(rows_ref, matched_ref)


FIRST = [("kxx", 0, 0), ("kxx", 0, 1), ("kxx", 1, 1), ("kuu", 2, 2), ("kuu", 2, 3), ("kuu", 3, 3)]


RIM = [("prec", 2), ("thick", 3), ("support", 2), ("uk", 2), ("kuk", 2)]
RIM_AT = {name: sum(n for _, n in RIM[:i]) for i, (name, _) in enumerate(RIM)}
RIM_STACKS = sum(n for _, n in RIM)


def stiff_kernel(rows_ref, vec_ref, thick_ref, support_ref, uk_ref, kuk_ref, prec_ref, sums_ref, rim_ref, k_ref):
    slots = rows_ref.shape[0]
    rows_dev, ncol = thick_ref.shape
    prows = rows_dev // slots
    totals = {}
    for s in range(slots):
        at = slice(s * prows, (s + 1) * prows)
        live = live_of(rows_ref, s, (prows, LANES))
        thick, support = cut(thick_ref[at, :]), cut(support_ref[at, :])
        live_thick = masked(live, thick_ref[at, :])
        prec = each(lambda f, t: jnp.where(live, 1.0 / (f + 12.0 * t), 0.0), support, thick)
        prec_ref[at, :] = joined(prec)
        for v in range(2):
            kw = stiffness(masked(live, vec_ref[v, at, :]), live_thick, thick, support)
            k_ref[v, at, :] = joined(kw)
            uk_ref[v, at, :] = joined(times(prec, kw))
        for v in range(2):
            kuk_ref[v, at, :] = joined(stiffness(cut(uk_ref[v, at, :]), live_thick, thick, support))
        for a in range(2):
            wa = masked(live, vec_ref[a, at, :])
            for b in range(a, 2):
                for name, product in (
                    (("kxx", a, b), times(wa, cut(k_ref[b, at, :]))),
                    (("kuu", 2 + a, 2 + b), times(cut(uk_ref[a, at, :]), cut(kuk_ref[b, at, :]))),
                ):
                    part = folded(product)
                    totals[name] = totals[name] + part if s else part
    for k, name in enumerate(FIRST):
        sums_ref[8 * k : 8 * k + 8, :] = totals[name]
    sources = {"prec": prec_ref, "thick": thick_ref, "support": support_ref, "uk": uk_ref, "kuk": kuk_ref}
    for name, depths in RIM:
        for depth in range(depths):
            for at, v, s, side in stacked(rows_ref, prows):
                rows = pl.ds(edge_row(rows_ref, s, side, depth, prows), 1)
                to = STACK * (RIM_AT[name] + depth) + at
                ref = sources[name]
                rim_ref[to : to + 1, :] = ref[rows, :] if len(ref.shape) == 2 else ref[v, rows, :]


def rim_of(rim_ref, name, depth):
    at = STACK * (RIM_AT[name] + depth)
    return cut(rim_ref[at : at + STACK, :])


def sent_stack(ref, kind, depth, halves):
    at = (2 * kind + depth) * halves
    return [ref[STACK * (at + h) : STACK * (at + h + 1), :] for h in range(halves)]


PIECE = 32


def gram_kernel(
    rows_ref, arrived_ref, vec_ref, thick_ref, support_ref, prec_ref, uk_in, kuk_in, sums_in, rim_ref,
    edge_ref, below_ref, above_ref, v_ref, uk_ref, kuk_ref, stress_ref, out_ref,
):
    slots = rows_ref.shape[0]
    rows_dev, ncol = prec_ref.shape
    prows = rows_dev // slots
    halves = ncol // LANES
    forces, index = unpacked(arrived_ref, ncol)
    lane = iota(index.shape, 1).astype(jnp.float32)
    pick = jnp.concatenate(
        [
            jnp.where(index == lane + float(h * LANES), 1.0, 0.0).astype(jnp.bfloat16)
            for h in range(rows_dev // LANES)
        ],
        axis=1,
    )
    placed = lax.dot_general(
        pick, forces, (((0,), (0,)), ((), ())), preferred_element_type=jnp.float32
    )
    for j in range(3):
        stress_ref[j] = placed[:, j * ncol : (j + 1) * ncol]
    totals = {name: sums_in[8 * k : 8 * k + 8, :] for k, name in enumerate(FIRST)}

    def add(name, product):
        part = folded(product)
        totals[name] = totals[name] + part if name in totals else part

    def add_stack(first, second, product):
        part = sum(product[1:], product[0])
        vector = iota(part.shape, 0) // 2 % 2
        totals[first] = totals[first] + jnp.where(vector == 0, part, 0.0)
        if second is not None:
            totals[second] = totals[second] + jnp.where(vector == 1, part, 0.0)

    uk_ref[...] = uk_in[...]
    kuk_ref[...] = kuk_in[...]
    label = edge_ref[2 * STACK * halves :, :]

    def depths_of(ref):
        return [[ref[STACK * (d * halves + h) : STACK * (d * halves + h + 1), :] for h in range(halves)] for d in range(2)]

    own = depths_of(edge_ref)
    if len(arrived_ref.shape) == 2:
        labels = [ref[2 * STACK * halves :, :] for ref in (below_ref, above_ref)]
    else:
        backs = (1, 3) if lax.axis_size("patch") == 4 else (1, -1)
        labels = [neighbour_labels(arrived_ref, back, halves) for back in backs]
    met = opposite(label, [(near, depths_of(ref)) for near, ref in zip(labels, (below_ref, above_ref))])
    added = interface_rows(own, met)
    scaled = [times(rim_of(rim_ref, "prec", d), added[d]) for d in range(2)]
    bend = [
        each(lambda t, y, x: t * (y - (x + x)), rim_of(rim_ref, "thick", 0), scaled[1], scaled[0]),
        each(lambda t, y, x: t * (y - (x + x)), rim_of(rim_ref, "thick", 1), scaled[0], scaled[1]),
        times(rim_of(rim_ref, "thick", 2), scaled[1]),
    ]
    across = [second_cols(times(rim_of(rim_ref, "thick", d), second_cols(scaled[d]))) for d in range(2)]
    extra = [
        each(
            lambda f, z, p, q, c: f * z + (p - (q + q)) + c,
            rim_of(rim_ref, "support", 0), scaled[0], bend[1], bend[0], across[0],
        ),
        each(
            lambda f, z, p, q, r, c: f * z + (p - (q + q) + r) + c,
            rim_of(rim_ref, "support", 1), scaled[1], bend[0], bend[1], bend[2], across[1],
        ),
        each(lambda p, q: p - (q + q), bend[1], bend[2]),
        bend[2],
    ]
    for d in range(2):
        n, z, e, x = added[d], scaled[d], extra[d], own[d]
        kuk = rim_of(rim_ref, "kuk", d)
        add_stack(("kxx", 0, 0), ("kxx", 1, 1), times(x, n))
        add_stack(("kxx", 0, 1), None, times(x, other_vector(n)))
        add_stack(("kuu", 2, 2), ("kuu", 3, 3), each(lambda r, p, q: r * (p + p + q), z, kuk, e))
        turned, z_turned = other_vector(each(lambda p, q: p + q, kuk, e)), other_vector(z)
        add_stack(("kuu", 2, 3), None, each(lambda r, t, p, w: r * t + p * w, z, turned, kuk, z_turned))
    for d in range(4):
        for at, v, s, side in stacked(rows_ref, prows):
            rows = pl.ds(edge_row(rows_ref, s, side, d, prows), 1)
            kuk_ref[v, rows, :] += joined([p[at : at + 1] for p in extra[d]])
            if d < 2:
                uk_ref[v, rows, :] += joined([p[at : at + 1] for p in scaled[d]])
    for s in range(slots):
        at = slice(s * prows, (s + 1) * prows)
        live = live_of(rows_ref, s, (prows, LANES))
        stress = [cut(stress_ref[j, at, :]) for j in range(3)]
        prec = cut(prec_ref[at, :])
        x = [masked(live, vec_ref[v, at, :]) for v in range(2)]
        for b in range(2):
            gx = geometric(x[b], stress)
            v_ref[b, at, :] = joined(each(lambda w, p, g: w + p * g, x[b], prec, gx))
            for a in range(b + 1):
                add(("gxx", a, b), times(x[a], gx))
    basis = [(v_ref, 0), (v_ref, 1), (uk_ref, 0), (uk_ref, 1)]
    pieces = [(s, c) for s in range(slots) for c in range(0, prows, PIECE)]

    def piece(ref, v, s, c, low=0, high=0):
        start, stop = max(c - low, 0), min(c + PIECE + high, prows)
        parts = cut(ref[v, s * prows + start : s * prows + stop, :])
        zero = [jnp.zeros((8, LANES), jnp.float32)]
        head, tail = zero * ((start - c + low) // 8), zero * ((c + PIECE + high - stop) // 8)
        return [jnp.concatenate([*head, p, *tail], axis=0) if head or tail else p for p in parts]

    for s, c in pieces:
        stress = [piece(stress_ref, j, s, c) for j in range(3)]
        first = []
        for b in range(4):
            held = piece(*basis[b], s, c, high=8)
            w = [p[:PIECE] for p in held]
            along_rows = [pltpu.roll(p, PIECE + 7, 0)[:PIECE] - q for p, q in zip(held, w)]
            along_cols = minus(col_after(w), w)
            first.append((along_rows, along_cols))
            fr, fc = membrane(along_rows, along_cols, stress)
            for a in range(b + 1):
                add(("guu", a, b), each(lambda p, x, q, y: p * x + q * y, first[a][0], fr, first[a][1], fc))
    for s, c in pieces:
        at = slice(s * prows + c, s * prows + c + PIECE)
        live = iota((PIECE, LANES), 0) < rows_ref[s] - c
        thick, support = cut(thick_ref[at, :]), cut(support_ref[at, :])
        live_thick = masked(live, thick_ref[at, :])
        bends = []
        for v in range(2):
            held = piece(v_ref, v, s, c, 8, 8)
            w = [p[8 : 8 + PIECE] for p in held]
            rows = [
                pltpu.roll(p, PIECE + 15, 0)[8 : 8 + PIECE] + pltpu.roll(p, 1, 0)[8 : 8 + PIECE] - (q + q)
                for p, q in zip(held, w)
            ]
            bends.append((w, rows, second_cols(w)))
        for b in range(2):
            w, rows, cols = bends[b]
            sw, tr, tc = times(support, w), times(live_thick, rows), times(thick, cols)
            for a in range(b + 1):
                add(
                    ("kuu", a, b),
                    each(lambda u, x, p, y, q, z: u * x + p * y + q * z, bends[a][0], sw, bends[a][1], tr, bends[a][2], tc),
                )
        for b in range(2):
            kuk = piece(kuk_ref, b, s, c)
            for a in range(2):
                add(("kuu", a, 2 + b), times(bends[a][0], kuk))
    for d in range(2):
        for at, v, s, side in stacked(rows_ref, prows):
            row = v_ref[v, pl.ds(edge_row(rows_ref, s, side, d, prows), 1), :]
            for h, part in enumerate(cut(row)):
                to = STACK * (d * halves + h) + at
                out_ref[to : to + 1, :] = part
        for h, part in enumerate(each(lambda u, z: u + z, rim_of(rim_ref, "uk", d), scaled[d])):
            to = STACK * ((2 + d) * halves + h)
            out_ref[to : to + STACK, :] = part
    tile = packed([column_sums(totals[name]) for name in NAMES])
    out_ref[4 * STACK * halves :, :] = jnp.where(iota(tile.shape, 1) == LANES - 1, label, tile)


def apply_kernel(rows_ref, thick_ref, support_ref, prec_ref, stress_ref, v_ref, kuk_ref, a_ref, c_ref, d_ref):
    slots = rows_ref.shape[0]
    rows_dev, ncol = thick_ref.shape
    prows = rows_dev // slots
    for s in range(slots):
        at = slice(s * prows, (s + 1) * prows)
        live = live_of(rows_ref, s, (prows, LANES))
        thick, support = cut(thick_ref[at, :]), cut(support_ref[at, :])
        live_thick = masked(live, thick_ref[at, :])
        prec = cut(prec_ref[at, :])
        stress = [cut(stress_ref[j, at, :]) for j in range(3)]
        for v in range(2):
            w = cut(v_ref[v, at, :])
            a_ref[v, at, :] = joined(each(lambda u, p, g: u + p * g, w, prec, geometric(w, stress)))
            c_ref[v, at, :] = joined(times(prec, stiffness(w, live_thick, thick, support)))
            d_ref[v, at, :] = joined(times(prec, cut(kuk_ref[v, at, :])))


def line_parts(ref):
    halves = (ref.shape[0] // STACK - 1) // 4
    tag = 4 * STACK * halves
    return ref[tag:, LANES - 1 :], [sent_stack(ref, kind, d, halves) for kind in range(2) for d in range(2)]


def line_kernel(near, *refs):
    line, out_ref = refs[:-2], refs[-1]
    held = [line_parts(ref) for ref in line]
    sums = [None] * 6
    for (label, stacks), others in zip(held, near):
        met = opposite(label, [held[k] for k in others])
        g, k = (meeting(stacks[2 * i : 2 * i + 2], met[2 * i : 2 * i + 2]) for i in range(2))
        g_turned, k_turned = [other_vector(w) for w in g], [other_vector(w) for w in k]
        for i, (p, q) in enumerate(((g, g), (g, g_turned), (g, k), (g, k_turned), (k, k), (k, k_turned))):
            part = each(
                lambda a, b, c, d: penalty_value * (a * b) + penalty_slope * (c * d), p[0], q[0], p[1], q[1]
            )
            part = sum(part[1:], part[0])
            sums[i] = part if sums[i] is None else sums[i] + part
    total = line[0][-STACK:, :]
    for ref in line[1:]:
        total = total + ref[-STACK:, :]
    row = iota(total.shape, 0)
    masks = [(row % 2 == 1) & (row // 2 % 2 == v) for v in range(2)]
    rows = {
        (0, 0): (0, 0), (1, 1): (0, 1), (0, 1): (1, 0), (0, 2): (2, 0), (1, 3): (2, 1), (0, 3): (3, 0), (1, 2): (3, 1),
        (2, 2): (4, 0), (3, 3): (4, 1), (2, 3): (5, 0),
    }
    out_ref[...] = total + packed([column_sums(jnp.where(masks[rows[p][1]], sums[rows[p][0]], 0.0)) for p in UU])


def join_kernel(near, rows_ref, prec_ref, stress_ref, uk_ref, c_in, d_in, *refs):
    line, (b_ref, c_ref, d_ref) = refs[:-4], refs[-3:]
    c_ref[...] = c_in[...]
    d_ref[...] = d_in[...]
    prows = c_in.shape[1] // 2
    for s in range(2):
        at = slice(s * prows, (s + 1) * prows)
        prec = cut(prec_ref[at, :])
        stress = [cut(stress_ref[j, at, :]) for j in range(3)]
        for v in range(2):
            uk = cut(uk_ref[v, at, :])
            gk = geometric(uk, stress)
            b_ref[v, at, :] = joined(each(lambda u, p, g: u + p * g, uk, prec, gk))
    label, stacks = line_parts(line[0])
    met = opposite(label, [line_parts(ref) for ref in line[1:]])
    for i, ref in enumerate((c_ref, d_ref)):
        added = interface_rows(stacks[2 * i : 2 * i + 2], met[2 * i : 2 * i + 2])
        for d in range(2):
            for at, v, s, side in stacked(rows_ref, prows):
                rows = pl.ds(edge_row(rows_ref, s, side, d, prows), 1)
                ref[v, rows, :] += prec_ref[rows, :] * joined([p[at : at + 1] for p in added[d]])


def form(table, left, right):
    total = None
    for i, c in left.items():
        row = None
        for j, d in right.items():
            term = d * table[i, j]
            row = term if row is None else row + term
        total = c * row if total is None else total + c * row
    return total


def final_kernel(cells, total_ref, a_ref, b_ref, c_ref, d_ref, out_ref, held, sems):
    rows_dev, ncol = a_ref.shape[1:]
    prows = rows_dev // 2
    total = total_ref[...]

    def value(*name):
        k = AT[name]
        return jnp.broadcast_to(total[k % 8 : k % 8 + 1, k // 8 : k // 8 + 1], (8, LANES))

    k_table, g_table = {}, {}
    for a, b in UU:
        k_table[a, b] = k_table[b, a] = value("kuu", a, b)
        g_table[a, b] = g_table[b, a] = value("guu", a, b)
    first_a, cross_k, second_a = (value("kxx", a, b) for a, b in XX)
    first_g, cross_g, second_g = (value("gxx", a, b) for a, b in XX)
    ratio = cross_k / first_a
    other_a = second_a - ratio * cross_k
    other_q = second_g - 2.0 * ratio * cross_g + ratio * ratio * first_g
    mu_first = first_g / first_a
    mu_other = other_q / other_a
    one = jnp.ones_like(ratio)
    new_first = {0: one, 2: -mu_first}
    new_second = {0: -ratio, 1: one, 2: mu_other * ratio, 3: -mu_other}
    a1 = form(k_table, new_first, new_first)
    c = form(k_table, new_first, new_second)
    a2 = form(k_table, new_second, new_second)
    g1 = form(g_table, new_first, new_first)
    h = form(g_table, new_first, new_second)
    g2 = form(g_table, new_second, new_second)
    r = c / a1
    b2 = a2 - r * c
    q2 = g2 - 2.0 * r * h + r * r * g1
    mus = [g1 / a1, q2 / b2]
    scales = [jnp.sqrt(norm_scale * cells / a1), jnp.sqrt(norm_scale * cells / b2)]
    lead = [
        {i: scales[0] * f for i, f in new_first.items()},
        {i: scales[1] * (f - r * new_first[i] if i in new_first else f) for i, f in new_second.items()},
    ]
    copies = []
    tall = (prows // 8, 8, LANES)
    for s in range(2):
        at = pl.ds(s * prows, prows)
        for v in range(2):
            for h in range(ncol // LANES):
                cols = pl.ds(h * LANES, LANES)
                acc = None
                for i in (0, 1):
                    if i in lead[v]:
                        f, g = lead[v][i], lead[v][2 + i]
                        parts = [ref[i, at, cols].reshape(tall) for ref in (a_ref, b_ref, c_ref, d_ref)]
                        term = f * parts[0] + g * parts[1]
                        term = term - ((mus[v] * f) * parts[2] + (mus[v] * g) * parts[3])
                        acc = term if acc is None else acc + term
                held[v, at, cols] = acc.reshape(prows, LANES)
            copies.append(pltpu.make_async_copy(held.at[v, at, :], out_ref.at[v, at, :], sems.at[2 * s + v]))
            copies[-1].start()
    for copy in copies:
        copy.wait()


def call(body, outs, kinds, scratch=(), flops=1_000_000, out_kind="v"):
    spaces = {"s": pltpu.SMEM, "v": pltpu.VMEM, "h": pltpu.HBM, "a": pl.ANY}
    return pl.pallas_call(
        body,
        out_shape=[pltpu.HBM(s, d) if out_kind == "h" else jax.ShapeDtypeStruct(s, d) for s, d in outs],
        in_specs=[pl.BlockSpec(memory_space=spaces[k]) for k in kinds],
        out_specs=[pl.BlockSpec(memory_space=spaces[out_kind]) for _ in outs],
        scratch_shapes=list(scratch),
        compiler_params=pltpu.CompilerParams(vmem_limit_bytes=32 * 1024 * 1024),
        cost_estimate=pl.CostEstimate(flops=flops, bytes_accessed=2_000_000, transcendentals=0),
    )


def per_device(vectors, prestress, thickness, foundation, patch_rows, matched, elem_row):
    owners = lax.axis_size("patch")
    inner = lax.axis_size(("sub", "half"))
    slots = patch_rows.shape[0]
    rows_dev, ncol = thickness.shape
    f32, bf16 = jnp.float32, jnp.bfloat16
    cells = float(owners * inner * rows_dev * ncol)
    field = ((2, rows_dev, ncol), f32)
    one = ((rows_dev, ncol), f32)
    sums = ((8 * len(FIRST), LANES), f32)
    tile = ((8, LANES), f32)

    width = 3 * ncol + LANES
    elem = pltpu.VMEM((1, rows_dev), jnp.int32)
    planes = jnp.transpose(prestress, (1, 0, 2))
    if rows_dev == 16 * owners * inner:
        tiles = 3 * (ncol // LANES)
        shape = (owners * inner, 16 * tiles + 8, LANES)
        planes = planes.reshape(3, owners * inner, 16, ncol)
        sems = [pltpu.SemaphoreType.DMA, pltpu.SemaphoreType.DMA((tiles,)), pltpu.SemaphoreType.DMA((tiles + 1,))]
        pack = pack_blocks_kernel
        scratch = [pltpu.VMEM(planes.shape, bf16), pltpu.VMEM((owners * inner, 8, LANES), bf16), pltpu.SMEM(matched.shape, jnp.int32)]
        extra = [pltpu.with_memory_space_constraint(matched, pltpu.HBM)]
    else:
        shape = (rows_dev, width)
        sems = [pltpu.SemaphoreType.DMA((5,))]
        pack = pack_rows_kernel
        scratch, extra = [pltpu.VMEM(shape, bf16)], []
    (payload,) = call(pack, [(shape, bf16)], "h" * (2 + len(extra)), [elem, *scratch, *sems], out_kind="h")(
        pltpu.with_memory_space_constraint(planes, pltpu.HBM),
        pltpu.with_memory_space_constraint(elem_row.reshape(1, rows_dev), pltpu.HBM),
        *extra,
    )
    arrived = lax.all_to_all(
        payload, ("patch", "sub", "half"), split_axis=0, concat_axis=0, tiled=True
    )
    halves = ncol // LANES
    (edges,) = call(edge_kernel, [(((2 * halves + 1) * STACK, LANES), f32)], "ssv")(patch_rows, matched, vectors)
    below, above = neighbours(edges[: 2 * STACK * halves] if extra else edges, "patch")
    u_k, k_uk, prec, part, rim = call(
        stiff_kernel,
        [field, field, one, sums, ((RIM_STACKS * STACK, ncol), f32)],
        "svvv",
        [pltpu.VMEM(field[0], f32)],
    )(patch_rows, vectors, thickness, foundation)
    v, u_k, k_uk, stress, sent = call(
        gram_kernel,
        [field, field, field, ((3, rows_dev, ncol), f32), (((4 * halves + 1) * STACK, LANES), f32)],
        "svvvvvvvvvvvv",
    )(
        patch_rows, arrived, vectors, thickness, foundation, prec, u_k, k_uk, part, rim,
        edges, below, above,
    )
    line, near = line_shared(sent, "patch")
    a, c, d = call(apply_kernel, [field] * 3, "svvvvvv")(
        patch_rows, thickness, foundation, prec, stress, v, k_uk
    )
    (total,) = call(functools.partial(line_kernel, near), [tile], "v" * owners + "a")(*line, a)
    total = summed_over_both(total, "sub", "half")
    b, c, d = call(functools.partial(join_kernel, near), [field] * 3, "sv" + "v" * (len(near[0]) + 5) + "a")(
        patch_rows, prec, stress, u_k, c, d, line[0], *[line[k] for k in near[0]], line[2]
    )
    (modes,) = call(
        functools.partial(final_kernel, cells),
        [field],
        "vvvvv",
        [pltpu.VMEM(field[0], f32), pltpu.SemaphoreType.DMA((4,))],
        out_kind="h",
    )(total, a, b, c, d)
    return modes


def solution(mesh):
    in_specs = (
        P(None, ("groups", "patch", "sub", "half"), None),
        P(("groups", "patch", "sub", "half"), None, None),
        P(("groups", "patch", "sub", "half"), None),
        P(("groups", "patch", "sub", "half"), None),
        P(("groups", "patch", "sub", "half")),
        P(("groups", "patch", "sub", "half")),
        P(("groups", "patch", "sub", "half")),
    )
    out_specs = P(None, ("groups", "patch", "sub", "half"), None)
    return jax.shard_map(
        per_device, mesh=mesh, in_specs=in_specs, out_specs=out_specs, check_vma=False
    )
```
